128 devices in a mesh: dp: 16 (over z_hi, y, core), mp: 8 (over z_lo, x).
Axes of the slice: x: 4, y: 4, z: 4 (z_hi: 2, z_lo: 2; z = z_hi * 2 + z_lo), core: 2. Of those that a mesh axis runs over, the one named last changes fastest.
Arguments:
- patches: bfloat16 [8192, 6144], P('dp'), may hold values from -6 to 6
- norm_gain: float32 [6144], replicated, may hold values from 0.1 to 1.9
- qkv_weight: bfloat16 [6144, 24, 384], P('dp', 'mp'), may hold values from -0.078125 to 0.078125
- qk_gain: float32 [2, 24, 128], P(None, 'mp'), may hold values from 0.1 to 24, as said below
- out_weight: bfloat16 [6144, 3072], P('dp', 'mp'), may hold values from -0.109375 to 0.109375
- final_gain: float32 [6144], replicated, may hold values from 0.1 to 1.9
- proj_weight: bfloat16 [6144, 4096], P('dp', 'mp'), may hold values from -0.078125 to 0.078125
- text_embed: bfloat16 [16, 1024, 4096], P('dp', 'mp'), may hold values from -6 to 6
- slot_offset: int32 [32], P('dp'), may hold values from 0 to 768, as said below
- text_len: int32 [16], P('dp'), may hold values from 0 to 512
Outputs:
- block_out: bfloat16 [8192, 6144], P('dp', 'mp')
- sequence: bfloat16 [16, 1024, 4096], P('dp', 'mp')
The draws below stay inside these ranges and needn't reach their ends.
Inputs may be any that keep to these rules, and one draw needn't show every extreme that they name: `slot_offset`: images 2r and 2r + 1 lie in packed row r; every offset is a multiple of half of 256; image 2r + 1 starts at or after the end of image 2r, and both end inside the row. `qk_gain`: positive gains.
All inputs are finite; a program needn't handle non-finite values.
Results may differ from the reference program's by a relative error of at most 0.015.
The reference program's roundings to bfloat16 on the way (of `normed_in`, `weights`, `attended`, `normed_out` and `projected`) count: a program that leaves them out, or rounds other values in their place, can miss the bound.
Values may be sent and summed in bfloat16 or wider, within the bound.
No kernel may reach another device: no remote copies, remote signals or barrier semaphores. Data moves between devices by JAX's collectives and lax.ppermute only.
A program may use at most 128 MiB of HBM per device.

```python
import math
import jax
import jax.numpy as jnp
from jax import lax

D = 6144
HEADS = 24
HD = 128
E = 4096
PATCHES = 256
SEQ_LEN = 1024
IMAGES = 32
TOKENS = 8192
ROWS = 16
N_MP = 8


def draw_qk_gain(key, part):
    key = jax.random.fold_in(key, 11)
    first_key = jax.random.fold_in(key, 0)
    normals = jnp.clip(jax.random.normal(first_key, (2, HEADS, HD), jnp.float32), -4.0, 4.0)
    gains = jnp.exp(0.5 * normals)
    return gains.astype(jnp.float32)


def draw_slot_offset(key, part):
    key = jax.random.fold_in(key, 5)
    lead_key, gap_key = jax.random.split(key)
    pairs = IMAGES // 2
    half = PATCHES // 2
    lead = jax.random.randint(lead_key, (pairs,), 0, 5)
    spacing = jax.random.randint(gap_key, (pairs,), 0, 5 - lead)
    first = lead * half
    second = (lead + 2 + spacing) * half
    return jnp.stack([first, second], 1).reshape(IMAGES).astype(jnp.int32)


def place_ends(values, key, low, top_value):
    index_at = [jax.random.randint(jax.random.fold_in(key, axis), (), 0, length) for axis, length in enumerate(values.shape)]
    main_axis = values.shape.index(max(values.shape))
    neighbour = index_at[:main_axis] + [(index_at[main_axis] + 1) % values.shape[main_axis]] + index_at[main_axis + 1:]
    return values.at[tuple(index_at)].set(low).at[tuple(neighbour)].set(top_value)


def block_scale(rng, extent, pieces, low, high):
    loudness, own = 1.0, jax.random.fold_in(rng, 6)
    for dim, parts in pieces:
        draws = jnp.exp(jax.random.uniform(jax.random.fold_in(own, dim), (parts,), jnp.float32, low / len(pieces), high / len(pieces)))
        loudness = loudness * jnp.repeat(draws, extent[dim] // parts).reshape([-1 if axis == dim else 1 for axis in range(len(extent))])
    return loudness


def centred(key, shape, spread, reach, shards=(), kind=jnp.bfloat16):
    array = jax.random.normal(key, shape, jnp.float32) * spread
    if len(shards) > 0:
        array = block_scale(key, shape, shards, -0.22, 0.18) * array
    return jnp.clip(array, min=-reach, max=reach).astype(kind)


def setup_inputs(seed: int = 0) -> dict:
    key_of = jax.random.split(jax.random.key(seed), 11)
    return {
        "patches": centred(key_of[0], (TOKENS, D), 1.0, 6.0, ((0, 16),)),
        "norm_gain": jnp.clip(1.0 + 0.18 * jax.random.normal(key_of[1], (D,), jnp.float32), 0.1, 1.9),
        "qkv_weight": centred(key_of[2], (D, HEADS, 3 * HD), D ** -0.5, 0.078125, ((0, 16), (1, 8))),
        "qk_gain": draw_qk_gain(jax.random.fold_in(key_of[10], 71), 0),
        "out_weight": centred(key_of[4], (D, HEADS * HD), (HEADS * HD) ** -0.5, 0.109375, ((0, 16), (1, 8))),
        "final_gain": jnp.clip(1.0 + 0.18 * jax.random.normal(key_of[5], (D,), jnp.float32), 0.1, 1.9),
        "proj_weight": centred(key_of[6], (D, E), D ** -0.5, 0.078125, ((0, 16), (1, 8))),
        "text_embed": centred(key_of[7], (ROWS, SEQ_LEN, E), 1.0, 6.0, ((0, 16), (1, 8))),
        "slot_offset": draw_slot_offset(jax.random.fold_in(key_of[10], 71), 0),
        "text_len": place_ends(jax.random.randint(key_of[9], (ROWS,), 0, SEQ_LEN - 2 * PATCHES + 1), jax.random.fold_in(key_of[9], 1), 0, SEQ_LEN - 2 * PATCHES).astype(jnp.int32),
    }


epsilon = 1e-06

def layer_norm(values, gain):
    values = values.astype(jnp.float32)
    row_mean = lax.optimization_barrier(jnp.mean(values, -1, keepdims=True))
    squares = lax.optimization_barrier(jnp.mean(values * values, -1, keepdims=True))
    return (values - row_mean) * lax.rsqrt(squares - row_mean * row_mean + epsilon) * gain

def reference(patches, norm_gain, qkv_weight, qk_gain, out_weight, final_gain, proj_weight, text_embed, slot_offset, text_len):
    normed_in = layer_norm(patches, norm_gain).astype(jnp.bfloat16)
    mixed = jnp.dot(normed_in, qkv_weight.reshape(D, HEADS * 3 * HD), preferred_element_type=jnp.float32)
    mixed = mixed.reshape(TOKENS, HEADS, 3 * HD)
    query_norm = layer_norm(mixed[..., :HD], qk_gain[0]).astype(jnp.bfloat16)
    key_norm = layer_norm(mixed[..., HD:2 * HD], qk_gain[1]).astype(jnp.bfloat16)
    value_rows = mixed[..., 2 * HD:].astype(jnp.bfloat16)
    shape4 = (IMAGES, PATCHES, HEADS, HD)

    def one_image(inputs):
        query_img, key_img, value_img = inputs
        scores = jnp.einsum('qhd,khd->hqk', query_img.astype(jnp.float32), key_img.astype(jnp.float32)) / math.sqrt(HD)
        weights = jax.nn.softmax(scores, axis=-1).astype(jnp.bfloat16)
        return jnp.einsum('hqk,khd->qhd', weights.astype(jnp.float32), value_img.astype(jnp.float32)).astype(jnp.bfloat16)
    attended = lax.map(one_image, (query_norm.reshape(shape4), key_norm.reshape(shape4), value_rows.reshape(shape4)))
    attended = attended.reshape(TOKENS, HEADS * HD)
    group_cols = HEADS * HD // N_MP
    branch = jnp.zeros((TOKENS, D), jnp.float32)
    for group in range(N_MP):
        att_group = attended[:, group * group_cols:(group + 1) * group_cols]
        weight_group = out_weight[:, group * group_cols:(group + 1) * group_cols]
        term = jnp.dot(att_group, weight_group.T, preferred_element_type=jnp.float32)
        branch = branch + term.astype(jnp.bfloat16).astype(jnp.float32)
    block_out = (patches.astype(jnp.float32) + branch).astype(jnp.bfloat16)
    normed_out = layer_norm(block_out, final_gain).astype(jnp.bfloat16)
    projected = jnp.dot(normed_out, proj_weight, preferred_element_type=jnp.float32).astype(jnp.bfloat16)
    offsets = slot_offset.reshape(ROWS, 2)
    first = offsets[:, 0:1]
    second = offsets[:, 1:2]
    position = jnp.arange(SEQ_LEN, dtype=jnp.int32)[None, :]
    in_first = (position >= first) & (position < first + PATCHES)
    in_second = (position >= second) & (position < second + PATCHES)
    base = (2 * PATCHES * jnp.arange(ROWS, dtype=jnp.int32))[:, None]
    row_index = jnp.where(in_first, base + position - first, jnp.where(in_second, base + PATCHES + position - second, 0)).astype(jnp.int32)
    gathered = jnp.take(projected, row_index.reshape(-1), axis=0).reshape(ROWS, SEQ_LEN, E)
    before = jnp.clip(position - first, 0, PATCHES) + jnp.clip(position - second, 0, PATCHES)
    rank = position - before
    covered = in_first | in_second
    is_text = jnp.logical_not(covered) & (rank < text_len[:, None])
    zero_value = jnp.zeros((), jnp.bfloat16)
    sequence = jnp.where(covered[..., None], gathered, jnp.where(is_text[..., None], text_embed, zero_value))
    return (block_out, sequence)
```

```python
import math

import jax
import jax.numpy as jnp
from jax import lax
from jax.sharding import PartitionSpec as P

PATCHES = 256
HALF = 128
AXES = ("dp", "mp")
epsilon = 1e-06


def device_index(zh, y, c, zl, x):
    return ((zh * 4 + y) * 2 + c) * 8 + zl * 4 + x


def move(values, target):
    pairs = []
    for zh in range(2):
        for y in range(4):
            for c in range(2):
                for zl in range(2):
                    for x in range(4):
                        pairs.append(
                            (device_index(zh, y, c, zl, x), device_index(*target(zh, y, c, zl, x)))
                        )
    return lax.ppermute(values, AXES, pairs)


def swap_core(values):
    return move(values, lambda zh, y, c, zl, x: (zh, y, 1 - c, zl, x))


def swap_zh(values):
    return move(values, lambda zh, y, c, zl, x: (1 - zh, y, c, zl, x))


def swap_zl(values):
    return move(values, lambda zh, y, c, zl, x: (zh, y, c, 1 - zl, x))


def spread_y(values):
    return move(values, lambda zh, y, c, zl, x: (zh, (y + 1 - 2 * c) % 4, c, zl, x))


def shift_x(values, step):
    return move(values, lambda zh, y, c, zl, x: (zh, y, c, zl, (x + step) % 4))


def transpose_mesh(values):
    return move(values, lambda zh, y, c, zl, x: (zl, x, c, zh, y))


def layer_norm(values, gain):
    values = values.astype(jnp.float32)
    row_mean = jnp.mean(values, -1, keepdims=True)
    squares = jnp.mean(values * values, -1, keepdims=True)
    return (values - row_mean) * lax.rsqrt(squares - row_mean * row_mean + epsilon) * gain


def pick(values, index):
    return lax.dynamic_index_in_dim(values, index, 0, keepdims=False)


def gather_pieces(own, zh, y, c):
    def dp_index(zh, y, c):
        return (zh % 2) * 8 + (y % 4) * 2 + c % 2

    pieces = [(own, dp_index(zh, y, c))]
    other = swap_core(own)
    far = swap_zh(own)
    first = spread_y(jnp.stack([own, other]))
    pieces.append((other, dp_index(zh, y, c + 1)))
    far_other = swap_core(far)
    pieces.append((far, dp_index(zh + 1, y, c)))
    pieces.append((far_other, dp_index(zh + 1, y, c + 1)))
    far_first = spread_y(jnp.stack([far, far_other]))
    step = 2 * c - 1
    for row, block in ((zh, first), (zh + 1, far_first)):
        second = spread_y(block[0])
        block_other = swap_core(block)
        pieces.append((block[0], dp_index(row, y + step, c)))
        pieces.append((block[1], dp_index(row, y + step, c + 1)))
        pieces.append((block_other[0], dp_index(row, y - step, c + 1)))
        pieces.append((block_other[1], dp_index(row, y - step, c)))
        second_other = swap_core(second)
        pieces.append((second, dp_index(row, y + 2, c)))
        pieces.append((second_other, dp_index(row, y + 2, c + 1)))
    return pieces


def local(
    patches,
    norm_gain,
    qkv_weight,
    qk_gain,
    out_weight,
    final_gain,
    proj_weight,
    text_embed,
    slot_offset,
    text_len,
):
    tok_count, width = patches.shape
    local_heads = qkv_weight.shape[1]
    head_size = qk_gain.shape[2]
    depth = qkv_weight.shape[0]
    dp = lax.axis_index("dp")
    mp = lax.axis_index("mp")
    zh, y, c = dp // 8, (dp // 2) % 4, dp % 2
    zl, x = mp // 4, mp % 4

    pieces = gather_pieces(qkv_weight.transpose(1, 0, 2), zh, y, c)

    turned = transpose_mesh(jnp.concatenate([out_weight, proj_weight], axis=1))
    gathered = lax.all_gather(turned, "dp", axis=0, tiled=True)
    gathered = gathered.reshape(8, 2 * depth, out_weight.shape[1] + proj_weight.shape[1])
    out_parts = gathered[:, :, : out_weight.shape[1]]
    proj_parts = gathered[:, :, out_weight.shape[1] :]

    normed_in = layer_norm(patches, norm_gain).astype(jnp.bfloat16)
    columns = normed_in.reshape(tok_count, 16, depth).transpose(1, 0, 2)
    mixed = jnp.zeros((local_heads, tok_count, 3 * head_size), jnp.float32)
    for shard, index in pieces:
        mixed = mixed + jnp.einsum(
            "td,hdc->htc", pick(columns, index), shard, preferred_element_type=jnp.float32
        )
    query_norm = layer_norm(mixed[..., :head_size], qk_gain[0][:, None]).astype(jnp.bfloat16)
    key_norm = layer_norm(mixed[..., head_size : 2 * head_size], qk_gain[1][:, None]).astype(
        jnp.bfloat16
    )
    value_rows = mixed[..., 2 * head_size :].astype(jnp.bfloat16)
    image_count = tok_count // PATCHES
    shape4 = (local_heads, image_count, PATCHES, head_size)
    scores = jnp.einsum(
        "hiqd,hikd->hiqk",
        query_norm.reshape(shape4),
        key_norm.reshape(shape4),
        preferred_element_type=jnp.float32,
    ) / math.sqrt(head_size)
    weights = jax.nn.softmax(scores, axis=-1).astype(jnp.bfloat16)
    attended = jnp.einsum(
        "hiqk,hikd->iqhd", weights, value_rows.reshape(shape4), preferred_element_type=jnp.float32
    )
    attended = attended.astype(jnp.bfloat16).reshape(tok_count, local_heads * head_size)

    near = {(0, 0): attended, (1, 0): swap_zl(attended)}
    half = tok_count // 2
    for dz in range(2):
        mine = near[dz, 0]
        left = shift_x(mine, 1)
        right = shift_x(mine, -1)
        near[dz, 3] = left
        near[dz, 1] = right
        near[dz, 2] = jnp.concatenate([shift_x(left[:half], 1), shift_x(right[half:], -1)], 0)
    group = {(dz, dx): ((zl + dz) % 2) * 4 + (x + dx) % 4 for dz in range(2) for dx in range(4)}

    branch = jnp.zeros((tok_count, 2 * depth), jnp.float32)
    for place, part in near.items():
        term = lax.dot_general(
            part,
            pick(out_parts, group[place]),
            (((1,), (1,)), ((), ())),
            preferred_element_type=jnp.float32,
        )
        branch = branch + term.astype(jnp.bfloat16).astype(jnp.float32)
    column_count = 2 * depth
    own_cols = lax.dynamic_slice_in_dim(patches, mp * column_count, column_count, 1)
    block_out = (own_cols.astype(jnp.float32) + branch).astype(jnp.bfloat16)
    block_vals = block_out.astype(jnp.float32)
    row_sums, row_squares = lax.psum(
        (jnp.sum(block_vals, 1), jnp.sum(block_vals * block_vals, 1)), "mp"
    )
    row_mean = (row_sums / width)[:, None]
    row_var = (row_squares / width)[:, None] - row_mean * row_mean
    gain_cols = lax.dynamic_slice_in_dim(final_gain, mp * column_count, column_count, 0)
    normed_cols = ((block_vals - row_mean) * lax.rsqrt(row_var + epsilon) * gain_cols).astype(
        jnp.bfloat16
    )

    part = {}
    for dx in (2, 1, 3, 0):
        part[dx] = jnp.stack(
            [
                jnp.dot(
                    normed_cols,
                    pick(proj_parts, group[dz, dx]),
                    preferred_element_type=jnp.float32,
                )
                for dz in range(2)
            ]
        )
    far = part[2].astype(jnp.bfloat16)
    to_right = shift_x(far[:, half:], 1).astype(jnp.float32)
    to_left = shift_x(far[:, :half], -1).astype(jnp.float32)
    right = jnp.concatenate([part[1][:, :half], part[1][:, half:] + to_right], 1)
    left = jnp.concatenate([part[3][:, :half] + to_left, part[3][:, half:]], 1)
    total = (
        part[0]
        + shift_x(right.astype(jnp.bfloat16), 1).astype(jnp.float32)
        + shift_x(left.astype(jnp.bfloat16), -1).astype(jnp.float32)
    )
    total = total[0] + swap_zl(total[1].astype(jnp.bfloat16)).astype(jnp.float32)
    projected = total.astype(jnp.bfloat16).reshape(4, HALF, -1)

    first, second = slot_offset[0] // HALF, slot_offset[1] // HALF

    def source(block):
        in_first = (block >= first) & (block < first + 2)
        in_second = (block >= second) & (block < second + 2)
        index = jnp.where(in_first, block - first, jnp.where(in_second, block - second + 2, 0))
        return in_first | in_second, index

    arrived = []
    zero_value = jnp.zeros((), jnp.bfloat16)
    for dz in range(2):
        for dx in range(4):
            covered, index = source(group[dz, dx])
            block = jnp.where(covered, pick(projected, index), zero_value)
            if (dz, dx) != (0, 0):
                block = move(
                    block,
                    lambda zh, y, c, zl, x: (zh, y, c, (zl + dz) % 2, (x + dx) % 4),
                )
            arrived.append(block)
    arrived = jnp.stack(arrived)
    place = jnp.arange(8)
    relative = ((place // 4 + zl) % 2) * 4 + (x - place) % 4
    arrived = jnp.take(arrived, relative, axis=0).transpose(1, 0, 2).reshape(HALF, -1)

    covered, _ = source(mp)
    position = mp * HALF + jnp.arange(HALF, dtype=jnp.int32)
    before = jnp.clip(position - slot_offset[0], 0, PATCHES) + jnp.clip(
        position - slot_offset[1], 0, PATCHES
    )
    is_text = (position - before) < text_len[0]
    sequence = jnp.where(
        covered, arrived, jnp.where(is_text[:, None], text_embed[0], zero_value)
    )
    return (block_out, sequence[None])


def solution(mesh):
    in_specs = (
        P("dp", None),
        P(),
        P("dp", "mp", None),
        P(None, "mp", None),
        P("dp", "mp"),
        P(),
        P("dp", "mp"),
        P("dp", "mp", None),
        P("dp"),
        P("dp"),
    )
    out_specs = (P("dp", "mp"), P("dp", "mp", None))
    return jax.shard_map(local, mesh=mesh, in_specs=in_specs, out_specs=out_specs, check_vma=False)
```

```python
import functools
import math

import jax
import jax.numpy as jnp
import numpy as np
from jax import lax
from jax.experimental import pallas as pl
from jax.experimental.pallas import tpu as pltpu
from jax.sharding import PartitionSpec as P

PATCHES = 256
HALF = 128
AXES = ("dp", "mp")
VMEM = 40 * 1024 * 1024
epsilon = 1e-06


def coordinates():
    return [
        (zh, y, c, zl, x)
        for zh in range(2)
        for y in range(4)
        for c in range(2)
        for zl in range(2)
        for x in range(4)
    ]


def device_index(zh, y, c, zl, x):
    return ((zh * 4 + y) * 2 + c) * 8 + zl * 4 + x


def move(values, target):
    pairs = [(device_index(*at), device_index(*target(*at))) for at in coordinates()]
    return lax.ppermute(values, AXES, pairs)


def swap_core(values):
    return move(values, lambda zh, y, c, zl, x: (zh, y, 1 - c, zl, x))


def swap_zh(values):
    return move(values, lambda zh, y, c, zl, x: (1 - zh, y, c, zl, x))


def swap_zl(values):
    return move(values, lambda zh, y, c, zl, x: (zh, y, c, 1 - zl, x))


def spread_y(values):
    return move(values, lambda zh, y, c, zl, x: (zh, (y + 1 - 2 * c) % 4, c, zl, x))


def shift_x(values, step):
    return move(values, lambda zh, y, c, zl, x: (zh, y, c, zl, (x + step) % 4))


def transpose_mesh(values):
    return move(values, lambda zh, y, c, zl, x: (zl, x, c, zh, y))


def arrival_table():
    table = np.zeros((16, 16), np.int32)
    for zh in range(2):
        for y in range(4):
            for c in range(2):
                step = 2 * c - 1
                order = []
                for row in (zh, 1 - zh):
                    order += [(row, y, c), (row, y, 1 - c)]
                for row in (zh, 1 - zh):
                    order += [
                        (row, y + step, c),
                        (row, y + step, 1 - c),
                        (row, y - step, 1 - c),
                        (row, y - step, c),
                    ]
                for row in (zh, 1 - zh):
                    order += [(row, y + 2, c), (row, y + 2, 1 - c)]
                table[zh * 8 + y * 2 + c] = [r * 8 + (yy % 4) * 2 + cc for r, yy, cc in order]
    return table


def relative_table():
    arrivals = arrival_table()
    table = np.zeros((16, 8, 16), np.int32)
    for dp in range(16):
        for mp in range(8):
            for k in range(16):
                group = arrivals[dp, k] // 2
                dz = (group // 4) ^ (mp // 4)
                table[dp, mp, k] = dz * 4 + (group - mp) % 4
    return table


def norm_kernel(values_ref, gain_ref, out_ref):
    values = values_ref[...].astype(jnp.float32)
    width = values.shape[1]
    row_mean = jnp.sum(values, -1, keepdims=True) / width
    squares = jnp.sum(values * values, -1, keepdims=True) / width
    scale = lax.rsqrt(squares - row_mean * row_mean + epsilon)
    normed = ((values - row_mean) * scale * gain_ref[...]).astype(jnp.bfloat16)
    depth = out_ref.shape[2]
    for k in range(out_ref.shape[0]):
        out_ref[k] = normed[:, k * depth : (k + 1) * depth]


def norm_columns(values, gain, chunks):
    rows, width = values.shape
    block = 64
    return pl.pallas_call(
        norm_kernel,
        grid=(rows // block,),
        in_specs=[
            pl.BlockSpec((block, width), lambda i: (i, 0)),
            pl.BlockSpec((1, width), lambda i: (0, 0)),
        ],
        out_specs=pl.BlockSpec((chunks, block, width // chunks), lambda i: (0, i, 0)),
        out_shape=jax.ShapeDtypeStruct((chunks, rows, width // chunks), jnp.bfloat16),
        compiler_params=pltpu.CompilerParams(vmem_limit_bytes=VMEM),
        cost_estimate=pl.CostEstimate(
            flops=8 * rows * width, bytes_accessed=4 * rows * width, transcendentals=rows
        ),
        name="norm_columns",
    )(values, gain.reshape(1, width))


def row_norm(values, gain):
    row_mean = jnp.mean(values, -1, keepdims=True)
    squares = jnp.mean(values * values, -1, keepdims=True)
    return (values - row_mean) * lax.rsqrt(squares - row_mean * row_mean + epsilon) * gain


def accumulate_kernel(shard_counts, has_total, attend, index_ref, *refs):
    del index_ref
    count = sum(shard_counts)
    columns, refs = refs[:count], refs[count:]
    shards, refs = refs[: len(shard_counts)], refs[len(shard_counts) :]
    total = None
    if has_total:
        total, refs = refs[0][0], refs[1:]
    at = 0
    for held, number in zip(shards, shard_counts):
        for k in range(number):
            term = jnp.dot(columns[at][0], held[k, 0], preferred_element_type=jnp.float32)
            total = term if total is None else total + term
            at += 1
    if not attend:
        refs[0][0] = total
        return
    gain_ref, out_ref = refs
    size = gain_ref.shape[2]
    gains = gain_ref[0]
    query = row_norm(total[:, :size], gains[0:1]).astype(jnp.bfloat16)
    key = row_norm(total[:, size : 2 * size], gains[1:2]).astype(jnp.bfloat16)
    value = total[:, 2 * size :].astype(jnp.bfloat16)
    for image in range(total.shape[0] // PATCHES):
        rows = slice(image * PATCHES, (image + 1) * PATCHES)
        scores = lax.dot_general(
            query[rows], key[rows], (((1,), (1,)), ((), ())), preferred_element_type=jnp.float32
        ) / math.sqrt(size)
        raised = jnp.exp(scores - jnp.max(scores, -1, keepdims=True))
        weights = (raised / jnp.sum(raised, -1, keepdims=True)).astype(jnp.bfloat16)
        out_ref[rows, :] = jnp.dot(
            weights, value[rows], preferred_element_type=jnp.float32
        ).astype(jnp.bfloat16)


def accumulate(columns, shards, index, total=None, gains=None):
    shards = [held if held.ndim == 4 else held[None] for held in shards]
    counts = tuple(held.shape[0] for held in shards)
    _, rows, depth = columns.shape
    heads, wide = shards[0].shape[1], shards[0].shape[3]
    in_specs = [
        pl.BlockSpec((1, rows, depth), functools.partial(lambda k, h, index: (index[k], 0, 0), k))
        for k in range(sum(counts))
    ]
    in_specs += [
        pl.BlockSpec((number, 1, depth, wide), lambda h, index: (0, h, 0, 0)) for number in counts
    ]
    operands = [columns] * sum(counts) + shards
    total_spec = pl.BlockSpec((1, rows, wide), lambda h, index: (h, 0, 0))
    if total is not None:
        in_specs.append(total_spec)
        operands.append(total)
    aliases = {}
    if gains is None:
        out_spec = total_spec
        out_shape = jax.ShapeDtypeStruct((heads, rows, wide), jnp.float32)
        if total is not None:
            aliases = {len(operands): 0}
    else:
        in_specs.append(pl.BlockSpec((1, 2, wide // 3), lambda h, index: (h, 0, 0)))
        operands.append(gains)
        out_spec = pl.BlockSpec((rows, wide // 3), lambda h, index: (0, h))
        out_shape = jax.ShapeDtypeStruct((rows, heads * wide // 3), jnp.bfloat16)
    flops = 2 * sum(counts) * rows * depth * wide * heads
    return pl.pallas_call(
        functools.partial(accumulate_kernel, counts, total is not None, gains is not None),
        grid_spec=pltpu.PrefetchScalarGridSpec(
            num_scalar_prefetch=1, grid=(heads,), in_specs=in_specs, out_specs=out_spec
        ),
        out_shape=out_shape,
        input_output_aliases=aliases,
        compiler_params=pltpu.CompilerParams(vmem_limit_bytes=VMEM),
        cost_estimate=pl.CostEstimate(
            flops=flops,
            bytes_accessed=2 * sum(counts) * (rows + heads * wide) * depth,
            transcendentals=0,
        ),
        name="accumulate",
    )(index, *operands)


def out_kernel(shard_counts, index_ref, *refs):
    near, refs = refs[:8], refs[8:]
    shards, refs = refs[: len(shard_counts)], refs[len(shard_counts) :]
    patches_ref, block_ref, stats_ref, total_ref = refs
    total_ref[...] = jnp.zeros_like(total_ref)
    at = 0
    for held, number in zip(shards, shard_counts):
        for k in range(number):
            place = index_ref[16 + at]
            half = index_ref[at] % 2
            for r in range(8):

                @pl.when(place == r)
                def _():
                    term = lax.dot_general(
                        near[r][...],
                        held[k],
                        (((1,), (1,)), ((), ())),
                        preferred_element_type=jnp.float32,
                    )
                    total_ref[half] += term.astype(jnp.bfloat16).astype(jnp.float32)

            at += 1
    depth = total_ref.shape[2]
    sums, squares = 0.0, 0.0
    for half in range(2):
        cols = slice(half * depth, (half + 1) * depth)
        block = (patches_ref[:, cols].astype(jnp.float32) + total_ref[half]).astype(jnp.bfloat16)
        block_ref[:, cols] = block
        block = block.astype(jnp.float32)
        sums += jnp.sum(block, 1, keepdims=True)
        squares += jnp.sum(block * block, 1, keepdims=True)
    stats_ref[0] = jnp.broadcast_to(sums, (sums.shape[0], stats_ref.shape[2]))
    stats_ref[1] = jnp.broadcast_to(squares, (sums.shape[0], stats_ref.shape[2]))


def out_project(near, shards, patches, index):
    shards = [held if held.ndim == 3 else held[None] for held in shards]
    counts = tuple(held.shape[0] for held in shards)
    rows, depth = near[0].shape
    in_specs = [pl.BlockSpec((rows, depth), lambda i, index: (0, 0)) for _ in near]
    in_specs += [
        pl.BlockSpec((number, depth, depth), lambda i, index: (0, 0, 0)) for number in counts
    ]
    in_specs.append(pl.BlockSpec((rows, 2 * depth), lambda i, index: (0, index[32])))
    return pl.pallas_call(
        functools.partial(out_kernel, counts),
        grid_spec=pltpu.PrefetchScalarGridSpec(
            num_scalar_prefetch=1,
            grid=(1,),
            in_specs=in_specs,
            out_specs=[
                pl.BlockSpec((rows, 2 * depth), lambda i, index: (0, 0)),
                pl.BlockSpec((2, rows, 8), lambda i, index: (0, 0, 0)),
            ],
            scratch_shapes=[pltpu.VMEM((2, rows, depth), jnp.float32)],
        ),
        out_shape=[
            jax.ShapeDtypeStruct((rows, 2 * depth), jnp.bfloat16),
            jax.ShapeDtypeStruct((2, rows, 8), jnp.float32),
        ],
        compiler_params=pltpu.CompilerParams(vmem_limit_bytes=VMEM),
        cost_estimate=pl.CostEstimate(
            flops=2 * 16 * rows * depth * depth,
            bytes_accessed=2 * 16 * (rows + depth) * depth,
            transcendentals=0,
        ),
        name="out_project",
    )(index, *near, *shards, patches)


def project_kernel(shard_counts, width, index_ref, *refs):
    block_ref, stats_ref, gain_ref = refs[:3]
    shards, refs = refs[3 : 3 + len(shard_counts)], refs[3 + len(shard_counts) :]
    far_low_ref, far_high_ref, right_ref, left_ref, own_ref, normed_ref = refs
    row_mean = stats_ref[0, :, 0:1] / width
    scale = lax.rsqrt(stats_ref[1, :, 0:1] / width - row_mean * row_mean + epsilon)
    depth = normed_ref.shape[2]
    for half in range(2):
        cols = slice(half * depth, (half + 1) * depth)
        values = block_ref[:, cols].astype(jnp.float32)
        normed_ref[half] = ((values - row_mean) * scale * gain_ref[:, cols]).astype(jnp.bfloat16)
    flat = []
    for held, number in zip(shards, shard_counts):
        for k in range(number):
            flat.append((held, k))
    middle = far_low_ref.shape[1]
    for pair in range(8):
        total = None
        for at in (2 * pair, 2 * pair + 1):
            held, k = flat[at]
            term = jnp.dot(
                normed_ref[index_ref[at] % 2], held[k], preferred_element_type=jnp.float32
            )
            total = term if total is None else total + term
        total = total.astype(jnp.bfloat16)
        place = index_ref[16 + 2 * pair]
        dz, dx = place // 4, place % 4

        @pl.when(dx == 0)
        def _():
            own_ref[dz] = total

        @pl.when(dx == 1)
        def _():
            right_ref[dz] = total

        @pl.when(dx == 2)
        def _():
            far_low_ref[dz] = total[:middle]
            far_high_ref[dz] = total[middle:]

        @pl.when(dx == 3)
        def _():
            left_ref[dz] = total


def project(block, stats, gain, shards, index, width):
    shards = [held if held.ndim == 3 else held[None] for held in shards]
    counts = tuple(held.shape[0] for held in shards)
    rows = block.shape[0]
    depth, wide = shards[0].shape[1:]
    in_specs = [
        pl.BlockSpec((rows, 2 * depth), lambda i, index: (0, 0)),
        pl.BlockSpec((2, rows, 8), lambda i, index: (0, 0, 0)),
        pl.BlockSpec((1, 2 * depth), lambda i, index: (0, index[32])),
    ]
    in_specs += [
        pl.BlockSpec((number, depth, wide), lambda i, index: (0, 0, 0)) for number in counts
    ]
    outs = [(2, rows // 2, wide)] * 2 + [(2, rows, wide)] * 3
    return pl.pallas_call(
        functools.partial(project_kernel, counts, width),
        grid_spec=pltpu.PrefetchScalarGridSpec(
            num_scalar_prefetch=1,
            grid=(1,),
            in_specs=in_specs,
            out_specs=[pl.BlockSpec(shape, lambda i, index: (0, 0, 0)) for shape in outs],
            scratch_shapes=[pltpu.VMEM((2, rows, depth), jnp.bfloat16)],
        ),
        out_shape=[jax.ShapeDtypeStruct(shape, jnp.bfloat16) for shape in outs],
        compiler_params=pltpu.CompilerParams(vmem_limit_bytes=VMEM),
        cost_estimate=pl.CostEstimate(
            flops=2 * 16 * rows * depth * wide,
            bytes_accessed=2 * 16 * (rows + depth) * wide,
            transcendentals=rows,
        ),
        name="project",
    )(index, block, stats, gain.reshape(1, width), *shards)


def gather_shards(own):
    other = swap_core(own)
    far = swap_zh(own)
    first = spread_y(jnp.stack([own, other]))
    far_other = swap_core(far)
    far_first = spread_y(jnp.stack([far, far_other]))
    second = spread_y(first[0])
    first_other = swap_core(first)
    far_second = spread_y(far_first[0])
    far_first_other = swap_core(far_first)
    second_other = swap_core(second)
    far_second_other = swap_core(far_second)
    return [
        own,
        other,
        far,
        far_other,
        first,
        first_other,
        far_first,
        far_first_other,
        second,
        second_other,
        far_second,
        far_second_other,
    ]


def local(
    patches,
    norm_gain,
    qkv_weight,
    qk_gain,
    out_weight,
    final_gain,
    proj_weight,
    text_embed,
    slot_offset,
    text_len,
):
    tok_count, width = patches.shape
    dp = lax.axis_index("dp")
    mp = lax.axis_index("mp")
    zl, x = mp // 4, mp % 4
    arrivals = jnp.asarray(arrival_table())[dp]
    relative = jnp.asarray(relative_table())[dp, mp]
    index = jnp.concatenate([arrivals, relative, mp[None].astype(jnp.int32)])

    heads_held = gather_shards(qkv_weight.transpose(1, 0, 2))
    out_held = gather_shards(transpose_mesh(out_weight))
    proj_held = gather_shards(transpose_mesh(proj_weight))

    columns = norm_columns(patches, norm_gain, 16)
    total = accumulate(columns, heads_held[0:2], arrivals[0:2])
    total = accumulate(columns, heads_held[2:4], arrivals[2:4], total)
    total = accumulate(columns, heads_held[4:6], arrivals[4:8], total)
    total = accumulate(columns, heads_held[6:8], arrivals[8:12], total)
    total = accumulate(columns, heads_held[8:10], arrivals[12:14], total)
    attended = accumulate(
        columns, heads_held[10:12], arrivals[14:16], total, qk_gain.transpose(1, 0, 2)
    )

    near = {(0, 0): attended, (1, 0): swap_zl(attended)}
    half = tok_count // 2
    for dz in range(2):
        mine = near[dz, 0]
        left = shift_x(mine, 1)
        right = shift_x(mine, -1)
        near[dz, 3] = left
        near[dz, 1] = right
        near[dz, 2] = jnp.concatenate([shift_x(left[:half], 1), shift_x(right[half:], -1)], 0)

    block_out, stats = out_project(
        [near[r // 4, r % 4] for r in range(8)], out_held, patches, index
    )
    stats = stats[:, :, 0].reshape(8, 128)
    stats = stats + swap_zl(stats)
    stats = stats + shift_x(stats, 1) + shift_x(stats, -1) + shift_x(stats, 2)
    stats = jnp.broadcast_to(stats.reshape(2, tok_count, 1), (2, tok_count, 8))

    far_low, far_high, right, left, own = project(
        block_out, stats, final_gain, proj_held, index, width
    )
    to_right = shift_x(far_high, 1)
    to_left = shift_x(far_low, -1)

    def plus(a, b):
        return (a.astype(jnp.float32) + b.astype(jnp.float32)).astype(jnp.bfloat16)

    right = jnp.concatenate([right[:, :half], plus(right[:, half:], to_right)], 1)
    left = jnp.concatenate([plus(left[:, :half], to_left), left[:, half:]], 1)
    total = (
        own.astype(jnp.float32)
        + shift_x(right, 1).astype(jnp.float32)
        + shift_x(left, -1).astype(jnp.float32)
    )
    total = total[0] + swap_zl(total[1].astype(jnp.bfloat16)).astype(jnp.float32)
    projected = total.astype(jnp.bfloat16).reshape(4, HALF, -1)

    first, second = slot_offset[0] // HALF, slot_offset[1] // HALF

    def source(block):
        in_first = (block >= first) & (block < first + 2)
        in_second = (block >= second) & (block < second + 2)
        at = jnp.where(in_first, block - first, jnp.where(in_second, block - second + 2, 0))
        return in_first | in_second, at

    arrived = []
    zero_value = jnp.zeros((), jnp.bfloat16)
    for dz in range(2):
        for dx in range(4):
            covered, at = source(((zl + dz) % 2) * 4 + (x + dx) % 4)
            block = lax.dynamic_index_in_dim(projected, at, 0, keepdims=False)
            block = jnp.where(covered, block, zero_value)
            if (dz, dx) != (0, 0):
                block = move(
                    block,
                    lambda zh, y, c, zl, x: (zh, y, c, (zl + dz) % 2, (x + dx) % 4),
                )
            arrived.append(block)
    arrived = jnp.stack(arrived)
    place = jnp.arange(8)
    relative = ((place // 4 + zl) % 2) * 4 + (x - place) % 4
    arrived = jnp.take(arrived, relative, axis=0).transpose(1, 0, 2).reshape(HALF, -1)

    covered, _ = source(mp)
    position = mp * HALF + jnp.arange(HALF, dtype=jnp.int32)
    before = jnp.clip(position - slot_offset[0], 0, PATCHES) + jnp.clip(
        position - slot_offset[1], 0, PATCHES
    )
    is_text = (position - before) < text_len[0]
    sequence = jnp.where(
        covered, arrived, jnp.where(is_text[:, None], text_embed[0], zero_value)
    )
    return (block_out, sequence[None])


def solution(mesh):
    in_specs = (
        P("dp", None),
        P(),
        P("dp", "mp", None),
        P(None, "mp", None),
        P("dp", "mp"),
        P(),
        P("dp", "mp"),
        P("dp", "mp", None),
        P("dp"),
        P("dp"),
    )
    out_specs = (P("dp", "mp"), P("dp", "mp", None))
    return jax.shard_map(local, mesh=mesh, in_specs=in_specs, out_specs=out_specs, check_vma=False)
```

```python
import functools
import math

import jax
import jax.numpy as jnp
import numpy as np
from jax import lax
from jax.experimental import pallas as pl
from jax.experimental.pallas import tpu as pltpu
from jax.sharding import PartitionSpec as P

PATCHES = 256
HALF = 128
AXES = ("dp", "mp")
VMEM = 40 * 1024 * 1024
epsilon = 1e-06


def coordinates():
    return [
        (zh, y, c, zl, x)
        for zh in range(2)
        for y in range(4)
        for c in range(2)
        for zl in range(2)
        for x in range(4)
    ]


def device_index(zh, y, c, zl, x):
    return ((zh * 4 + y) * 2 + c) * 8 + zl * 4 + x


def move(values, target):
    pairs = [(device_index(*at), device_index(*target(*at))) for at in coordinates()]
    return lax.ppermute(values, AXES, pairs)


def swap_core(values):
    return move(values, lambda zh, y, c, zl, x: (zh, y, 1 - c, zl, x))


def swap_zh(values):
    return move(values, lambda zh, y, c, zl, x: (1 - zh, y, c, zl, x))


def swap_zl(values):
    return move(values, lambda zh, y, c, zl, x: (zh, y, c, 1 - zl, x))


def spread_y(values):
    return move(values, lambda zh, y, c, zl, x: (zh, (y + 1 - 2 * c) % 4, c, zl, x))


def shift_x(values, step):
    return move(values, lambda zh, y, c, zl, x: (zh, y, c, zl, (x + step) % 4))


def transpose_mesh(values):
    return move(values, lambda zh, y, c, zl, x: (zl, x, c, zh, y))


def per_device(order):
    table = np.zeros((16, 16), np.int32)
    for zh in range(2):
        for y in range(4):
            for c in range(2):
                met = order(zh, y, c, 2 * c - 1)
                table[zh * 8 + y * 2 + c] = [r % 2 * 8 + yy % 4 * 2 + cc % 2 for r, yy, cc in met]
    return table


def early_order(zh, y, c, step):
    order = []
    for row in (zh, zh + 1):
        order += [(row, y, c), (row, y, c + 1)]
    for row in (zh, zh + 1):
        order += [(row, y + step, c), (row, y + step, c + 1)]
        order += [(row, y - step, c + 1), (row, y - step, c)]
    for row in (zh, zh + 1):
        order += [(row, y + 2, c), (row, y + 2, c + 1)]
    return order


def late_order(zh, y, c, step):
    order = []
    for yy, cores in (
        (y, (c, c + 1)),
        (y + step, (c, c + 1)),
        (y - step, (c + 1, c)),
        (y + 2, (c, c + 1)),
    ):
        for core in cores:
            order += [(zh, yy, core), (zh + 1, yy, core)]
    return order


NEAR = [(0, 0), (1, 0), (0, 1), (0, 3), (1, 1), (1, 3), (0, 2), (1, 2)]


def place_tables():
    met = per_device(late_order)
    groups = np.zeros((8, 8), np.int32)
    shards = np.zeros((16, 8, 16), np.int32)
    for mp in range(8):
        for r, (dz, dx) in enumerate(NEAR):
            group = (mp // 4 ^ dz) * 4 + (mp + dx) % 4
            groups[mp, r] = group
            for dp in range(16):
                for half in range(2):
                    shards[dp, mp, 2 * r + half] = np.argmax(met[dp] == 2 * group + half)
    return groups, shards


def norm_kernel(values_ref, gain_ref, out_ref):
    values = values_ref[...].astype(jnp.float32)
    width = values.shape[1]
    row_mean = jnp.sum(values, -1, keepdims=True) / width
    squares = jnp.sum(values * values, -1, keepdims=True) / width
    scale = lax.rsqrt(squares - row_mean * row_mean + epsilon)
    normed = ((values - row_mean) * scale * gain_ref[...]).astype(jnp.bfloat16)
    depth = out_ref.shape[2]
    for k in range(out_ref.shape[0]):
        out_ref[k] = normed[:, k * depth : (k + 1) * depth]


def norm_columns(values, gain, chunks):
    rows, width = values.shape
    block = 64
    return pl.pallas_call(
        norm_kernel,
        grid=(rows // block,),
        in_specs=[
            pl.BlockSpec((block, width), lambda i: (i, 0)),
            pl.BlockSpec((1, width), lambda i: (0, 0)),
        ],
        out_specs=pl.BlockSpec((chunks, block, width // chunks), lambda i: (0, i, 0)),
        out_shape=jax.ShapeDtypeStruct((chunks, rows, width // chunks), jnp.bfloat16),
        compiler_params=pltpu.CompilerParams(vmem_limit_bytes=VMEM),
        cost_estimate=pl.CostEstimate(
            flops=8 * rows * width, bytes_accessed=4 * rows * width, transcendentals=rows
        ),
        name="norm_columns",
    )(values, gain.reshape(1, width))


def row_norm(values, gain):
    row_mean = jnp.mean(values, -1, keepdims=True)
    squares = jnp.mean(values * values, -1, keepdims=True)
    return (values - row_mean) * lax.rsqrt(squares - row_mean * row_mean + epsilon) * gain


def accumulate_kernel(shard_counts, has_total, attend, index_ref, *refs):
    del index_ref
    count = sum(shard_counts)
    columns, refs = refs[:count], refs[count:]
    shards, refs = refs[: len(shard_counts)], refs[len(shard_counts) :]
    total = None
    if has_total:
        total, refs = refs[0][0], refs[1:]
    at = 0
    for held, number in zip(shards, shard_counts):
        for k in range(number):
            term = jnp.dot(columns[at][0], held[k, 0], preferred_element_type=jnp.float32)
            total = term if total is None else total + term
            at += 1
    if not attend:
        refs[0][0] = total
        return
    gain_ref, out_ref = refs
    size = gain_ref.shape[2]
    gains = gain_ref[0]
    query = row_norm(total[:, :size], gains[0:1]).astype(jnp.bfloat16)
    key = row_norm(total[:, size : 2 * size], gains[1:2]).astype(jnp.bfloat16)
    value = total[:, 2 * size :].astype(jnp.bfloat16)
    for image in range(total.shape[0] // PATCHES):
        rows = slice(image * PATCHES, (image + 1) * PATCHES)
        scores = lax.dot_general(
            query[rows], key[rows], (((1,), (1,)), ((), ())), preferred_element_type=jnp.float32
        ) / math.sqrt(size)
        raised = jnp.exp(scores - jnp.max(scores, -1, keepdims=True))
        weights = (raised / jnp.sum(raised, -1, keepdims=True)).astype(jnp.bfloat16)
        out_ref[rows, :] = jnp.dot(
            weights, value[rows], preferred_element_type=jnp.float32
        ).astype(jnp.bfloat16)


def accumulate(columns, shards, index, total=None, gains=None):
    shards = [held if held.ndim == 4 else held[None] for held in shards]
    counts = tuple(held.shape[0] for held in shards)
    _, rows, depth = columns.shape
    heads, wide = shards[0].shape[1], shards[0].shape[3]
    in_specs = [
        pl.BlockSpec((1, rows, depth), functools.partial(lambda k, h, index: (index[k], 0, 0), k))
        for k in range(sum(counts))
    ]
    in_specs += [
        pl.BlockSpec((number, 1, depth, wide), lambda h, index: (0, h, 0, 0)) for number in counts
    ]
    operands = [columns] * sum(counts) + shards
    total_spec = pl.BlockSpec((1, rows, wide), lambda h, index: (h, 0, 0))
    if total is not None:
        in_specs.append(total_spec)
        operands.append(total)
    aliases = {}
    if gains is None:
        out_spec = total_spec
        out_shape = jax.ShapeDtypeStruct((heads, rows, wide), jnp.float32)
        if total is not None:
            aliases = {len(operands): 0}
    else:
        in_specs.append(pl.BlockSpec((1, 2, wide // 3), lambda h, index: (h, 0, 0)))
        operands.append(gains)
        out_spec = pl.BlockSpec((rows, wide // 3), lambda h, index: (0, h))
        out_shape = jax.ShapeDtypeStruct((rows, heads * wide // 3), jnp.bfloat16)
    flops = 2 * sum(counts) * rows * depth * wide * heads
    return pl.pallas_call(
        functools.partial(accumulate_kernel, counts, total is not None, gains is not None),
        grid_spec=pltpu.PrefetchScalarGridSpec(
            num_scalar_prefetch=1, grid=(heads,), in_specs=in_specs, out_specs=out_spec
        ),
        out_shape=out_shape,
        input_output_aliases=aliases,
        compiler_params=pltpu.CompilerParams(vmem_limit_bytes=VMEM),
        cost_estimate=pl.CostEstimate(
            flops=flops,
            bytes_accessed=2 * sum(counts) * (rows + heads * wide) * depth,
            transcendentals=0,
        ),
        name="accumulate",
    )(index, *operands)


def out_kernel(split, has_total, finish, index_ref, *refs):
    del index_ref
    near, refs = refs[: sum(split)], refs[sum(split) :]
    shards, refs = refs[: 2 * len(split)], refs[2 * len(split) :]
    total = [refs[0][0], refs[0][1]] if has_total else [None, None]
    refs = refs[1:] if has_total else refs
    at = 0
    for piece, number in enumerate(split):
        values = near[at][...]
        if number == 2:
            values = jnp.concatenate([values, near[at + 1][...]], 0)
        at += number
        for half in range(2):
            term = lax.dot_general(
                values,
                shards[2 * piece + half][0],
                (((1,), (1,)), ((), ())),
                preferred_element_type=jnp.float32,
            )
            term = term.astype(jnp.bfloat16).astype(jnp.float32)
            total[half] = term if total[half] is None else total[half] + term
    if not finish:
        refs[0][0] = total[0]
        refs[0][1] = total[1]
        return
    patches_ref, block_ref, stats_ref = refs
    depth = total[0].shape[1]
    rows = total[0].shape[0]
    sums, squares = 0.0, 0.0
    for half in range(2):
        cols = slice(half * depth, (half + 1) * depth)
        block = (patches_ref[:, cols].astype(jnp.float32) + total[half]).astype(jnp.bfloat16)
        block_ref[:, cols] = block
        block = block.astype(jnp.float32)
        sums += jnp.sum(block, 1, keepdims=True)
        squares += jnp.sum(block * block, 1, keepdims=True)
    lane = lax.broadcasted_iota(jnp.int32, (rows, 128), 1)
    both = jnp.where(lane == 0, sums, squares)
    stats_ref[...] = both.T[:8]


def out_project(near, shards, index, total=None, patches=None):
    split = tuple(len(piece) for piece in near)
    pieces = [part for piece in near for part in piece]
    rows, depth = near[0][0].shape
    whole = lambda shape: pl.BlockSpec(shape, lambda i, index: (0,) * len(shape))
    in_specs = [whole(part.shape) for part in pieces]
    in_specs += [
        pl.BlockSpec(
            (1, depth, depth), functools.partial(lambda k, i, index: (index[k], 0, 0), k)
        )
        for k in range(2 * len(near))
    ]
    operands = pieces + [shards] * (2 * len(near))
    if total is not None:
        in_specs.append(whole(total.shape))
        operands.append(total)
    if patches is None:
        out_shape = jax.ShapeDtypeStruct((2, rows, depth), jnp.float32)
        out_specs = whole(out_shape.shape)
    else:
        in_specs.append(
            pl.BlockSpec((rows, 2 * depth), lambda i, index: (0, index[2 * len(near)]))
        )
        operands.append(patches)
        out_shape = [
            jax.ShapeDtypeStruct((rows, 2 * depth), jnp.bfloat16),
            jax.ShapeDtypeStruct((8, rows), jnp.float32),
        ]
        out_specs = [whole(out.shape) for out in out_shape]
    return pl.pallas_call(
        functools.partial(out_kernel, split, total is not None, patches is not None),
        grid_spec=pltpu.PrefetchScalarGridSpec(
            num_scalar_prefetch=1, grid=(1,), in_specs=in_specs, out_specs=out_specs
        ),
        out_shape=out_shape,
        compiler_params=pltpu.CompilerParams(vmem_limit_bytes=VMEM),
        cost_estimate=pl.CostEstimate(
            flops=4 * len(near) * rows * depth * depth,
            bytes_accessed=4 * len(near) * (rows + depth) * depth,
            transcendentals=0,
        ),
        name="out_project",
    )(index, *operands)


def project_kernel(split, has_total, finish, width, index_ref, *refs):
    near, refs = refs[: sum(split)], refs[sum(split) :]
    stats_ref, refs = refs[0], refs[1:]
    gains, refs = refs[: len(split)], refs[len(split) :]
    shards, refs = refs[: 2 * len(split)], refs[2 * len(split) :]
    total = None
    if has_total:
        total, refs = refs[0][...], refs[1:]
    rows = stats_ref.shape[1]
    row = lax.broadcasted_iota(jnp.int32, (128, rows), 0)
    stats = jnp.where(row == 0, stats_ref[0:1], stats_ref[1:2]).T
    row_mean = stats[:, 0:1] / width
    scale = lax.rsqrt(stats[:, 1:2] / width - row_mean * row_mean + epsilon)
    depth = shards[0].shape[1]
    at = 0
    for piece, number in enumerate(split):
        values = near[at][...]
        if number == 2:
            values = jnp.concatenate([values, near[at + 1][...]], 0)
        at += number
        values = values.astype(jnp.float32)
        normed = ((values - row_mean) * scale * gains[piece][...]).astype(jnp.bfloat16)
        for half in range(2):
            term = jnp.dot(
                normed[:, half * depth : (half + 1) * depth],
                shards[2 * piece + half][0],
                preferred_element_type=jnp.float32,
            )
            total = term if total is None else total + term
    if not finish:
        refs[0][...] = total
        return
    out_ref, held_ref = refs
    held_ref[...] = total.astype(jnp.bfloat16).reshape(held_ref.shape)
    at = 3 * len(split)
    for block in range(out_ref.shape[0]):
        source = index_ref[at + block]
        value = held_ref[jnp.maximum(source, 0)]
        out_ref[block] = jnp.where(source >= 0, value, jnp.zeros_like(value))


def project(near, stats, gain, shards, index, total=None, finish=False):
    split = tuple(len(piece) for piece in near)
    pieces = [part for piece in near for part in piece]
    rows = stats.shape[1]
    width = gain.shape[0]
    depth, wide = shards.shape[1:]
    count = len(near)
    whole = lambda shape: pl.BlockSpec(shape, lambda i, index: (0,) * len(shape))
    in_specs = [whole(part.shape) for part in pieces]
    in_specs.append(whole(stats.shape))
    in_specs += [
        pl.BlockSpec((1, 2 * depth), functools.partial(lambda k, i, index: (0, index[k]), k))
        for k in range(2 * count, 3 * count)
    ]
    in_specs += [
        pl.BlockSpec((1, depth, wide), functools.partial(lambda k, i, index: (index[k], 0, 0), k))
        for k in range(2 * count)
    ]
    operands = pieces + [stats] + [gain.reshape(1, width)] * count + [shards] * (2 * count)
    if total is not None:
        in_specs.append(whole(total.shape))
        operands.append(total)
    scratch = []
    if finish:
        out_shape = jax.ShapeDtypeStruct((8, HALF, wide), jnp.bfloat16)
        scratch = [pltpu.VMEM((rows // HALF, HALF, wide), jnp.bfloat16)]
    else:
        out_shape = jax.ShapeDtypeStruct((rows, wide), jnp.float32)
    return pl.pallas_call(
        functools.partial(project_kernel, split, total is not None, finish, width),
        grid_spec=pltpu.PrefetchScalarGridSpec(
            num_scalar_prefetch=1,
            grid=(1,),
            in_specs=in_specs,
            out_specs=whole(out_shape.shape),
            scratch_shapes=scratch,
        ),
        out_shape=out_shape,
        compiler_params=pltpu.CompilerParams(vmem_limit_bytes=VMEM),
        cost_estimate=pl.CostEstimate(
            flops=4 * count * rows * depth * wide,
            bytes_accessed=4 * count * (rows + wide) * depth,
            transcendentals=rows,
        ),
        name="project",
    )(index, *operands)


def pack_kernel(place_ref, arrived_ref, text_ref, out_ref):
    start, first, second, length = (place_ref[k] for k in range(4))
    rows, wide = arrived_ref.shape[1:]
    covered = ((start >= first) & (start < first + PATCHES)) | (
        (start >= second) & (start < second + PATCHES)
    )

    @pl.when(covered)
    def _():
        for k in range(arrived_ref.shape[0]):
            out_ref[:, k * wide : (k + 1) * wide] = arrived_ref[k]

    @pl.when(jnp.logical_not(covered))
    def _():
        position = start + lax.broadcasted_iota(jnp.int32, (rows, wide), 0)
        before = jnp.clip(position - first, 0, PATCHES) + jnp.clip(position - second, 0, PATCHES)
        is_text = position - before < length
        for k in range(arrived_ref.shape[0]):
            text = text_ref[:, k * wide : (k + 1) * wide].astype(jnp.float32)
            out_ref[:, k * wide : (k + 1) * wide] = jnp.where(is_text, text, 0.0).astype(
                jnp.bfloat16
            )


def pack(arrived, text, place):
    whole = lambda shape: pl.BlockSpec(shape, lambda i, index: (0,) * len(shape))
    return pl.pallas_call(
        pack_kernel,
        grid_spec=pltpu.PrefetchScalarGridSpec(
            num_scalar_prefetch=1,
            grid=(1,),
            in_specs=[whole(arrived.shape), whole(text.shape)],
            out_specs=whole(text.shape),
        ),
        out_shape=jax.ShapeDtypeStruct(text.shape, text.dtype),
        compiler_params=pltpu.CompilerParams(vmem_limit_bytes=VMEM),
        cost_estimate=pl.CostEstimate(
            flops=text.size, bytes_accessed=6 * text.size, transcendentals=0
        ),
        name="pack",
    )(place, arrived, text)


def after(values, *others):
    return lax.optimization_barrier((values, *others))[0]


def spread_x(mine):
    half = mine.shape[0] // 2
    right, left = shift_x(mine, -1), shift_x(mine, 1)
    return right, left, (shift_x(left[:half], 1), shift_x(right[half:], -1))


def local(
    patches,
    norm_gain,
    qkv_weight,
    qk_gain,
    out_weight,
    final_gain,
    proj_weight,
    text_embed,
    slot_offset,
    text_len,
):
    dp = lax.axis_index("dp")
    mp = lax.axis_index("mp")
    met = jnp.asarray(per_device(early_order))[dp]
    groups, shards = place_tables()
    groups, shards = jnp.asarray(groups)[mp], jnp.asarray(shards)[dp, mp]

    own = qkv_weight.transpose(1, 0, 2)
    other = swap_core(own)
    pair = jnp.stack([own, other])
    first = spread_y(pair)
    far = swap_zh(after(own, pair))
    columns = norm_columns(after(patches, pair), norm_gain, 16)
    total = accumulate(columns, [own, other], met[0:2])
    far_other = swap_core(after(far, total))
    far_first = spread_y(jnp.stack([far, far_other]))

    def prepare(own, far):
        mine = jnp.stack([own, far])
        return jnp.concatenate([mine, swap_core(mine)])

    turned = transpose_mesh(after(out_weight, far_other))
    proj_far = swap_zh(after(proj_weight, far_other))

    total = accumulate(columns, [far, far_other], met[2:4], total)
    first, total = lax.optimization_barrier((first, total))
    second = spread_y(first[0])
    first_other = swap_core(first)
    total = accumulate(columns, [first, first_other], met[4:8], total)

    turned_far = swap_zh(after(turned, first_other))
    far_first, total = lax.optimization_barrier((far_first, total))
    far_second = spread_y(far_first[0])
    far_first_other = swap_core(far_first)
    second_other = swap_core(second)
    out_quad = prepare(turned, turned_far)
    out_first = spread_y(after(out_quad, far_first_other))
    proj_quad = prepare(proj_weight, after(proj_far, far_first_other))
    total = accumulate(columns, [far_first, far_first_other], met[8:12], total)
    total = accumulate(columns, [second, second_other], met[12:14], total)
    far_second, total = lax.optimization_barrier((far_second, total))
    far_second_other = swap_core(far_second)
    attended = accumulate(
        columns, [far_second, far_second_other], met[14:16], total, qk_gain.transpose(1, 0, 2)
    )

    near_att = {(0, 0): (attended,)}
    att_z = swap_zl(attended)
    right, left, beyond = spread_x(attended)
    near_att[0, 1], near_att[0, 3], near_att[0, 2] = (right,), (left,), beyond
    near_att[1, 0] = (att_z,)
    right, left, beyond = spread_x(att_z)
    near_att[1, 1], near_att[1, 3], near_att[1, 2] = (right,), (left,), beyond

    out_first = after(out_first, attended)
    out_second = spread_y(out_first[:2])
    out_all = jnp.concatenate(
        [out_quad, out_first, swap_core(out_first), out_second, swap_core(out_second)]
    )
    proj_first = spread_y(after(proj_quad, out_first))
    proj_second = spread_y(proj_first[:2])
    proj_all = jnp.concatenate(
        [proj_quad, proj_first, swap_core(proj_first), proj_second, swap_core(proj_second)]
    )

    mp_slot = mp[None].astype(jnp.int32)
    partial = out_project([near_att[r] for r in NEAR[:4]], out_all, shards[:8])
    block_out, stats = out_project(
        [near_att[r] for r in NEAR[4:]],
        out_all,
        jnp.concatenate([shards[8:], mp_slot]),
        partial,
        patches,
    )

    near = {(0, 0): (block_out,)}
    block_z = swap_zl(block_out)
    right, left, beyond = spread_x(block_out)
    near[0, 1], near[0, 3], near[0, 2] = (right,), (left,), beyond
    stats = stats + swap_zl(stats)
    stats = stats + shift_x(stats, 1) + shift_x(stats, -1) + shift_x(stats, 2)
    near[1, 0] = (block_z,)
    right, left, beyond = spread_x(block_z)
    near[1, 1], near[1, 3], near[1, 2] = (right,), (left,), beyond

    slot = slot_offset // HALF
    block = jnp.arange(8, dtype=jnp.int32)
    in_first = (block >= slot[0]) & (block < slot[0] + 2)
    in_second = (block >= slot[1]) & (block < slot[1] + 2)
    source = jnp.where(in_first, block - slot[0], jnp.where(in_second, block - slot[1] + 2, -1))

    total = None
    for at in range(0, 8, 2):
        index = [shards[2 * at : 2 * at + 4], groups[at : at + 2]]
        index = jnp.concatenate(index + [source])
        total = project(
            [near[r] for r in NEAR[at : at + 2]], stats, final_gain, proj_all, index, total, at == 6
        )
    arrived = lax.all_to_all(total, "mp", split_axis=0, concat_axis=0, tiled=True)
    place = jnp.concatenate([mp_slot * HALF, slot_offset, text_len])
    sequence = pack(arrived, text_embed[0], place)
    return (block_out, sequence[None])


def solution(mesh):
    in_specs = (
        P("dp", None),
        P(),
        P("dp", "mp", None),
        P(None, "mp", None),
        P("dp", "mp"),
        P(),
        P("dp", "mp"),
        P("dp", "mp", None),
        P("dp"),
        P("dp"),
    )
    out_specs = (P("dp", "mp"), P("dp", "mp", None))
    return jax.shard_map(local, mesh=mesh, in_specs=in_specs, out_specs=out_specs, check_vma=False)
```

```python
import functools
import math

import jax
import jax.numpy as jnp
import numpy as np
from jax import lax
from jax.experimental import pallas as pl
from jax.experimental.pallas import tpu as pltpu
from jax.sharding import PartitionSpec as P

PATCHES = 256
HALF = 128
AXES = ("dp", "mp")
VMEM = 40 * 1024 * 1024
epsilon = 1e-06
SMALL = pl.CostEstimate(flops=1, bytes_accessed=1, transcendentals=0)


def coordinates():
    return [
        (zh, y, c, zl, x)
        for zh in range(2)
        for y in range(4)
        for c in range(2)
        for zl in range(2)
        for x in range(4)
    ]


def device_index(zh, y, c, zl, x):
    return ((zh * 4 + y) * 2 + c) * 8 + zl * 4 + x


def move(values, target):
    pairs = [(device_index(*at), device_index(*target(*at))) for at in coordinates()]
    return lax.ppermute(values, AXES, pairs)


def swap_core(values):
    return move(values, lambda zh, y, c, zl, x: (zh, y, 1 - c, zl, x))


def swap_zh(values):
    return move(values, lambda zh, y, c, zl, x: (1 - zh, y, c, zl, x))


def swap_zl(values):
    return move(values, lambda zh, y, c, zl, x: (zh, y, c, 1 - zl, x))


def spread_y(values):
    return move(values, lambda zh, y, c, zl, x: (zh, (y + 1 - 2 * c) % 4, c, zl, x))


def shift_x(values, step):
    return move(values, lambda zh, y, c, zl, x: (zh, y, c, zl, (x + step) % 4))


def transpose_mesh(values):
    return move(values, lambda zh, y, c, zl, x: (zl, x, c, zh, y))


def per_device(order):
    table = np.zeros((16, 16), np.int32)
    for zh in range(2):
        for y in range(4):
            for c in range(2):
                met = order(zh, y, c, 2 * c - 1)
                table[zh * 8 + y * 2 + c] = [r % 2 * 8 + yy % 4 * 2 + cc % 2 for r, yy, cc in met]
    return table


def early_order(zh, y, c, step):
    return [
        (zh, y, c),
        (zh, y, c + 1),
        (zh + 1, y, c),
        (zh + 1, y, c + 1),
        (zh, y + step, c),
        (zh, y - step, c + 1),
        (zh, y + step, c + 1),
        (zh, y - step, c),
        (zh + 1, y + step, c),
        (zh + 1, y - step, c + 1),
        (zh, y + 2, c),
        (zh, y + 2, c + 1),
        (zh + 1, y + step, c + 1),
        (zh + 1, y - step, c),
        (zh + 1, y + 2, c),
        (zh + 1, y + 2, c + 1),
    ]


def late_order(zh, y, c, step):
    order = []
    for yy, cores in (
        (y, (c, c + 1)),
        (y + step, (c, c + 1)),
        (y - step, (c + 1, c)),
        (y + 2, (c, c + 1)),
    ):
        for core in cores:
            order += [(zh, yy, core), (zh + 1, yy, core)]
    return order


NEAR = [(0, 0), (1, 0), (0, 1), (0, 3), (1, 1), (1, 3), (0, 2), (1, 2)]


def place_tables():
    met = per_device(late_order)
    groups = np.zeros((8, 8), np.int32)
    shards = np.zeros((16, 8, 16), np.int32)
    for mp in range(8):
        for r, (dz, dx) in enumerate(NEAR):
            group = (mp // 4 ^ dz) * 4 + (mp + dx) % 4
            groups[mp, r] = group
            for dp in range(16):
                for half in range(2):
                    shards[dp, mp, 2 * r + half] = np.argmax(met[dp] == 2 * group + half)
    return groups, shards


def norm_kernel(values_ref, gain_ref, out_ref):
    values = values_ref[...].astype(jnp.float32)
    width = values.shape[1]
    row_mean = jnp.sum(values, -1, keepdims=True) / width
    squares = jnp.sum(values * values, -1, keepdims=True) / width
    scale = lax.rsqrt(squares - row_mean * row_mean + epsilon)
    normed = ((values - row_mean) * scale * gain_ref[...]).astype(jnp.bfloat16)
    depth = out_ref.shape[2]
    for k in range(out_ref.shape[0]):
        out_ref[k] = normed[:, k * depth : (k + 1) * depth]


def norm_columns(values, gain, chunks):
    rows, width = values.shape
    block = 64
    return pl.pallas_call(
        norm_kernel,
        grid=(rows // block,),
        in_specs=[
            pl.BlockSpec((block, width), lambda i: (i, 0)),
            pl.BlockSpec((1, width), lambda i: (0, 0)),
        ],
        out_specs=pl.BlockSpec((chunks, block, width // chunks), lambda i: (0, i, 0)),
        out_shape=jax.ShapeDtypeStruct((chunks, rows, width // chunks), jnp.bfloat16),
        compiler_params=pltpu.CompilerParams(vmem_limit_bytes=VMEM),
        cost_estimate=SMALL,
        name="norm_columns",
    )(values, gain.reshape(1, width))


def row_norm(values, gain):
    row_mean = jnp.mean(values, -1, keepdims=True)
    squares = jnp.mean(values * values, -1, keepdims=True)
    return (values - row_mean) * lax.rsqrt(squares - row_mean * row_mean + epsilon) * gain


def accumulate_kernel(shard_counts, has_total, attend, index_ref, *refs):
    del index_ref
    count = sum(shard_counts)
    columns, refs = refs[:count], refs[count:]
    shards, refs = refs[: len(shard_counts)], refs[len(shard_counts) :]
    total = None
    if has_total:
        total, refs = refs[0][0], refs[1:]
    at = 0
    for held, number in zip(shards, shard_counts):
        for k in range(number):
            term = jnp.dot(columns[at][0], held[k, 0], preferred_element_type=jnp.float32)
            total = term if total is None else total + term
            at += 1
    if not attend:
        refs[0][0] = total
        return
    gain_ref, out_ref = refs
    size = gain_ref.shape[2]
    gains = gain_ref[0]
    query = row_norm(total[:, :size], gains[0:1]).astype(jnp.bfloat16)
    key = row_norm(total[:, size : 2 * size], gains[1:2]).astype(jnp.bfloat16)
    value = total[:, 2 * size :].astype(jnp.bfloat16)
    for image in range(total.shape[0] // PATCHES):
        rows = slice(image * PATCHES, (image + 1) * PATCHES)
        scores = lax.dot_general(
            query[rows], key[rows], (((1,), (1,)), ((), ())), preferred_element_type=jnp.float32
        ) / math.sqrt(size)
        raised = jnp.exp(scores - jnp.max(scores, -1, keepdims=True))
        weights = (raised / jnp.sum(raised, -1, keepdims=True)).astype(jnp.bfloat16)
        out_ref[rows, :] = jnp.dot(
            weights, value[rows], preferred_element_type=jnp.float32
        ).astype(jnp.bfloat16)


def accumulate(columns, shards, index, total=None, gains=None):
    shards = [held if held.ndim == 4 else held[None] for held in shards]
    counts = tuple(held.shape[0] for held in shards)
    _, rows, depth = columns.shape
    heads, wide = shards[0].shape[1], shards[0].shape[3]
    in_specs = [
        pl.BlockSpec((1, rows, depth), functools.partial(lambda k, h, index: (index[k], 0, 0), k))
        for k in range(sum(counts))
    ]
    in_specs += [
        pl.BlockSpec((number, 1, depth, wide), lambda h, index: (0, h, 0, 0)) for number in counts
    ]
    operands = [columns] * sum(counts) + shards
    total_spec = pl.BlockSpec((1, rows, wide), lambda h, index: (h, 0, 0))
    if total is not None:
        in_specs.append(total_spec)
        operands.append(total)
    aliases = {}
    if gains is None:
        out_spec = total_spec
        out_shape = jax.ShapeDtypeStruct((heads, rows, wide), jnp.float32)
        if total is not None:
            aliases = {len(operands): 0}
    else:
        in_specs.append(pl.BlockSpec((1, 2, wide // 3), lambda h, index: (h, 0, 0)))
        operands.append(gains)
        out_spec = pl.BlockSpec((rows, wide // 3), lambda h, index: (0, h))
        out_shape = jax.ShapeDtypeStruct((rows, heads * wide // 3), jnp.bfloat16)
    return pl.pallas_call(
        functools.partial(accumulate_kernel, counts, total is not None, gains is not None),
        grid_spec=pltpu.PrefetchScalarGridSpec(
            num_scalar_prefetch=1, grid=(heads,), in_specs=in_specs, out_specs=out_spec
        ),
        out_shape=out_shape,
        input_output_aliases=aliases,
        compiler_params=pltpu.CompilerParams(vmem_limit_bytes=VMEM),
        cost_estimate=SMALL,
        name="accumulate",
    )(index, *operands)


def load_shards(parts, held_ref, sems):
    at = 0
    copies = []
    for k, part in enumerate(parts):
        number = part.shape[0]
        copies.append(pltpu.make_async_copy(part, held_ref.at[pl.ds(at, number)], sems.at[k]))
        at += number
    for copy in copies:
        copy.start()
    for copy in copies:
        copy.wait()


def read_piece(piece, refs):
    parts = [refs[k][first:last] for k, first, last in piece]
    return parts[0] if len(parts) == 1 else jnp.concatenate(parts, 0)


def out_kernel(pieces, held, count, index_ref, *refs):
    near, refs = refs[:held], refs[held:]
    parts, refs = refs[:count], refs[count:]
    patches_ref, block_ref, stats_ref, held_ref, sems = refs
    load_shards(parts, held_ref, sems)
    depth = held_ref.shape[1]
    rows = patches_ref.shape[0]
    sums, squares = 0.0, 0.0
    for half in range(2):
        total = None
        for k, piece in enumerate(pieces):
            term = lax.dot_general(
                read_piece(piece, near),
                held_ref[index_ref[2 * k + half]],
                (((1,), (1,)), ((), ())),
                preferred_element_type=jnp.float32,
            )
            term = term.astype(jnp.bfloat16).astype(jnp.float32)
            total = term if total is None else total + term
        cols = slice(half * depth, (half + 1) * depth)
        block = (patches_ref[:, cols].astype(jnp.float32) + total).astype(jnp.bfloat16)
        block_ref[:, cols] = block
        block = block.astype(jnp.float32)
        sums += jnp.sum(block, 1, keepdims=True)
        squares += jnp.sum(block * block, 1, keepdims=True)
    lane = lax.broadcasted_iota(jnp.int32, (rows, 128), 1)
    both = jnp.where(lane == 0, sums, squares)
    stats_ref[...] = both.T[:8]


def whole(shape):
    return pl.BlockSpec(shape, lambda i, index: (0,) * len(shape))


def out_project(near, pieces, parts, index, patches):
    rows, depth = near[0].shape
    in_specs = [whole(part.shape) for part in near]
    in_specs += [pl.BlockSpec(memory_space=pl.ANY) for _ in parts]
    in_specs.append(pl.BlockSpec((rows, 2 * depth), lambda i, index: (0, index[16])))
    out_shape = [
        jax.ShapeDtypeStruct((rows, 2 * depth), jnp.bfloat16),
        jax.ShapeDtypeStruct((8, rows), jnp.float32),
    ]
    return pl.pallas_call(
        functools.partial(out_kernel, pieces, len(near), len(parts)),
        grid_spec=pltpu.PrefetchScalarGridSpec(
            num_scalar_prefetch=1,
            grid=(1,),
            in_specs=in_specs,
            out_specs=[whole(out.shape) for out in out_shape],
            scratch_shapes=[
                pltpu.VMEM((16, depth, depth), jnp.bfloat16),
                pltpu.SemaphoreType.DMA((len(parts),)),
            ],
        ),
        out_shape=out_shape,
        compiler_params=pltpu.CompilerParams(vmem_limit_bytes=VMEM),
        cost_estimate=SMALL,
        name="out_project",
    )(index, *near, *parts, patches)


def project_kernel(pieces, held, count, kept, finish, width, index_ref, *refs):
    near, refs = refs[:held], refs[held:]
    stats_ref, refs = refs[0], refs[1:]
    gains, refs = refs[: len(pieces)], refs[len(pieces) :]
    parts, refs = refs[:count], refs[count:]
    if finish:
        total, (out_ref, held_ref, sems, blocks_ref) = refs[0][...], refs[1:]
    else:
        total, (out_ref, kept_ref, held_ref, sems) = None, refs
    load_shards(parts, held_ref, sems)
    rows = stats_ref.shape[1]
    row = lax.broadcasted_iota(jnp.int32, (128, rows), 0)
    stats = jnp.where(row == 0, stats_ref[0:1], stats_ref[1:2]).T
    row_mean = stats[:, 0:1] / width
    scale = lax.rsqrt(stats[:, 1:2] / width - row_mean * row_mean + epsilon)
    depth = held_ref.shape[1]
    for k, piece in enumerate(pieces):
        values = read_piece(piece, near).astype(jnp.float32)
        normed = ((values - row_mean) * scale * gains[k][...]).astype(jnp.bfloat16)
        for half in range(2):
            at = 2 * k + half if finish else index_ref[2 * k + half]
            term = jnp.dot(
                normed[:, half * depth : (half + 1) * depth],
                held_ref[at],
                preferred_element_type=jnp.float32,
            )
            total = term if total is None else total + term
    if not finish:
        out_ref[...] = total
        for k in range(kept):
            kept_ref[k] = held_ref[index_ref[2 * len(pieces) + k]]
        return
    blocks_ref[...] = total.astype(jnp.bfloat16).reshape(blocks_ref.shape)
    for block in range(out_ref.shape[0]):
        source = index_ref[len(pieces) + block]
        value = blocks_ref[jnp.maximum(source, 0)]
        out_ref[block] = jnp.where(source >= 0, value, jnp.zeros_like(value))


def project(near, pieces, stats, gain, parts, index, kept=0, total=None):
    rows = stats.shape[1]
    width = gain.shape[0]
    depth, wide = parts[0].shape[1:]
    count = len(pieces)
    finish = total is not None
    at = 0 if finish else 2 * count + kept
    in_specs = [whole(part.shape) for part in near]
    in_specs.append(whole(stats.shape))
    in_specs += [
        pl.BlockSpec((1, 2 * depth), functools.partial(lambda k, i, index: (0, index[k]), k))
        for k in range(at, at + count)
    ]
    in_specs += [pl.BlockSpec(memory_space=pl.ANY) for _ in parts]
    operands = list(near) + [stats] + [gain.reshape(1, width)] * count + list(parts)
    scratch = [
        pltpu.VMEM((sum(part.shape[0] for part in parts), depth, wide), jnp.bfloat16),
        pltpu.SemaphoreType.DMA((len(parts),)),
    ]
    if finish:
        in_specs.append(whole(total.shape))
        operands.append(total)
        out_shape = [jax.ShapeDtypeStruct((8, HALF, wide), jnp.bfloat16)]
        scratch.append(pltpu.VMEM((rows // HALF, HALF, wide), jnp.bfloat16))
    else:
        out_shape = [
            jax.ShapeDtypeStruct((rows, wide), jnp.float32),
            jax.ShapeDtypeStruct((kept, depth, wide), jnp.bfloat16),
        ]
    return pl.pallas_call(
        functools.partial(
            project_kernel, pieces, len(near), len(parts), kept, finish, width
        ),
        grid_spec=pltpu.PrefetchScalarGridSpec(
            num_scalar_prefetch=1,
            grid=(1,),
            in_specs=in_specs,
            out_specs=[whole(out.shape) for out in out_shape],
            scratch_shapes=scratch,
        ),
        out_shape=out_shape,
        compiler_params=pltpu.CompilerParams(vmem_limit_bytes=VMEM),
        cost_estimate=SMALL,
        name="project",
    )(index, *operands)


def pack_kernel(place_ref, arrived_ref, text_ref, out_ref):
    start, first, second, length = (place_ref[k] for k in range(4))
    rows, wide = arrived_ref.shape[1:]
    covered = ((start >= first) & (start < first + PATCHES)) | (
        (start >= second) & (start < second + PATCHES)
    )

    @pl.when(covered)
    def _():
        for k in range(arrived_ref.shape[0]):
            out_ref[:, k * wide : (k + 1) * wide] = arrived_ref[k]

    @pl.when(jnp.logical_not(covered))
    def _():
        position = start + lax.broadcasted_iota(jnp.int32, (rows, wide), 0)
        before = jnp.clip(position - first, 0, PATCHES) + jnp.clip(position - second, 0, PATCHES)
        is_text = position - before < length
        for k in range(arrived_ref.shape[0]):
            text = text_ref[:, k * wide : (k + 1) * wide].astype(jnp.float32)
            out_ref[:, k * wide : (k + 1) * wide] = jnp.where(is_text, text, 0.0).astype(
                jnp.bfloat16
            )


def pack(arrived, text, place):
    return pl.pallas_call(
        pack_kernel,
        grid_spec=pltpu.PrefetchScalarGridSpec(
            num_scalar_prefetch=1,
            grid=(1,),
            in_specs=[whole(arrived.shape), whole(text.shape)],
            out_specs=whole(text.shape),
        ),
        out_shape=jax.ShapeDtypeStruct(text.shape, text.dtype),
        compiler_params=pltpu.CompilerParams(vmem_limit_bytes=VMEM),
        cost_estimate=SMALL,
        name="pack",
    )(place, arrived, text)


def join(*values):
    return lax.optimization_barrier(values)


def local(
    patches,
    norm_gain,
    qkv_weight,
    qk_gain,
    out_weight,
    final_gain,
    proj_weight,
    text_embed,
    slot_offset,
    text_len,
):
    dp = lax.axis_index("dp")
    mp = lax.axis_index("mp")
    met = jnp.asarray(per_device(early_order))[dp]
    groups, shards = place_tables()
    groups, shards = jnp.asarray(groups)[mp], jnp.asarray(shards)[dp, mp]
    mp_slot = mp[None].astype(jnp.int32)

    own = qkv_weight.transpose(1, 0, 2)
    turned = transpose_mesh(out_weight)
    (other,) = join(swap_core(own))
    first = spread_y(join(own, other)[0])
    beside = spread_y(other)
    far = swap_zh(join(own, other)[0])
    columns = norm_columns(join(patches, other)[0], norm_gain, 16)
    total = accumulate(columns, [own, other], met[0:2])

    far, first, beside, turned, total = join(far, first, beside, turned, total)
    far_first = spread_y(far)
    second = spread_y(first)
    far_other, first_other, beside_other = join(
        swap_core(far), swap_core(first), swap_core(beside)
    )
    far_beside = spread_y(far_other)
    turned_far = swap_zh(join(turned, far_other)[0])
    proj_far = swap_zh(join(proj_weight, far_other)[0])
    total = accumulate(
        columns,
        [far, far_other, first, first_other, beside, beside_other],
        met[2:8],
        total,
    )

    far_first, second, far_beside, turned_far, proj_far, total = join(
        far_first, second, far_beside, turned_far, proj_far, total
    )
    far_second = spread_y(far_first)
    far_first_other, second_other, far_beside_other = join(
        swap_core(far_first), swap_core(second), swap_core(far_beside)
    )
    out_mine = jnp.stack([turned, join(turned_far, second_other)[0]])
    proj_mine = jnp.stack([proj_weight, join(proj_far, second_other)[0]])
    out_other = swap_core(out_mine)
    proj_other = swap_core(proj_mine)
    total = accumulate(
        columns,
        [far_first, far_first_other, second, second_other, far_beside, far_beside_other],
        met[8:14],
        total,
    )

    far_second, out_other, proj_other, total = join(far_second, out_other, proj_other, total)
    far_second_other = swap_core(far_second)
    out_quad = jnp.concatenate([out_mine, out_other])
    proj_quad = jnp.concatenate([proj_mine, proj_other])
    out_first = spread_y(out_quad)
    attended = accumulate(
        columns, [far_second, far_second_other], met[14:16], total, qk_gain.transpose(1, 0, 2)
    )

    out_quad, proj_quad = join(out_quad, proj_quad)
    rows = attended.shape[0]
    half = rows // 2
    middle = rows * 9 // 16
    quarter = middle // 2
    late = middle - half
    pieces = (
        ((0, 0, rows),),
        ((1, 0, rows),),
        ((2, 0, rows),),
        ((3, 0, rows),),
        ((5, half, half + middle), (6, 0, rows - middle)),
        ((4, half, half + middle), (6, rows - middle, 2 * (rows - middle))),
        ((4, 0, half), (5, 0, half)),
        ((7, 0, quarter), (8, 0, quarter), (9, 0, rows - middle)),
    )

    def gather_first(mine):
        return [swap_zl(mine), shift_x(mine, -1), shift_x(mine, 1)]

    def gather_second(far, right, left):
        return [
            shift_x(jnp.concatenate([left[:half], far[:middle]]), 1),
            shift_x(jnp.concatenate([right[half:], far[:middle]]), -1),
            swap_zl(jnp.concatenate([right[middle:], left[middle:]])),
        ]

    def gather_third(from_left, from_right):
        return [
            shift_x(from_left[half : half + quarter], 1),
            shift_x(from_right[half + quarter :], -1),
            swap_zl(from_right[late:half]),
        ]

    near = [attended]
    *got, out_first = join(*gather_first(attended), out_first)
    near += got
    out_second = spread_y(out_first[:2])
    out_first_other = swap_core(out_first)
    *got, out_second, out_first_other = join(*gather_second(*got), out_second, out_first_other)
    near += got
    proj_first = spread_y(join(proj_quad, out_second)[0])
    out_second_other = swap_core(out_second)
    *got, out_second_other = join(*gather_third(*got[:2]), out_second_other)
    near += got
    block_out, stats = out_project(
        near,
        pieces,
        [out_quad, out_first, out_first_other, out_second, out_second_other],
        jnp.concatenate([shards, mp_slot]),
        patches,
    )

    near = [block_out]
    sent = gather_first(block_out)
    stats_x = join(shift_x(stats, 1), shift_x(stats, -1), shift_x(stats, 2))
    stats = stats + stats_x[0] + stats_x[1] + stats_x[2]
    *got, proj_first, stats = join(*sent, proj_first, stats)
    near += got
    proj_second = spread_y(proj_first[:2])
    proj_first_other = swap_core(proj_first)
    *got, proj_second, proj_first_other, stats_z = join(
        *gather_second(*got), proj_second, proj_first_other, swap_zl(stats)
    )
    near += got
    stats = stats + stats_z
    last = gather_third(*got[:2])
    proj_second_other = swap_core(proj_second)

    slot = slot_offset // HALF
    block = jnp.arange(8, dtype=jnp.int32)
    in_first = (block >= slot[0]) & (block < slot[0] + 2)
    in_second = (block >= slot[1]) & (block < slot[1] + 2)
    source = jnp.where(in_first, block - slot[0], jnp.where(in_second, block - slot[1] + 2, -1))

    total, left = project(
        near,
        pieces[:7],
        stats,
        final_gain,
        [proj_quad, proj_first, proj_first_other, proj_second, proj_second_other],
        jnp.concatenate([shards, groups[:7]]),
        kept=2,
    )
    (outgoing,) = project(
        last,
        (tuple((k - 7, first, last) for k, first, last in pieces[7]),),
        stats,
        final_gain,
        [left],
        jnp.concatenate([groups[7:], source]),
        total=total,
    )
    arrived = lax.all_to_all(outgoing, "mp", split_axis=0, concat_axis=0, tiled=True)
    place = jnp.concatenate([mp_slot * HALF, slot_offset, text_len])
    sequence = pack(arrived, text_embed[0], place)
    return (block_out, sequence[None])


def solution(mesh):
    in_specs = (
        P("dp", None),
        P(),
        P("dp", "mp", None),
        P(None, "mp", None),
        P("dp", "mp"),
        P(),
        P("dp", "mp"),
        P("dp", "mp", None),
        P("dp"),
        P("dp"),
    )
    out_specs = (P("dp", "mp"), P("dp", "mp", None))
    return jax.shard_map(local, mesh=mesh, in_specs=in_specs, out_specs=out_specs, check_vma=False)
```

```python
import functools
import math

import jax
import jax.numpy as jnp
import numpy as np
from jax import lax
from jax.experimental import pallas as pl
from jax.experimental.pallas import tpu as pltpu
from jax.sharding import PartitionSpec as P

PATCHES = 256
HALF = 128
AXES = ("dp", "mp")
MEGA = 1024 * 1024
epsilon = 1e-06
SMALL = pl.CostEstimate(flops=1, bytes_accessed=1, transcendentals=0)


def coordinates():
    return [
        (zh, y, c, zl, x)
        for zh in range(2)
        for y in range(4)
        for c in range(2)
        for zl in range(2)
        for x in range(4)
    ]


def device_index(zh, y, c, zl, x):
    return ((zh * 4 + y) * 2 + c) * 8 + zl * 4 + x


def move(values, target):
    pairs = [(device_index(*at), device_index(*target(*at))) for at in coordinates()]
    return lax.ppermute(values, AXES, pairs)


def swap_core(values):
    return move(values, lambda zh, y, c, zl, x: (zh, y, 1 - c, zl, x))


def swap_zh(values):
    return move(values, lambda zh, y, c, zl, x: (1 - zh, y, c, zl, x))


def swap_zl(values):
    return move(values, lambda zh, y, c, zl, x: (zh, y, c, 1 - zl, x))


def spread_y(values):
    return move(values, lambda zh, y, c, zl, x: (zh, (y + 1 - 2 * c) % 4, c, zl, x))


def shift_x(values, step):
    return move(values, lambda zh, y, c, zl, x: (zh, y, c, zl, (x + step) % 4))


def transpose_mesh(values):
    return move(values, lambda zh, y, c, zl, x: (zl, x, c, zh, y))


def per_device(order):
    table = np.zeros((16, 16), np.int32)
    for zh in range(2):
        for y in range(4):
            for c in range(2):
                met = order(zh, y, c, 2 * c - 1)
                table[zh * 8 + y * 2 + c] = [r % 2 * 8 + yy % 4 * 2 + cc % 2 for r, yy, cc in met]
    return table


def early_order(zh, y, c, step):
    return [
        (zh, y, c),
        (zh, y, c + 1),
        (zh + 1, y, c),
        (zh + 1, y, c + 1),
        (zh, y + step, c),
        (zh, y - step, c + 1),
        (zh, y + step, c + 1),
        (zh, y - step, c),
        (zh + 1, y + step, c),
        (zh + 1, y - step, c + 1),
        (zh, y + 2, c),
        (zh, y + 2, c + 1),
        (zh + 1, y + step, c + 1),
        (zh + 1, y - step, c),
        (zh + 1, y + 2, c),
        (zh + 1, y + 2, c + 1),
    ]


def late_order(zh, y, c, step):
    order = []
    for yy, cores in (
        (y, (c, c + 1)),
        (y + step, (c, c + 1)),
        (y - step, (c + 1, c)),
        (y + 2, (c, c + 1)),
    ):
        for core in cores:
            order += [(zh, yy, core), (zh + 1, yy, core)]
    return order


NEAR = [(0, 0), (1, 0), (0, 1), (0, 3), (0, 2), (1, 1), (1, 3), (1, 2)]


def place_tables():
    met = per_device(late_order)
    groups = np.zeros((8, 8), np.int32)
    shards = np.zeros((16, 8, 16), np.int32)
    for mp in range(8):
        for r, (dz, dx) in enumerate(NEAR):
            group = (mp // 4 ^ dz) * 4 + (mp + dx) % 4
            groups[mp, r] = group
            for dp in range(16):
                for half in range(2):
                    shards[dp, mp, 2 * r + half] = np.argmax(met[dp] == 2 * group + half)
    return groups, shards


def norm_kernel(values_ref, gain_ref, out_ref):
    values = values_ref[...].astype(jnp.float32)
    width = values.shape[1]
    row_mean = jnp.sum(values, -1, keepdims=True) / width
    squares = jnp.sum(values * values, -1, keepdims=True) / width
    scale = lax.rsqrt(squares - row_mean * row_mean + epsilon)
    normed = ((values - row_mean) * scale * gain_ref[...]).astype(jnp.bfloat16)
    depth = out_ref.shape[2]
    for k in range(out_ref.shape[0]):
        out_ref[k] = normed[:, k * depth : (k + 1) * depth]


def norm_columns(values, gain, chunks):
    rows, width = values.shape
    block = 64
    return pl.pallas_call(
        norm_kernel,
        grid=(rows // block,),
        in_specs=[
            pl.BlockSpec((block, width), lambda i: (i, 0)),
            pl.BlockSpec((1, width), lambda i: (0, 0)),
        ],
        out_specs=pl.BlockSpec((chunks, block, width // chunks), lambda i: (0, i, 0)),
        out_shape=jax.ShapeDtypeStruct((chunks, rows, width // chunks), jnp.bfloat16),
        compiler_params=pltpu.CompilerParams(vmem_limit_bytes=16 * MEGA),
        cost_estimate=SMALL,
        name="norm_columns",
    )(values, gain.reshape(1, width))


def row_norm(values, gain):
    row_mean = jnp.mean(values, -1, keepdims=True)
    squares = jnp.mean(values * values, -1, keepdims=True)
    return (values - row_mean) * lax.rsqrt(squares - row_mean * row_mean + epsilon) * gain


def accumulate_kernel(shard_counts, has_total, attend, index_ref, *refs):
    del index_ref
    count = sum(shard_counts)
    columns, refs = refs[:count], refs[count:]
    shards, refs = refs[: len(shard_counts)], refs[len(shard_counts) :]
    total = None
    if has_total:
        total, refs = refs[0][0], refs[1:]
    at = 0
    for held, number in zip(shards, shard_counts):
        for k in range(number):
            term = jnp.dot(columns[at][0], held[k, 0], preferred_element_type=jnp.float32)
            total = term if total is None else total + term
            at += 1
    if not attend:
        refs[0][0] = total
        return
    gain_ref, out_ref, *image_refs = refs
    size = gain_ref.shape[2]
    gains = gain_ref[0]
    query = row_norm(total[:, :size], gains[0:1]).astype(jnp.bfloat16)
    key = row_norm(total[:, size : 2 * size], gains[1:2]).astype(jnp.bfloat16)
    value = total[:, 2 * size :].astype(jnp.bfloat16)
    for image in range(total.shape[0] // PATCHES):
        rows = slice(image * PATCHES, (image + 1) * PATCHES)
        scores = lax.dot_general(
            query[rows], key[rows], (((1,), (1,)), ((), ())), preferred_element_type=jnp.float32
        ) / math.sqrt(size)
        raised = jnp.exp(scores - jnp.max(scores, -1, keepdims=True))
        weights = (raised / jnp.sum(raised, -1, keepdims=True)).astype(jnp.bfloat16)
        attended = jnp.dot(weights, value[rows], preferred_element_type=jnp.float32)
        attended = attended.astype(jnp.bfloat16)
        out_ref[rows, :] = attended
        image_refs[image][...] = attended


def accumulate(columns, shards, index, total=None, gains=None):
    shards = [held if held.ndim == 4 else held[None] for held in shards]
    counts = tuple(held.shape[0] for held in shards)
    _, rows, depth = columns.shape
    heads, wide = shards[0].shape[1], shards[0].shape[3]
    in_specs = [
        pl.BlockSpec((1, rows, depth), functools.partial(lambda k, h, index: (index[k], 0, 0), k))
        for k in range(sum(counts))
    ]
    in_specs += [
        pl.BlockSpec((number, 1, depth, wide), lambda h, index: (0, h, 0, 0)) for number in counts
    ]
    operands = [columns] * sum(counts) + shards
    total_spec = pl.BlockSpec((1, rows, wide), lambda h, index: (h, 0, 0))
    if total is not None:
        in_specs.append(total_spec)
        operands.append(total)
    aliases = {}
    if gains is None:
        out_spec = total_spec
        out_shape = jax.ShapeDtypeStruct((heads, rows, wide), jnp.float32)
        if total is not None:
            aliases = {len(operands): 0}
    else:
        in_specs.append(pl.BlockSpec((1, 2, wide // 3), lambda h, index: (h, 0, 0)))
        operands.append(gains)
        sizes = [rows] + [PATCHES] * (rows // PATCHES)
        out_spec = [pl.BlockSpec((size, wide // 3), lambda h, index: (0, h)) for size in sizes]
        out_shape = [
            jax.ShapeDtypeStruct((size, heads * wide // 3), jnp.bfloat16) for size in sizes
        ]
    return pl.pallas_call(
        functools.partial(accumulate_kernel, counts, total is not None, gains is not None),
        grid_spec=pltpu.PrefetchScalarGridSpec(
            num_scalar_prefetch=1, grid=(heads,), in_specs=in_specs, out_specs=out_spec
        ),
        out_shape=out_shape,
        input_output_aliases=aliases,
        compiler_params=pltpu.CompilerParams(vmem_limit_bytes=20 * MEGA),
        cost_estimate=SMALL,
        name="accumulate",
    )(index, *operands)


def load_shards(parts, held_ref, sems):
    at = 0
    copies = []
    for k, part in enumerate(parts):
        number = part.shape[0]
        copies.append(pltpu.make_async_copy(part, held_ref.at[pl.ds(at, number)], sems.at[k]))
        at += number
    for copy in copies:
        copy.start()
    for copy in copies:
        copy.wait()


def read_piece(piece, refs):
    parts = [refs[k][...] for k in piece]
    return parts[0] if len(parts) == 1 else jnp.concatenate(parts, 0)


def out_kernel(pieces, held, count, kept, finish, index_ref, *refs):
    near, refs = refs[:held], refs[held:]
    parts, refs = refs[:count], refs[count:]
    if finish:
        given_ref, own_ref, block_ref, *half_refs, stats_ref, held_ref, sems = refs
    else:
        total_ref, kept_ref, held_ref, sems = refs
    load_shards(parts, held_ref, sems)
    depth = held_ref.shape[1]
    sums, squares = 0.0, 0.0
    for half in range(2):
        total = given_ref[half] if finish else None
        for k, piece in enumerate(pieces):
            term = lax.dot_general(
                read_piece(piece, near),
                held_ref[2 * k + half if finish else index_ref[2 * k + half]],
                (((1,), (1,)), ((), ())),
                preferred_element_type=jnp.float32,
            )
            term = term.astype(jnp.bfloat16).astype(jnp.float32)
            total = term if total is None else total + term
        if not finish:
            total_ref[half] = total
            continue
        cols = slice(half * depth, (half + 1) * depth)
        block = (own_ref[:, cols].astype(jnp.float32) + total).astype(jnp.bfloat16)
        block_ref[:, cols] = block
        rows = block.shape[0] // 2
        half_refs[0][:, cols] = block[:rows]
        half_refs[1][:, cols] = block[rows:]
        block = block.astype(jnp.float32)
        sums += jnp.sum(block, 1, keepdims=True)
        squares += jnp.sum(block * block, 1, keepdims=True)
    if not finish:
        for k in range(kept):
            kept_ref[k] = held_ref[index_ref[2 * len(pieces) + k]]
        return
    lane = lax.broadcasted_iota(jnp.int32, (sums.shape[0], 128), 1)
    both = jnp.where(lane == 0, sums, squares)
    stats_ref[...] = both.T[:8]


def whole(shape):
    return pl.BlockSpec(shape, lambda i, index: (0,) * len(shape))


def out_project(near, pieces, parts, index, kept=0, total=None, own=None):
    depth = parts[0].shape[1]
    finish = total is not None
    in_specs = [whole(part.shape) for part in near]
    in_specs += [pl.BlockSpec(memory_space=pl.ANY) for _ in parts]
    operands = list(near) + list(parts)
    rows = near[0].shape[0]
    if finish:
        rows = own.shape[0]
        in_specs += [whole(total.shape), whole(own.shape)]
        operands += [total, own]
        out_shape = [
            jax.ShapeDtypeStruct((rows, 2 * depth), jnp.bfloat16),
            jax.ShapeDtypeStruct((rows // 2, 2 * depth), jnp.bfloat16),
            jax.ShapeDtypeStruct((rows // 2, 2 * depth), jnp.bfloat16),
            jax.ShapeDtypeStruct((8, rows), jnp.float32),
        ]
    else:
        out_shape = [
            jax.ShapeDtypeStruct((2, rows, depth), jnp.float32),
            jax.ShapeDtypeStruct((kept, depth, depth), jnp.bfloat16),
        ]
    return pl.pallas_call(
        functools.partial(out_kernel, pieces, len(near), len(parts), kept, finish),
        grid_spec=pltpu.PrefetchScalarGridSpec(
            num_scalar_prefetch=1,
            grid=(1,),
            in_specs=in_specs,
            out_specs=[whole(out.shape) for out in out_shape],
            scratch_shapes=[
                pltpu.VMEM((sum(part.shape[0] for part in parts), depth, depth), jnp.bfloat16),
                pltpu.SemaphoreType.DMA((len(parts),)),
            ],
        ),
        out_shape=out_shape,
        compiler_params=pltpu.CompilerParams(vmem_limit_bytes=20 * MEGA),
        cost_estimate=SMALL,
        name="out_project",
    )(index, *operands)


def project_kernel(pieces, held, count, kept, finish, width, index_ref, *refs):
    near, refs = refs[:held], refs[held:]
    stats_ref, refs = refs[0], refs[1:]
    gains, refs = refs[: len(pieces)], refs[len(pieces) :]
    parts, refs = refs[:count], refs[count:]
    if finish:
        total, (out_ref, held_ref, sems, blocks_ref) = refs[0][...], refs[1:]
    else:
        total, (out_ref, kept_ref, held_ref, sems) = None, refs
    load_shards(parts, held_ref, sems)
    rows = stats_ref.shape[1]
    row = lax.broadcasted_iota(jnp.int32, (128, rows), 0)
    stats = jnp.where(row == 0, stats_ref[0:1], stats_ref[1:2]).T
    row_mean = stats[:, 0:1] / width
    scale = lax.rsqrt(stats[:, 1:2] / width - row_mean * row_mean + epsilon)
    depth = held_ref.shape[1]
    for k, piece in enumerate(pieces):
        values = read_piece(piece, near).astype(jnp.float32)
        normed = ((values - row_mean) * scale * gains[k][...]).astype(jnp.bfloat16)
        for half in range(2):
            at = 2 * k + half if finish else index_ref[2 * k + half]
            term = jnp.dot(
                normed[:, half * depth : (half + 1) * depth],
                held_ref[at],
                preferred_element_type=jnp.float32,
            )
            total = term if total is None else total + term
    if not finish:
        out_ref[...] = total
        for k in range(kept):
            kept_ref[k] = held_ref[index_ref[2 * len(pieces) + k]]
        return
    blocks_ref[...] = total.astype(jnp.bfloat16).reshape(blocks_ref.shape)
    for block in range(out_ref.shape[0]):
        source = index_ref[len(pieces) + block]
        value = blocks_ref[jnp.maximum(source, 0)]
        out_ref[block] = jnp.where(source >= 0, value, jnp.zeros_like(value))


def project(near, pieces, stats, gain, parts, index, kept=0, total=None):
    rows = stats.shape[1]
    width = gain.shape[0]
    depth, wide = parts[0].shape[1:]
    count = len(pieces)
    finish = total is not None
    at = 0 if finish else 2 * count + kept
    in_specs = [whole(part.shape) for part in near]
    in_specs.append(whole(stats.shape))
    in_specs += [
        pl.BlockSpec((1, 2 * depth), functools.partial(lambda k, i, index: (0, index[k]), k))
        for k in range(at, at + count)
    ]
    in_specs += [pl.BlockSpec(memory_space=pl.ANY) for _ in parts]
    operands = list(near) + [stats] + [gain.reshape(1, width)] * count + list(parts)
    scratch = [
        pltpu.VMEM((sum(part.shape[0] for part in parts), depth, wide), jnp.bfloat16),
        pltpu.SemaphoreType.DMA((len(parts),)),
    ]
    if finish:
        in_specs.append(whole(total.shape))
        operands.append(total)
        out_shape = [jax.ShapeDtypeStruct((8, HALF, wide), jnp.bfloat16)]
        scratch.append(pltpu.VMEM((rows // HALF, HALF, wide), jnp.bfloat16))
    else:
        out_shape = [
            jax.ShapeDtypeStruct((rows, wide), jnp.float32),
            jax.ShapeDtypeStruct((kept, depth, wide), jnp.bfloat16),
        ]
    return pl.pallas_call(
        functools.partial(
            project_kernel, pieces, len(near), len(parts), kept, finish, width
        ),
        grid_spec=pltpu.PrefetchScalarGridSpec(
            num_scalar_prefetch=1,
            grid=(1,),
            in_specs=in_specs,
            out_specs=[whole(out.shape) for out in out_shape],
            scratch_shapes=scratch,
        ),
        out_shape=out_shape,
        compiler_params=pltpu.CompilerParams(vmem_limit_bytes=28 * MEGA),
        cost_estimate=SMALL,
        name="project",
    )(index, *operands)


def pack_kernel(place_ref, arrived_ref, text_ref, out_ref):
    start, first, second, length = (place_ref[k] for k in range(4))
    rows, wide = arrived_ref.shape[1:]
    covered = ((start >= first) & (start < first + PATCHES)) | (
        (start >= second) & (start < second + PATCHES)
    )

    @pl.when(covered)
    def _():
        for k in range(arrived_ref.shape[0]):
            out_ref[:, k * wide : (k + 1) * wide] = arrived_ref[k]

    @pl.when(jnp.logical_not(covered))
    def _():
        position = start + lax.broadcasted_iota(jnp.int32, (rows, wide), 0)
        before = jnp.clip(position - first, 0, PATCHES) + jnp.clip(position - second, 0, PATCHES)
        is_text = position - before < length
        for k in range(arrived_ref.shape[0]):
            text = text_ref[:, k * wide : (k + 1) * wide].astype(jnp.float32)
            out_ref[:, k * wide : (k + 1) * wide] = jnp.where(is_text, text, 0.0).astype(
                jnp.bfloat16
            )


def pack(arrived, text, place):
    return pl.pallas_call(
        pack_kernel,
        grid_spec=pltpu.PrefetchScalarGridSpec(
            num_scalar_prefetch=1,
            grid=(1,),
            in_specs=[whole(arrived.shape), whole(text.shape)],
            out_specs=whole(text.shape),
        ),
        out_shape=jax.ShapeDtypeStruct(text.shape, text.dtype),
        compiler_params=pltpu.CompilerParams(vmem_limit_bytes=8 * MEGA),
        cost_estimate=SMALL,
        name="pack",
    )(place, arrived, text)


def join(*values):
    return lax.optimization_barrier(values)


def local(
    patches,
    norm_gain,
    qkv_weight,
    qk_gain,
    out_weight,
    final_gain,
    proj_weight,
    text_embed,
    slot_offset,
    text_len,
):
    dp = lax.axis_index("dp")
    mp = lax.axis_index("mp")
    met = jnp.asarray(per_device(early_order))[dp]
    groups, shards = place_tables()
    groups, shards = jnp.asarray(groups)[mp], jnp.asarray(shards)[dp, mp]
    mp_slot = mp[None].astype(jnp.int32)

    own = qkv_weight.transpose(1, 0, 2)
    first = spread_y(own)
    other = swap_core(own)
    far = swap_zh(own)
    turned = transpose_mesh(out_weight)
    (other,) = join(other)
    beside = spread_y(other)
    columns = norm_columns(join(patches, other)[0], norm_gain, 16)
    total = accumulate(columns, [own, other], met[0:2])

    far, first, beside, turned, total = join(far, first, beside, turned, total)
    far_first = spread_y(far)
    second = spread_y(first)
    far_other, first_other, beside_other = join(
        swap_core(far), swap_core(first), swap_core(beside)
    )
    far_beside = spread_y(far_other)
    turned_far = swap_zh(join(turned, far_other)[0])
    proj_far = swap_zh(join(proj_weight, far_other)[0])
    total = accumulate(
        columns,
        [far, far_other, first, first_other, beside, beside_other],
        met[2:8],
        total,
    )

    turned_far, proj_far, total = join(turned_far, proj_far, total)
    out_mine = jnp.stack([turned, turned_far])
    proj_mine = jnp.stack([proj_weight, proj_far])
    own_cols = lax.dynamic_slice_in_dim(patches, mp * (2 * 384), 2 * 384, 1)
    far_first, second, far_beside, out_mine, proj_mine, own_cols, total = join(
        far_first, second, far_beside, out_mine, proj_mine, own_cols, total
    )
    far_second = spread_y(far_first)
    far_first_other, second_other, far_beside_other, out_other = join(
        swap_core(far_first), swap_core(second), swap_core(far_beside), swap_core(out_mine)
    )
    out_quad = jnp.concatenate([out_mine, out_other])
    out_first = spread_y(out_quad)
    total = accumulate(
        columns,
        [far_first, far_first_other, second, second_other, far_beside, far_beside_other],
        met[8:14],
        total,
    )

    far_second, proj_mine, total = join(far_second, proj_mine, total)
    far_second_other = swap_core(far_second)
    proj_other = swap_core(proj_mine)
    attended = accumulate(
        columns, [far_second, far_second_other], met[14:16], total, qk_gain.transpose(1, 0, 2)
    )

    whole_att, low, high, out_first, proj_other = join(*attended, out_first, proj_other)
    proj_quad = jnp.concatenate([proj_mine, proj_other])
    far = swap_zl(whole_att)
    out_second = spread_y(out_first[:2])
    out_first_other = swap_core(out_first)
    left_low, right_high, far, out_second, out_first_other, low, high = join(
        shift_x(low, 1), shift_x(high, -1), far, out_second, out_first_other, low, high
    )
    near = [whole_att, far]
    out_second_other = swap_core(out_second)
    right_low, left_high, beyond_low, beyond_high, out_second_other = join(
        shift_x(low, -1),
        shift_x(high, 1),
        shift_x(left_low, 1),
        shift_x(right_high, -1),
        out_second_other,
    )
    near += [right_low, right_high, left_low, left_high, beyond_low, beyond_high]
    proj_first = spread_y(join(proj_quad, out_second_other)[0])
    last = [shift_x(far, -1), shift_x(far, 1), swap_zl(beyond_low), swap_zl(beyond_high)]
    pieces = ((0,), (1,), (2, 3), (4, 5), (6, 7))
    last_pieces = ((0,), (1,), (2, 3))
    total, left = out_project(
        near,
        pieces,
        [out_quad, out_first, out_first_other, out_second, out_second_other],
        shards,
        kept=6,
    )
    *last, total, left = join(*last, total, left)
    block_out, low, high, stats = out_project(
        last, last_pieces, [left], shards, total=total, own=own_cols
    )

    stats_x = join(shift_x(stats, 1), shift_x(stats, -1), shift_x(stats, 2))
    stats = stats + stats_x[0] + stats_x[1] + stats_x[2]
    low, high, whole_block, stats, proj_first = join(low, high, block_out, stats, proj_first)
    far = swap_zl(whole_block)
    proj_second = spread_y(proj_first[:2])
    proj_first_other = swap_core(proj_first)
    left_low, right_high, stats_z, proj_first_other, low, high = join(
        shift_x(low, 1), shift_x(high, -1), swap_zl(stats), proj_first_other, low, high
    )
    stats = stats + stats_z
    right_low, left_high, beyond_low, beyond_high, far, proj_second = join(
        shift_x(low, -1),
        shift_x(high, 1),
        shift_x(left_low, 1),
        shift_x(right_high, -1),
        far,
        proj_second,
    )
    near = [whole_block, far]
    near += [right_low, right_high, left_low, left_high, beyond_low, beyond_high]
    proj_second_other = swap_core(proj_second)
    last = [shift_x(far, -1), shift_x(far, 1), swap_zl(beyond_low), swap_zl(beyond_high)]

    slot = slot_offset // HALF
    block = jnp.arange(8, dtype=jnp.int32)
    in_first = (block >= slot[0]) & (block < slot[0] + 2)
    in_second = (block >= slot[1]) & (block < slot[1] + 2)
    source = jnp.where(in_first, block - slot[0], jnp.where(in_second, block - slot[1] + 2, -1))

    total, left = project(
        near,
        pieces,
        stats,
        final_gain,
        [proj_quad, proj_first, proj_first_other, proj_second, proj_second_other],
        jnp.concatenate([shards, groups[:5]]),
        kept=6,
    )
    *last, total, left = join(*last, total, left)
    (outgoing,) = project(
        last,
        last_pieces,
        stats,
        final_gain,
        [left],
        jnp.concatenate([groups[5:], source]),
        total=total,
    )
    arrived = lax.all_to_all(outgoing, "mp", split_axis=0, concat_axis=0, tiled=True)
    place = jnp.concatenate([mp_slot * HALF, slot_offset, text_len])
    sequence = pack(arrived, text_embed[0], place)
    return (block_out, sequence[None])


def solution(mesh):
    in_specs = (
        P("dp", None),
        P(),
        P("dp", "mp", None),
        P(None, "mp", None),
        P("dp", "mp"),
        P(),
        P("dp", "mp"),
        P("dp", "mp", None),
        P("dp"),
        P("dp"),
    )
    out_specs = (P("dp", "mp"), P("dp", "mp", None))
    return jax.shard_map(local, mesh=mesh, in_specs=in_specs, out_specs=out_specs, check_vma=False)
```

```python
import functools
import math

import jax
import jax.numpy as jnp
import numpy as np
from jax import lax
from jax.experimental import pallas as pl
from jax.experimental.pallas import tpu as pltpu
from jax.sharding import PartitionSpec as P

PATCHES = 256
HALF = 128
AXES = ("dp", "mp")
MEGA = 1024 * 1024
epsilon = 1e-06
EXTRA = 16
SMALL = pl.CostEstimate(flops=1, bytes_accessed=1, transcendentals=0)


def coordinates():
    return [
        (zh, y, c, zl, x)
        for zh in range(2)
        for y in range(4)
        for c in range(2)
        for zl in range(2)
        for x in range(4)
    ]


def device_index(zh, y, c, zl, x):
    return ((zh * 4 + y) * 2 + c) * 8 + zl * 4 + x


def move(values, target):
    pairs = [(device_index(*at), device_index(*target(*at))) for at in coordinates()]
    return lax.ppermute(values, AXES, pairs)


def swap_core(values):
    return move(values, lambda zh, y, c, zl, x: (zh, y, 1 - c, zl, x))


def swap_zh(values):
    return move(values, lambda zh, y, c, zl, x: (1 - zh, y, c, zl, x))


def swap_zl(values):
    return move(values, lambda zh, y, c, zl, x: (zh, y, c, 1 - zl, x))


def spread_y(values):
    return move(values, lambda zh, y, c, zl, x: (zh, (y + 1 - 2 * c) % 4, c, zl, x))


def shift_x(values, step):
    return move(values, lambda zh, y, c, zl, x: (zh, y, c, zl, (x + step) % 4))


def transpose_mesh(values):
    return move(values, lambda zh, y, c, zl, x: (zl, x, c, zh, y))


def per_device(order):
    table = np.zeros((16, 16), np.int32)
    for zh in range(2):
        for y in range(4):
            for c in range(2):
                met = order(zh, y, c, 2 * c - 1)
                table[zh * 8 + y * 2 + c] = [r % 2 * 8 + yy % 4 * 2 + cc % 2 for r, yy, cc in met]
    return table


def early_order(zh, y, c, step):
    return [
        (zh, y, c),
        (zh, y, c + 1),
        (zh + 1, y, c),
        (zh + 1, y, c + 1),
        (zh, y + step, c),
        (zh, y - step, c + 1),
        (zh, y + step, c + 1),
        (zh, y - step, c),
        (zh + 1, y + step, c),
        (zh + 1, y - step, c + 1),
        (zh, y + 2, c),
        (zh, y + 2, c + 1),
        (zh + 1, y + step, c + 1),
        (zh + 1, y - step, c),
        (zh + 1, y + 2, c),
        (zh + 1, y + 2, c + 1),
    ]


def late_order(zh, y, c, step):
    order = []
    for yy, cores in (
        (y, (c, c + 1)),
        (y + step, (c, c + 1)),
        (y - step, (c + 1, c)),
        (y + 2, (c, c + 1)),
    ):
        for core in cores:
            order += [(zh, yy, core), (zh + 1, yy, core)]
    return order


NEAR = [(0, 0), (1, 0), (0, 1), (0, 3), (0, 2), (1, 1), (1, 3), (1, 2)]


def place_tables():
    met = per_device(late_order)
    groups = np.zeros((8, 8), np.int32)
    shards = np.zeros((16, 8, 16), np.int32)
    for mp in range(8):
        for r, (dz, dx) in enumerate(NEAR):
            group = (mp // 4 ^ dz) * 4 + (mp + dx) % 4
            groups[mp, r] = group
            for dp in range(16):
                for half in range(2):
                    shards[dp, mp, 2 * r + half] = np.argmax(met[dp] == 2 * group + half)
    return groups, shards


def norm_kernel(values_ref, gain_ref, out_ref):
    values = values_ref[...].astype(jnp.float32)
    width = values.shape[1]
    row_mean = jnp.sum(values, -1, keepdims=True) / width
    squares = jnp.sum(values * values, -1, keepdims=True) / width
    scale = lax.rsqrt(squares - row_mean * row_mean + epsilon)
    normed = ((values - row_mean) * scale * gain_ref[...]).astype(jnp.bfloat16)
    depth = out_ref.shape[2]
    for k in range(out_ref.shape[0]):
        out_ref[k] = normed[:, k * depth : (k + 1) * depth]


def norm_columns(values, gain, chunks):
    rows, width = values.shape
    block = 64
    return pl.pallas_call(
        norm_kernel,
        grid=(rows // block,),
        in_specs=[
            pl.BlockSpec((block, width), lambda i: (i, 0)),
            pl.BlockSpec((1, width), lambda i: (0, 0)),
        ],
        out_specs=pl.BlockSpec((chunks, block, width // chunks), lambda i: (0, i, 0)),
        out_shape=jax.ShapeDtypeStruct((chunks, rows, width // chunks), jnp.bfloat16),
        compiler_params=pltpu.CompilerParams(vmem_limit_bytes=16 * MEGA),
        cost_estimate=SMALL,
        name="norm_columns",
    )(*in_hbm([values]), gain.reshape(1, width))


def row_norm(values, gain):
    row_mean = jnp.mean(values, -1, keepdims=True)
    squares = jnp.mean(values * values, -1, keepdims=True)
    return (values - row_mean) * lax.rsqrt(squares - row_mean * row_mean + epsilon) * gain


def accumulate_kernel(shard_counts, has_total, attend, index_ref, *refs):
    del index_ref
    count = sum(shard_counts)
    columns, refs = refs[:count], refs[count:]
    shards, refs = refs[: len(shard_counts)], refs[len(shard_counts) :]
    total = None
    if has_total:
        total, refs = refs[0][0], refs[1:]
    at = 0
    for held, number in zip(shards, shard_counts):
        for k in range(number):
            term = jnp.dot(columns[at][0], held[k, 0], preferred_element_type=jnp.float32)
            total = term if total is None else total + term
            at += 1
    if not attend:
        refs[0][0] = total
        return
    gain_ref, out_ref, *image_refs = refs
    size = gain_ref.shape[2]
    gains = gain_ref[0]
    query = row_norm(total[:, :size], gains[0:1]).astype(jnp.bfloat16)
    key = row_norm(total[:, size : 2 * size], gains[1:2]).astype(jnp.bfloat16)
    value = total[:, 2 * size :].astype(jnp.bfloat16)
    for image in range(total.shape[0] // PATCHES):
        rows = slice(image * PATCHES, (image + 1) * PATCHES)
        scores = lax.dot_general(
            query[rows], key[rows], (((1,), (1,)), ((), ())), preferred_element_type=jnp.float32
        ) / math.sqrt(size)
        raised = jnp.exp(scores - jnp.max(scores, -1, keepdims=True))
        weights = (raised / jnp.sum(raised, -1, keepdims=True)).astype(jnp.bfloat16)
        attended = jnp.dot(weights, value[rows], preferred_element_type=jnp.float32)
        attended = attended.astype(jnp.bfloat16)
        out_ref[rows, :] = attended
        image_refs[image][...] = attended


def accumulate(columns, shards, index, total=None, gains=None):
    shards = [held if held.ndim == 4 else held[None] for held in shards]
    counts = tuple(held.shape[0] for held in shards)
    _, rows, depth = columns.shape
    heads, wide = shards[0].shape[1], shards[0].shape[3]
    in_specs = [
        pl.BlockSpec((1, rows, depth), functools.partial(lambda k, h, index: (index[k], 0, 0), k))
        for k in range(sum(counts))
    ]
    in_specs += [
        pl.BlockSpec((number, 1, depth, wide), lambda h, index: (0, h, 0, 0)) for number in counts
    ]
    operands = [columns] * sum(counts) + (in_hbm(shards) if gains is None else shards)
    total_spec = pl.BlockSpec((1, rows, wide), lambda h, index: (h, 0, 0))
    if total is not None:
        in_specs.append(total_spec)
        operands.append(total)
    aliases = {}
    if gains is None:
        out_spec = total_spec
        out_shape = jax.ShapeDtypeStruct((heads, rows, wide), jnp.float32)
        if total is not None:
            aliases = {len(operands): 0}
    else:
        in_specs.append(pl.BlockSpec((1, 2, wide // 3), lambda h, index: (h, 0, 0)))
        operands.append(gains)
        sizes = [rows] + [PATCHES] * (rows // PATCHES)
        out_spec = [pl.BlockSpec((size, wide // 3), lambda h, index: (0, h)) for size in sizes]
        out_shape = [
            jax.ShapeDtypeStruct((size, heads * wide // 3), jnp.bfloat16) for size in sizes
        ]
    return pl.pallas_call(
        functools.partial(accumulate_kernel, counts, total is not None, gains is not None),
        grid_spec=pltpu.PrefetchScalarGridSpec(
            num_scalar_prefetch=1, grid=(heads,), in_specs=in_specs, out_specs=out_spec
        ),
        out_shape=out_shape,
        input_output_aliases=aliases,
        compiler_params=pltpu.CompilerParams(vmem_limit_bytes=20 * MEGA),
        cost_estimate=SMALL,
        name="accumulate",
    )(index, *operands)


def start_shards(parts, held_ref, sems):
    at = 0
    copies = []
    for k, part in enumerate(parts):
        number = part.shape[0]
        copies.append(pltpu.make_async_copy(part, held_ref.at[pl.ds(at, number)], sems.at[k]))
        copies[-1].start()
        at += number
    return copies


def start_pieces(pieces, near, near_ref, sems):
    copies = []
    count = 0
    for at, piece in enumerate(pieces):
        copies.append([])
        rows = near_ref.shape[1] // len(piece)
        for part, (k, first) in enumerate(piece):
            source = near[k].at[pl.ds(first, rows)]
            place = near_ref.at[at, pl.ds(part * rows, rows)]
            copies[-1].append(pltpu.make_async_copy(source, place, sems.at[count]))
            copies[-1][-1].start()
            count += 1
    return copies


def wait_all(copies):
    for copy in copies:
        copy.wait()


def out_kernel(pieces, held, count, kept, finish, index_ref, *refs):
    near, refs = refs[:held], refs[held:]
    parts, refs = refs[:count], refs[count:]
    if finish:
        given_ref, own_ref, block_ref, *half_refs, stats_ref = refs[:-4]
    else:
        total_ref, kept_ref = refs[:-4]
    near_ref, held_ref, near_sems, sems = refs[-4:]
    shard_copies = start_shards(parts, held_ref, sems)
    piece_copies = start_pieces(pieces, near, near_ref, near_sems)
    wait_all(shard_copies)
    depth = held_ref.shape[1]
    total = [given_ref[0], given_ref[1]] if finish else [None, None]
    for k in range(len(pieces)):
        wait_all(piece_copies[k])
        for half in range(2):
            term = lax.dot_general(
                near_ref[k],
                held_ref[2 * k + half if finish else index_ref[2 * k + half]],
                (((1,), (1,)), ((), ())),
                preferred_element_type=jnp.float32,
            )
            term = term.astype(jnp.bfloat16).astype(jnp.float32)
            total[half] = term if total[half] is None else total[half] + term
    if not finish:
        total_ref[0] = total[0]
        total_ref[1] = total[1]
        for k in range(kept):
            kept_ref[k] = held_ref[index_ref[2 * len(pieces) + k]]
        return
    sums, squares = 0.0, 0.0
    for half in range(2):
        cols = slice(half * depth, (half + 1) * depth)
        block = (own_ref[:, cols].astype(jnp.float32) + total[half]).astype(jnp.bfloat16)
        block_ref[:, cols] = block
        rows = block.shape[0] // 2
        half_refs[0][:rows, cols] = block[:rows]
        half_refs[1][:rows, cols] = block[rows:]
        block = block.astype(jnp.float32)
        sums += jnp.sum(block, 1, keepdims=True)
        squares += jnp.sum(block * block, 1, keepdims=True)
    lane = lax.broadcasted_iota(jnp.int32, (sums.shape[0], 128), 1)
    both = jnp.where(lane == 0, sums, squares).T[:8]
    stats_ref[...] = both
    row = lax.broadcasted_iota(jnp.int32, (EXTRA, both.shape[1]), 0)
    carried = jnp.zeros(row.shape, jnp.float32)
    for k in range(2):
        rest = both[k : k + 1]
        for part in range(3):
            rounded = rest.astype(jnp.bfloat16).astype(jnp.float32)
            carried = jnp.where(row == 3 * k + part, rounded, carried)
            rest = rest - rounded
    carried = carried.astype(jnp.bfloat16)
    for half_ref in half_refs:
        half_ref[rows:, : carried.shape[1]] = carried
        half_ref[rows:, carried.shape[1] :] = jnp.zeros(
            (EXTRA, half_ref.shape[1] - carried.shape[1]), jnp.bfloat16
        )


def held_scratch(pieces, near, parts, wide):
    rows = near[0].shape[0]
    depth = parts[0].shape[1]
    return [
        pltpu.VMEM((len(pieces), rows, near[0].shape[1]), jnp.bfloat16),
        pltpu.VMEM((sum(part.shape[0] for part in parts), depth, wide), jnp.bfloat16),
        pltpu.SemaphoreType.DMA((sum(len(piece) for piece in pieces),)),
        pltpu.SemaphoreType.DMA((len(parts),)),
    ]


def in_hbm(arrays):
    return [pltpu.with_memory_space_constraint(array, pltpu.HBM) for array in arrays]


def whole(shape):
    return pl.BlockSpec(shape, lambda i, index: (0,) * len(shape))


def out_project(near, pieces, parts, index, kept=0, total=None, patches=None):
    depth = parts[0].shape[1]
    finish = total is not None
    in_specs = [pl.BlockSpec(memory_space=pltpu.HBM) for _ in near]
    in_specs += [pl.BlockSpec(memory_space=pl.ANY if finish else pltpu.HBM) for _ in parts]
    operands = in_hbm(near) + (parts if finish else in_hbm(parts))
    rows = near[0].shape[0]
    if finish:
        rows = patches.shape[0]
        in_specs.append(whole(total.shape))
        in_specs.append(pl.BlockSpec((rows, 2 * depth), lambda i, index: (0, index[0])))
        operands += [total, *in_hbm([patches])]
        out_shape = [
            jax.ShapeDtypeStruct((rows, 2 * depth), jnp.bfloat16),
            jax.ShapeDtypeStruct((rows // 2 + EXTRA, 2 * depth), jnp.bfloat16),
            jax.ShapeDtypeStruct((rows // 2 + EXTRA, 2 * depth), jnp.bfloat16),
            jax.ShapeDtypeStruct((8, rows), jnp.float32),
        ]
    else:
        out_shape = [
            jax.ShapeDtypeStruct((2, rows, depth), jnp.float32),
            jax.ShapeDtypeStruct((kept, depth, depth), jnp.bfloat16),
        ]
    return pl.pallas_call(
        functools.partial(out_kernel, pieces, len(near), len(parts), kept, finish),
        grid_spec=pltpu.PrefetchScalarGridSpec(
            num_scalar_prefetch=1,
            grid=(1,),
            in_specs=in_specs,
            out_specs=[whole(out.shape) for out in out_shape],
            scratch_shapes=held_scratch(pieces, near, parts, depth),
        ),
        out_shape=out_shape,
        compiler_params=pltpu.CompilerParams(vmem_limit_bytes=20 * MEGA),
        cost_estimate=SMALL,
        name="out_project",
    )(index, *operands)


def sums_kernel(own_ref, *refs):
    *carried, out_ref = refs
    total = own_ref[...]
    row = lax.broadcasted_iota(jnp.int32, total.shape, 0)
    for ref in carried:
        parts = ref[...].astype(jnp.float32)
        sums, squares = (
            parts[k : k + 1] + parts[k + 1 : k + 2] + parts[k + 2 : k + 3] for k in (0, 3)
        )
        total = total + jnp.where(row == 0, sums, squares)
    out_ref[...] = total


def add_sums(own, carried):
    rows = own.shape[1]
    in_specs = [pl.BlockSpec(own.shape, lambda i: (0, 0))]
    for _, first in carried:
        place = (first + PATCHES) // EXTRA
        in_specs.append(
            pl.BlockSpec((EXTRA, rows), functools.partial(lambda place, i: (place, 0), place))
        )
    return pl.pallas_call(
        sums_kernel,
        grid=(1,),
        in_specs=in_specs,
        out_specs=pl.BlockSpec(own.shape, lambda i: (0, 0)),
        out_shape=jax.ShapeDtypeStruct(own.shape, own.dtype),
        compiler_params=pltpu.CompilerParams(vmem_limit_bytes=4 * MEGA),
        cost_estimate=SMALL,
        name="add_sums",
    )(own, *in_hbm([array for array, _ in carried]))


def project_kernel(pieces, held, count, kept, finish, width, index_ref, *refs):
    near, refs = refs[:held], refs[held:]
    stats_ref, refs = refs[0], refs[1:]
    gains, refs = refs[: len(pieces)], refs[len(pieces) :]
    parts, refs = refs[:count], refs[count:]
    if finish:
        total, (out_ref, *refs, blocks_ref) = refs[0][...], refs[1:]
    else:
        total, (out_ref, kept_ref, *refs) = None, refs
    near_ref, held_ref, near_sems, sems = refs
    depth = held_ref.shape[1]
    shard_copies = start_shards(parts, held_ref, sems)
    piece_copies = start_pieces(pieces, near, near_ref, near_sems)
    rows = stats_ref.shape[1]
    row = lax.broadcasted_iota(jnp.int32, (128, rows), 0)
    stats = jnp.where(row == 0, stats_ref[0:1], stats_ref[1:2]).T
    row_mean = stats[:, 0:1] / width
    scale = lax.rsqrt(stats[:, 1:2] / width - row_mean * row_mean + epsilon)
    wait_all(shard_copies)
    for k in range(len(pieces)):
        wait_all(piece_copies[k])
        values = near_ref[k].astype(jnp.float32)
        normed = ((values - row_mean) * scale * gains[k][...]).astype(jnp.bfloat16)
        for half in range(2):
            at = 2 * k + half if finish else index_ref[2 * k + half]
            term = jnp.dot(
                normed[:, half * depth : (half + 1) * depth],
                held_ref[at],
                preferred_element_type=jnp.float32,
            )
            total = term if total is None else total + term
    if not finish:
        out_ref[...] = total
        for k in range(kept):
            kept_ref[k] = held_ref[index_ref[2 * len(pieces) + k]]
        return
    blocks_ref[...] = total.astype(jnp.bfloat16).reshape(blocks_ref.shape)
    for block in range(out_ref.shape[0]):
        source = index_ref[len(pieces) + block]
        value = blocks_ref[jnp.maximum(source, 0)]
        out_ref[block] = jnp.where(source >= 0, value, jnp.zeros_like(value))


def project(near, pieces, stats, gain, parts, index, kept=0, total=None):
    rows = stats.shape[1]
    width = gain.shape[0]
    depth, wide = parts[0].shape[1:]
    count = len(pieces)
    finish = total is not None
    at = 0 if finish else 2 * count + kept
    in_specs = [pl.BlockSpec(memory_space=pltpu.HBM) for _ in near]
    in_specs.append(whole(stats.shape))
    in_specs += [
        pl.BlockSpec((1, 2 * depth), functools.partial(lambda k, i, index: (0, index[k]), k))
        for k in range(at, at + count)
    ]
    in_specs += [pl.BlockSpec(memory_space=pl.ANY if finish else pltpu.HBM) for _ in parts]
    operands = in_hbm(near) + [stats] + [gain.reshape(1, width)] * count
    operands += parts if finish else in_hbm(parts)
    scratch = held_scratch(pieces, near, parts, wide)
    if finish:
        in_specs.append(whole(total.shape))
        operands.append(total)
        out_shape = [jax.ShapeDtypeStruct((8, HALF, wide), jnp.bfloat16)]
        scratch.append(pltpu.VMEM((rows // HALF, HALF, wide), jnp.bfloat16))
    else:
        out_shape = [
            jax.ShapeDtypeStruct((rows, wide), jnp.float32),
            jax.ShapeDtypeStruct((kept, depth, wide), jnp.bfloat16),
        ]
    return pl.pallas_call(
        functools.partial(
            project_kernel, pieces, len(near), len(parts), kept, finish, width
        ),
        grid_spec=pltpu.PrefetchScalarGridSpec(
            num_scalar_prefetch=1,
            grid=(1,),
            in_specs=in_specs,
            out_specs=[whole(out.shape) for out in out_shape],
            scratch_shapes=scratch,
        ),
        out_shape=out_shape,
        compiler_params=pltpu.CompilerParams(vmem_limit_bytes=28 * MEGA),
        cost_estimate=SMALL,
        name="project",
    )(index, *operands)


def pack_kernel(place_ref, arrived_ref, text_ref, out_ref):
    start, first, second, length = (place_ref[k] for k in range(4))
    rows, wide = arrived_ref.shape[1:]
    covered = ((start >= first) & (start < first + PATCHES)) | (
        (start >= second) & (start < second + PATCHES)
    )

    @pl.when(covered)
    def _():
        for k in range(arrived_ref.shape[0]):
            out_ref[:, k * wide : (k + 1) * wide] = arrived_ref[k]

    @pl.when(jnp.logical_not(covered))
    def _():
        position = start + lax.broadcasted_iota(jnp.int32, (rows, wide), 0)
        before = jnp.clip(position - first, 0, PATCHES) + jnp.clip(position - second, 0, PATCHES)
        is_text = position - before < length
        for k in range(arrived_ref.shape[0]):
            text = text_ref[:, k * wide : (k + 1) * wide].astype(jnp.float32)
            out_ref[:, k * wide : (k + 1) * wide] = jnp.where(is_text, text, 0.0).astype(
                jnp.bfloat16
            )


def pack(arrived, text, place):
    return pl.pallas_call(
        pack_kernel,
        grid_spec=pltpu.PrefetchScalarGridSpec(
            num_scalar_prefetch=1,
            grid=(1,),
            in_specs=[whole(arrived.shape), whole(text.shape)],
            out_specs=whole(text.shape),
        ),
        out_shape=jax.ShapeDtypeStruct(text.shape, text.dtype),
        compiler_params=pltpu.CompilerParams(vmem_limit_bytes=8 * MEGA),
        cost_estimate=SMALL,
        name="pack",
    )(place, arrived, text)


def join(*values):
    return lax.optimization_barrier(values)


def piece_places(step):
    first = (
        ((0, 0),),
        ((1, 0),),
        ((5, step), (3, 0)),
        ((2, 0), (4, step)),
        ((4, 0), (5, 0)),
    )
    return first, (((0, 0),), ((1, 0),), ((2, 0), (2, PATCHES)))


def local(
    patches,
    norm_gain,
    qkv_weight,
    qk_gain,
    out_weight,
    final_gain,
    proj_weight,
    text_embed,
    slot_offset,
    text_len,
):
    dp = lax.axis_index("dp")
    mp = lax.axis_index("mp")
    met = jnp.asarray(per_device(early_order))[dp]
    groups, shards = place_tables()
    groups, shards = jnp.asarray(groups)[mp], jnp.asarray(shards)[dp, mp]
    mp_slot = mp[None].astype(jnp.int32)

    own = qkv_weight.transpose(1, 0, 2)
    first = spread_y(own)
    other = swap_core(own)
    turned = transpose_mesh(out_weight)
    (other,) = join(other)
    far = swap_zh(join(own, other)[0])
    beside = spread_y(other)
    columns = norm_columns(join(patches, other)[0], norm_gain, 16)
    total = accumulate(columns, [own, other], met[0:2])

    far, first, beside, turned, total = join(far, first, beside, turned, total)
    far_first = spread_y(far)
    second = spread_y(first)
    far_other, first_other, beside_other = join(
        swap_core(far), swap_core(first), swap_core(beside)
    )
    far_beside = spread_y(far_other)
    turned_far = swap_zh(join(turned, far_other)[0])
    proj_far = swap_zh(join(proj_weight, far_other)[0])
    total = accumulate(
        columns,
        [far, far_other, first, first_other, beside, beside_other],
        met[2:8],
        total,
    )
    turned_far, proj_far, total = join(turned_far, proj_far, total)
    out_mine = jnp.stack([turned, turned_far])
    proj_mine = jnp.stack([proj_weight, proj_far])

    far_first, second, far_beside, out_mine, proj_mine, total = join(
        far_first, second, far_beside, out_mine, proj_mine, total
    )
    far_second = spread_y(far_first)
    far_first_other, second_other, far_beside_other, out_other = join(
        swap_core(far_first), swap_core(second), swap_core(far_beside), swap_core(out_mine)
    )
    out_quad = jnp.concatenate([out_mine, out_other])
    total = accumulate(
        columns,
        [far_first, far_first_other, second, second_other, far_beside, far_beside_other],
        met[8:14],
        total,
    )

    far_second, out_quad, proj_mine, total = join(far_second, out_quad, proj_mine, total)
    far_second_other = swap_core(far_second)
    out_first = spread_y(out_quad)
    proj_other = swap_core(proj_mine)
    attended = accumulate(
        columns, [far_second, far_second_other], met[14:16], total, qk_gain.transpose(1, 0, 2)
    )

    whole_att, low, high, proj_other = join(*attended, proj_other)
    proj_quad = jnp.concatenate([proj_mine, proj_other])
    far = swap_zl(whole_att)
    left_low, right_high, far, out_first, low, high = join(
        shift_x(low, 1), shift_x(high, -1), far, out_first, low, high
    )
    out_second = spread_y(out_first[:2])
    out_first_other = swap_core(out_first)
    from_left, from_right, out_second, out_first_other, proj_quad = join(
        shift_x(jnp.concatenate([left_low, high]), 1),
        shift_x(jnp.concatenate([right_high, low]), -1),
        out_second,
        out_first_other,
        proj_quad,
    )
    near = [whole_att, far, left_low, right_high, from_left, from_right]
    pieces, last_pieces = piece_places(PATCHES)
    out_second_other = swap_core(out_second)
    proj_first = spread_y(proj_quad)
    beyond = jnp.concatenate([from_left[:PATCHES], from_right[:PATCHES]])
    last = [shift_x(far, -1), shift_x(far, 1), swap_zl(beyond)]
    parts = [out_quad, out_first, out_first_other, out_second, out_second_other]
    total, left = out_project(near, pieces, parts, shards, kept=6)
    block_out, low, high, stats = out_project(
        last, last_pieces, [left], mp_slot, total=total, patches=patches
    )

    proj_first, whole_block, low, high, stats = join(proj_first, block_out, low, high, stats)
    far = swap_zl(whole_block)
    proj_second = spread_y(proj_first[:2])
    proj_first_other = swap_core(proj_first)
    left_low, right_high, proj_first_other, proj_second, low, high = join(
        shift_x(low, 1), shift_x(high, -1), proj_first_other, proj_second, low, high
    )
    from_left, from_right, far = join(
        shift_x(jnp.concatenate([left_low, high]), 1),
        shift_x(jnp.concatenate([right_high, low]), -1),
        far,
    )
    stats = add_sums(stats, [(left_low, 0), (right_high, 0), (from_left, 0)])
    stats_z = swap_zl(stats)
    stats = stats + stats_z
    near = [whole_block, far, left_low, right_high, from_left, from_right]
    pieces, last_pieces = piece_places(PATCHES + EXTRA)
    beyond = jnp.concatenate([from_left[:PATCHES], from_right[:PATCHES]])
    beyond = join(beyond, stats_z)[0]
    last = [shift_x(far, -1), shift_x(far, 1), swap_zl(beyond)]
    parts = [proj_quad, proj_first, proj_first_other, proj_second, swap_core(proj_second)]

    slot = slot_offset // HALF
    block = jnp.arange(8, dtype=jnp.int32)
    in_first = (block >= slot[0]) & (block < slot[0] + 2)
    in_second = (block >= slot[1]) & (block < slot[1] + 2)
    source = jnp.where(in_first, block - slot[0], jnp.where(in_second, block - slot[1] + 2, -1))

    total, left = project(
        near,
        pieces,
        stats,
        final_gain,
        parts,
        jnp.concatenate([shards, groups[:5]]),
        kept=6,
    )
    (outgoing,) = project(
        last,
        last_pieces,
        stats,
        final_gain,
        [left],
        jnp.concatenate([groups[5:], source]),
        total=total,
    )
    arrived = lax.all_to_all(outgoing, "mp", split_axis=0, concat_axis=0, tiled=True)
    place = jnp.concatenate([mp_slot * HALF, slot_offset, text_len])
    sequence = pack(arrived, text_embed[0], place)
    return (block_out, sequence[None])


def solution(mesh):
    in_specs = (
        P("dp", None),
        P(),
        P("dp", "mp", None),
        P(None, "mp", None),
        P("dp", "mp"),
        P(),
        P("dp", "mp"),
        P("dp", "mp", None),
        P("dp"),
        P("dp"),
    )
    out_specs = (P("dp", "mp"), P("dp", "mp", None))
    return jax.shard_map(local, mesh=mesh, in_specs=in_specs, out_specs=out_specs, check_vma=False)
```

```python
import functools
import math

import jax
import jax.numpy as jnp
import numpy as np
from jax import lax
from jax.experimental import pallas as pl
from jax.experimental.pallas import tpu as pltpu
from jax.sharding import PartitionSpec as P

PATCHES = 256
HALF = 128
AXES = ("dp", "mp")
MEGA = 1024 * 1024
epsilon = 1e-06
EXTRA = 16
SMALL = pl.CostEstimate(flops=1, bytes_accessed=1, transcendentals=0)


def coordinates():
    return [
        (zh, y, c, zl, x)
        for zh in range(2)
        for y in range(4)
        for c in range(2)
        for zl in range(2)
        for x in range(4)
    ]


def device_index(zh, y, c, zl, x):
    return ((zh * 4 + y) * 2 + c) * 8 + zl * 4 + x


def move(values, target):
    pairs = [(device_index(*at), device_index(*target(*at))) for at in coordinates()]
    return lax.ppermute(values, AXES, pairs)


def swap_core(values):
    return move(values, lambda zh, y, c, zl, x: (zh, y, 1 - c, zl, x))


def swap_zh(values):
    return move(values, lambda zh, y, c, zl, x: (1 - zh, y, c, zl, x))


def swap_zl(values):
    return move(values, lambda zh, y, c, zl, x: (zh, y, c, 1 - zl, x))


def spread_y(values):
    return move(values, lambda zh, y, c, zl, x: (zh, (y + 1 - 2 * c) % 4, c, zl, x))


def shift_x(values, step):
    return move(values, lambda zh, y, c, zl, x: (zh, y, c, zl, (x + step) % 4))


def turn_first(values):
    return move(values, lambda zh, y, c, zl, x: (zl, (x + y) % 4, c, zh, x))


def turn_second(values):
    return move(values, lambda zh, y, c, zl, x: (zh, y, c, zl, (y - x) % 4))


def per_device(order):
    table = np.zeros((16, 16), np.int32)
    for zh in range(2):
        for y in range(4):
            for c in range(2):
                met = order(zh, y, c, 2 * c - 1)
                table[zh * 8 + y * 2 + c] = [r % 2 * 8 + yy % 4 * 2 + cc % 2 for r, yy, cc in met]
    return table


def early_order(zh, y, c, step):
    return [
        (zh, y, c),
        (zh, y, c + 1),
        (zh + 1, y, c),
        (zh + 1, y, c + 1),
        (zh, y + step, c),
        (zh, y - step, c + 1),
        (zh, y + step, c + 1),
        (zh, y - step, c),
        (zh + 1, y + step, c),
        (zh + 1, y - step, c + 1),
        (zh, y + 2, c),
        (zh, y + 2, c + 1),
        (zh + 1, y + step, c + 1),
        (zh + 1, y - step, c),
        (zh + 1, y + 2, c),
        (zh + 1, y + 2, c + 1),
    ]


def late_order(zh, y, c, step):
    order = []
    for yy, cores in (
        (y, (c, c + 1)),
        (y + step, (c, c + 1)),
        (y - step, (c + 1, c)),
        (y + 2, (c, c + 1)),
    ):
        for core in cores:
            order += [(zh, yy, core), (zh + 1, yy, core)]
    return order


NEAR = [(0, 0), (1, 0), (0, 1), (0, 3), (0, 2), (1, 1), (1, 3), (1, 2)]


def place_tables():
    met = per_device(late_order)
    groups = np.zeros((8, 8), np.int32)
    shards = np.zeros((2, 16, 8, 16), np.int32)
    for mp in range(8):
        for r, (dz, dx) in enumerate(NEAR):
            group = (mp // 4 ^ dz) * 4 + (mp + dx) % 4
            groups[mp, r] = group
            turned = group // 4 * 4 + (group + mp) % 4
            for dp in range(16):
                for half in range(2):
                    shards[0, dp, mp, 2 * r + half] = np.argmax(met[dp] == 2 * group + half)
                    shards[1, dp, mp, 2 * r + half] = np.argmax(met[dp] == 2 * turned + half)
    return groups, shards


def norm_kernel(values_ref, gain_ref, out_ref):
    values = values_ref[...].astype(jnp.float32)
    width = values.shape[1]
    row_mean = jnp.sum(values, -1, keepdims=True) / width
    squares = jnp.sum(values * values, -1, keepdims=True) / width
    scale = lax.rsqrt(squares - row_mean * row_mean + epsilon)
    normed = ((values - row_mean) * scale * gain_ref[...]).astype(jnp.bfloat16)
    depth = out_ref.shape[2]
    for k in range(out_ref.shape[0]):
        out_ref[k] = normed[:, k * depth : (k + 1) * depth]


def norm_columns(values, gain, chunks):
    rows, width = values.shape
    block = 64
    return pl.pallas_call(
        norm_kernel,
        grid=(rows // block,),
        in_specs=[
            pl.BlockSpec((block, width), lambda i: (i, 0)),
            pl.BlockSpec((1, width), lambda i: (0, 0)),
        ],
        out_specs=pl.BlockSpec((chunks, block, width // chunks), lambda i: (0, i, 0)),
        out_shape=jax.ShapeDtypeStruct((chunks, rows, width // chunks), jnp.bfloat16),
        compiler_params=pltpu.CompilerParams(vmem_limit_bytes=16 * MEGA),
        cost_estimate=SMALL,
        name="norm_columns",
    )(*in_hbm([values]), gain.reshape(1, width))


def row_norm(values, gain):
    row_mean = jnp.mean(values, -1, keepdims=True)
    squares = jnp.mean(values * values, -1, keepdims=True)
    return (values - row_mean) * lax.rsqrt(squares - row_mean * row_mean + epsilon) * gain


def accumulate_kernel(shard_counts, has_total, attend, index_ref, *refs):
    del index_ref
    count = sum(shard_counts)
    columns, refs = refs[:count], refs[count:]
    shards, refs = refs[: len(shard_counts)], refs[len(shard_counts) :]
    total = None
    if has_total:
        total, refs = refs[0][0], refs[1:]
    held = [ref[k, 0] for ref, number in zip(shards, shard_counts) for k in range(number)]
    term = jnp.dot(
        jnp.concatenate([ref[0] for ref in columns], 1),
        jnp.concatenate(held, 0),
        preferred_element_type=jnp.float32,
    )
    total = term if total is None else total + term
    if not attend:
        refs[0][0] = total
        return
    gain_ref, out_ref, *image_refs = refs
    size = gain_ref.shape[2]
    gains = gain_ref[0]
    query = row_norm(total[:, :size], gains[0:1]).astype(jnp.bfloat16)
    key = row_norm(total[:, size : 2 * size], gains[1:2]).astype(jnp.bfloat16)
    value = total[:, 2 * size :].astype(jnp.bfloat16)
    for image in range(total.shape[0] // PATCHES):
        rows = slice(image * PATCHES, (image + 1) * PATCHES)
        scores = lax.dot_general(
            query[rows], key[rows], (((1,), (1,)), ((), ())), preferred_element_type=jnp.float32
        ) / math.sqrt(size)
        raised = jnp.exp(scores - jnp.max(scores, -1, keepdims=True))
        weights = (raised / jnp.sum(raised, -1, keepdims=True)).astype(jnp.bfloat16)
        attended = jnp.dot(weights, value[rows], preferred_element_type=jnp.float32)
        attended = attended.astype(jnp.bfloat16)
        out_ref[rows, :] = attended
        image_refs[image][...] = attended


def accumulate(columns, shards, index, total=None, gains=None):
    shards = [held if held.ndim == 4 else held[None] for held in shards]
    counts = tuple(held.shape[0] for held in shards)
    _, rows, depth = columns.shape
    heads, wide = shards[0].shape[1], shards[0].shape[3]
    in_specs = [
        pl.BlockSpec((1, rows, depth), functools.partial(lambda k, h, index: (index[k], 0, 0), k))
        for k in range(sum(counts))
    ]
    in_specs += [
        pl.BlockSpec((number, 1, depth, wide), lambda h, index: (0, h, 0, 0)) for number in counts
    ]
    operands = [columns] * sum(counts) + (in_hbm(shards) if gains is None else shards)
    total_spec = pl.BlockSpec((1, rows, wide), lambda h, index: (h, 0, 0))
    if total is not None:
        in_specs.append(total_spec)
        operands.append(total)
    aliases = {}
    if gains is None:
        out_spec = total_spec
        out_shape = jax.ShapeDtypeStruct((heads, rows, wide), jnp.float32)
        if total is not None:
            aliases = {len(operands): 0}
    else:
        in_specs.append(pl.BlockSpec((1, 2, wide // 3), lambda h, index: (h, 0, 0)))
        operands.append(gains)
        sizes = [rows] + [PATCHES] * (rows // PATCHES)
        out_spec = [pl.BlockSpec((size, wide // 3), lambda h, index: (0, h)) for size in sizes]
        out_shape = [
            jax.ShapeDtypeStruct((size, heads * wide // 3), jnp.bfloat16) for size in sizes
        ]
    return pl.pallas_call(
        functools.partial(accumulate_kernel, counts, total is not None, gains is not None),
        grid_spec=pltpu.PrefetchScalarGridSpec(
            num_scalar_prefetch=1, grid=(heads,), in_specs=in_specs, out_specs=out_spec
        ),
        out_shape=out_shape,
        input_output_aliases=aliases,
        compiler_params=pltpu.CompilerParams(vmem_limit_bytes=20 * MEGA),
        cost_estimate=SMALL,
        name="accumulate",
    )(index, *operands)


def start_shards(parts, held_ref, sems):
    at = 0
    copies = []
    for k, part in enumerate(parts):
        number = part.shape[0]
        copies.append(pltpu.make_async_copy(part, held_ref.at[pl.ds(at, number)], sems.at[k]))
        copies[-1].start()
        at += number
    return copies


def start_pieces(pieces, near, near_ref, sems):
    copies = []
    count = 0
    for at, piece in enumerate(pieces):
        copies.append([])
        rows = near_ref.shape[1] // len(piece)
        for part, (k, first) in enumerate(piece):
            source = near[k].at[pl.ds(first, rows)]
            place = near_ref.at[at, pl.ds(part * rows, rows)]
            copies[-1].append(pltpu.make_async_copy(source, place, sems.at[count]))
            copies[-1][-1].start()
            count += 1
    return copies


def wait_all(copies):
    for copy in copies:
        copy.wait()


def out_kernel(pieces, held, count, kept, finish, index_ref, *refs):
    near, refs = refs[:held], refs[held:]
    parts, refs = refs[:count], refs[count:]
    if finish:
        given_ref, own_ref, block_ref, *half_refs, stats_ref = refs[:-4]
    else:
        total_ref, kept_ref = refs[:-4]
    near_ref, held_ref, near_sems, sems = refs[-4:]
    shard_copies = start_shards(parts, held_ref, sems)
    piece_copies = start_pieces(pieces, near, near_ref, near_sems)
    wait_all(shard_copies)
    depth = held_ref.shape[1]
    total = [given_ref[0], given_ref[1]] if finish else [None, None]
    for k in range(len(pieces)):
        wait_all(piece_copies[k])
        for half in range(2):
            term = lax.dot_general(
                near_ref[k],
                held_ref[2 * k + half if finish else index_ref[2 * k + half]],
                (((1,), (1,)), ((), ())),
                preferred_element_type=jnp.float32,
            )
            term = term.astype(jnp.bfloat16).astype(jnp.float32)
            total[half] = term if total[half] is None else total[half] + term
    if not finish:
        total_ref[0] = total[0]
        total_ref[1] = total[1]
        for k in range(kept):
            kept_ref[k] = held_ref[index_ref[2 * len(pieces) + k]]
        return
    sums, squares = 0.0, 0.0
    for half in range(2):
        cols = slice(half * depth, (half + 1) * depth)
        block = (own_ref[:, cols].astype(jnp.float32) + total[half]).astype(jnp.bfloat16)
        block_ref[:, cols] = block
        rows = block.shape[0] // 2
        half_refs[0][:rows, cols] = block[:rows]
        half_refs[1][:rows, cols] = block[rows:]
        block = block.astype(jnp.float32)
        sums += jnp.sum(block, 1, keepdims=True)
        squares += jnp.sum(block * block, 1, keepdims=True)
    lane = lax.broadcasted_iota(jnp.int32, (sums.shape[0], 128), 1)
    both = jnp.where(lane == 0, sums, squares).T[:8]
    stats_ref[...] = both
    row = lax.broadcasted_iota(jnp.int32, (EXTRA, both.shape[1]), 0)
    carried = jnp.zeros(row.shape, jnp.float32)
    for k in range(2):
        rest = both[k : k + 1]
        for part in range(3):
            rounded = rest.astype(jnp.bfloat16).astype(jnp.float32)
            carried = jnp.where(row == 3 * k + part, rounded, carried)
            rest = rest - rounded
    carried = carried.astype(jnp.bfloat16)
    for half_ref in half_refs:
        half_ref[rows:, : carried.shape[1]] = carried
        half_ref[rows:, carried.shape[1] :] = jnp.zeros(
            (EXTRA, half_ref.shape[1] - carried.shape[1]), jnp.bfloat16
        )


def held_scratch(pieces, near, parts, wide):
    rows = near[0].shape[0]
    depth = parts[0].shape[1]
    return [
        pltpu.VMEM((len(pieces), rows, near[0].shape[1]), jnp.bfloat16),
        pltpu.VMEM((sum(part.shape[0] for part in parts), depth, wide), jnp.bfloat16),
        pltpu.SemaphoreType.DMA((sum(len(piece) for piece in pieces),)),
        pltpu.SemaphoreType.DMA((len(parts),)),
    ]


def in_hbm(arrays):
    return [pltpu.with_memory_space_constraint(array, pltpu.HBM) for array in arrays]


def whole(shape):
    return pl.BlockSpec(shape, lambda i, index: (0,) * len(shape))


def out_project(near, pieces, parts, index, kept=0, total=None, patches=None):
    depth = parts[0].shape[1]
    finish = total is not None
    place = pl.ANY if finish else pltpu.HBM
    in_specs = [pl.BlockSpec(memory_space=place) for _ in (*near, *parts)]
    operands = [*near, *parts] if finish else in_hbm((*near, *parts))
    rows = near[0].shape[0]
    if finish:
        rows = patches.shape[0]
        in_specs.append(whole(total.shape))
        in_specs.append(pl.BlockSpec((rows, 2 * depth), lambda i, index: (0, index[0])))
        operands += [total, *in_hbm([patches])]
        out_shape = [
            jax.ShapeDtypeStruct((rows, 2 * depth), jnp.bfloat16),
            jax.ShapeDtypeStruct((rows // 2 + EXTRA, 2 * depth), jnp.bfloat16),
            jax.ShapeDtypeStruct((rows // 2 + EXTRA, 2 * depth), jnp.bfloat16),
            jax.ShapeDtypeStruct((8, rows), jnp.float32),
        ]
    else:
        out_shape = [
            jax.ShapeDtypeStruct((2, rows, depth), jnp.float32),
            jax.ShapeDtypeStruct((kept, depth, depth), jnp.bfloat16),
        ]
    return pl.pallas_call(
        functools.partial(out_kernel, pieces, len(near), len(parts), kept, finish),
        grid_spec=pltpu.PrefetchScalarGridSpec(
            num_scalar_prefetch=1,
            grid=(1,),
            in_specs=in_specs,
            out_specs=[whole(out.shape) for out in out_shape],
            scratch_shapes=held_scratch(pieces, near, parts, depth),
        ),
        out_shape=out_shape,
        compiler_params=pltpu.CompilerParams(vmem_limit_bytes=20 * MEGA),
        cost_estimate=SMALL,
        name="out_project",
    )(index, *operands)


def sums_kernel(own_ref, *refs):
    *carried, out_ref = refs
    total = own_ref[...]
    row = lax.broadcasted_iota(jnp.int32, total.shape, 0)
    for ref in carried:
        parts = ref[...].astype(jnp.float32)
        sums, squares = (
            parts[k : k + 1] + parts[k + 1 : k + 2] + parts[k + 2 : k + 3] for k in (0, 3)
        )
        total = total + jnp.where(row == 0, sums, squares)
    out_ref[...] = total


def add_sums(own, carried):
    rows = own.shape[1]
    in_specs = [pl.BlockSpec(own.shape, lambda i: (0, 0))]
    for _, first in carried:
        place = (first + PATCHES) // EXTRA
        in_specs.append(
            pl.BlockSpec((EXTRA, rows), functools.partial(lambda place, i: (place, 0), place))
        )
    return pl.pallas_call(
        sums_kernel,
        grid=(1,),
        in_specs=in_specs,
        out_specs=pl.BlockSpec(own.shape, lambda i: (0, 0)),
        out_shape=jax.ShapeDtypeStruct(own.shape, own.dtype),
        compiler_params=pltpu.CompilerParams(vmem_limit_bytes=4 * MEGA),
        cost_estimate=SMALL,
        name="add_sums",
    )(own, *in_hbm([array for array, _ in carried]))


def project_kernel(pieces, held, count, kept, finish, width, index_ref, *refs):
    near, refs = refs[:held], refs[held:]
    stats_ref, refs = refs[0], refs[1:]
    gains, refs = refs[: len(pieces)], refs[len(pieces) :]
    parts, refs = refs[:count], refs[count:]
    if finish:
        total, (out_ref, *refs, blocks_ref) = refs[0][...], refs[1:]
    else:
        total, (out_ref, kept_ref, *refs) = None, refs
    near_ref, held_ref, near_sems, sems = refs
    shard_copies = start_shards(parts, held_ref, sems)
    piece_copies = start_pieces(pieces, near, near_ref, near_sems)
    rows = stats_ref.shape[1]
    row = lax.broadcasted_iota(jnp.int32, (128, rows), 0)
    stats = jnp.where(row == 0, stats_ref[0:1], stats_ref[1:2]).T
    row_mean = stats[:, 0:1] / width
    scale = lax.rsqrt(stats[:, 1:2] / width - row_mean * row_mean + epsilon)
    wait_all(shard_copies)
    for k in range(len(pieces)):
        wait_all(piece_copies[k])
        values = near_ref[k].astype(jnp.float32)
        normed = ((values - row_mean) * scale * gains[k][...]).astype(jnp.bfloat16)
        held = [
            held_ref[2 * k + half if finish else index_ref[2 * k + half]] for half in range(2)
        ]
        term = jnp.dot(normed, jnp.concatenate(held, 0), preferred_element_type=jnp.float32)
        total = term if total is None else total + term
    if not finish:
        out_ref[...] = total
        for k in range(kept):
            kept_ref[k] = held_ref[index_ref[2 * len(pieces) + k]]
        return
    blocks_ref[...] = total.astype(jnp.bfloat16).reshape(blocks_ref.shape)
    for block in range(out_ref.shape[0]):
        source = index_ref[len(pieces) + block]
        value = blocks_ref[jnp.maximum(source, 0)]
        out_ref[block] = jnp.where(source >= 0, value, jnp.zeros_like(value))


def project(near, pieces, stats, gain, parts, index, kept=0, total=None):
    rows = stats.shape[1]
    width = gain.shape[0]
    depth, wide = parts[0].shape[1:]
    count = len(pieces)
    finish = total is not None
    at = 0 if finish else 2 * count + kept
    place = pl.ANY if finish else pltpu.HBM
    in_specs = [pl.BlockSpec(memory_space=place) for _ in near]
    in_specs.append(whole(stats.shape))
    in_specs += [
        pl.BlockSpec((1, 2 * depth), functools.partial(lambda k, i, index: (0, index[k]), k))
        for k in range(at, at + count)
    ]
    in_specs += [pl.BlockSpec(memory_space=place) for _ in parts]
    operands = (list(near) if finish else in_hbm(near)) + [stats]
    operands += [gain.reshape(1, width)] * count
    operands += parts if finish else in_hbm(parts)
    scratch = held_scratch(pieces, near, parts, wide)
    if finish:
        in_specs.append(whole(total.shape))
        operands.append(total)
        out_shape = [jax.ShapeDtypeStruct((8, HALF, wide), jnp.bfloat16)]
        scratch.append(pltpu.VMEM((rows // HALF, HALF, wide), jnp.bfloat16))
    else:
        out_shape = [
            jax.ShapeDtypeStruct((rows, wide), jnp.float32),
            jax.ShapeDtypeStruct((kept, depth, wide), jnp.bfloat16),
        ]
    return pl.pallas_call(
        functools.partial(
            project_kernel, pieces, len(near), len(parts), kept, finish, width
        ),
        grid_spec=pltpu.PrefetchScalarGridSpec(
            num_scalar_prefetch=1,
            grid=(1,),
            in_specs=in_specs,
            out_specs=[whole(out.shape) for out in out_shape],
            scratch_shapes=scratch,
        ),
        out_shape=out_shape,
        compiler_params=pltpu.CompilerParams(vmem_limit_bytes=28 * MEGA),
        cost_estimate=SMALL,
        name="project",
    )(index, *operands)


def pack_kernel(place_ref, arrived_ref, text_ref, out_ref):
    start, first, second, length = (place_ref[k] for k in range(4))
    rows, wide = arrived_ref.shape[1:]
    covered = ((start >= first) & (start < first + PATCHES)) | (
        (start >= second) & (start < second + PATCHES)
    )

    @pl.when(covered)
    def _():
        for k in range(arrived_ref.shape[0]):
            out_ref[:, k * wide : (k + 1) * wide] = arrived_ref[k]

    @pl.when(jnp.logical_not(covered))
    def _():
        position = start + lax.broadcasted_iota(jnp.int32, (rows, wide), 0)
        before = jnp.clip(position - first, 0, PATCHES) + jnp.clip(position - second, 0, PATCHES)
        is_text = position - before < length
        for k in range(arrived_ref.shape[0]):
            text = text_ref[:, k * wide : (k + 1) * wide].astype(jnp.float32)
            out_ref[:, k * wide : (k + 1) * wide] = jnp.where(is_text, text, 0.0).astype(
                jnp.bfloat16
            )


def pack(arrived, text, place):
    return pl.pallas_call(
        pack_kernel,
        grid_spec=pltpu.PrefetchScalarGridSpec(
            num_scalar_prefetch=1,
            grid=(1,),
            in_specs=[whole(arrived.shape), whole(text.shape)],
            out_specs=whole(text.shape),
        ),
        out_shape=jax.ShapeDtypeStruct(text.shape, text.dtype),
        compiler_params=pltpu.CompilerParams(vmem_limit_bytes=8 * MEGA),
        cost_estimate=SMALL,
        name="pack",
    )(place, arrived, text)


def join(*values):
    return lax.optimization_barrier(values)


def piece_places(step):
    first = (
        ((0, 0),),
        ((1, 0),),
        ((5, step), (3, 0)),
        ((2, 0), (4, step)),
        ((4, 0), (5, 0)),
    )
    return first, (((0, 0),), ((1, 0),), ((2, 0), (2, PATCHES)))


def local(
    patches,
    norm_gain,
    qkv_weight,
    qk_gain,
    out_weight,
    final_gain,
    proj_weight,
    text_embed,
    slot_offset,
    text_len,
):
    own = qkv_weight.transpose(1, 0, 2)
    first = spread_y(own)
    other = swap_core(own)
    far = swap_zh(own)
    half_turned = turn_first(out_weight)
    (other,) = join(other)
    beside = spread_y(other)
    columns = norm_columns(join(patches, other)[0], norm_gain, 16)
    dp = lax.axis_index("dp")
    mp = lax.axis_index("mp")
    met = jnp.asarray(per_device(early_order))[dp]
    total = accumulate(columns, [own, other], met[0:2])

    far, first, beside, half_turned, total = join(far, first, beside, half_turned, total)
    far_first = spread_y(far)
    second = spread_y(first)
    far_beside = swap_zh(beside)
    turned = turn_second(half_turned)
    far_other, first_other, beside_other = join(
        swap_core(far), swap_core(first), swap_core(beside)
    )
    total = accumulate(
        columns,
        [far, far_other, first, first_other, beside, beside_other],
        met[2:8],
        total,
    )
    total, slot_offset, text_len, dp, mp = join(total, slot_offset, text_len, dp, mp)
    groups, shards = place_tables()
    groups, shards = jnp.asarray(groups)[mp], jnp.asarray(shards)[:, dp, mp]
    shards, out_shards = shards[0], shards[1]
    mp_slot = mp[None].astype(jnp.int32)
    slot = slot_offset // HALF
    block = jnp.arange(8, dtype=jnp.int32)
    in_first = (block >= slot[0]) & (block < slot[0] + 2)
    in_second = (block >= slot[1]) & (block < slot[1] + 2)
    source = jnp.where(in_first, block - slot[0], jnp.where(in_second, block - slot[1] + 2, -1))

    first_index = jnp.concatenate([shards, groups[:5]])
    last_index = jnp.concatenate([groups[5:], source])
    pack_index = jnp.concatenate([mp_slot * HALF, slot_offset, text_len])

    far_first, second, far_beside, turned, total, first_index, last_index, pack_index = join(
        far_first, second, far_beside, turned, total, first_index, last_index, pack_index
    )
    far_second = spread_y(far_first)
    turned_far = swap_zh(turned)
    proj_far = swap_zh(join(proj_weight, turned)[0])
    far_first_other, second_other, far_beside_other = join(
        swap_core(far_first), swap_core(second), swap_core(far_beside)
    )
    total = accumulate(
        columns,
        [far_first, far_first_other, second, second_other, far_beside, far_beside_other],
        met[8:14],
        total,
    )

    far_second, turned_far, proj_far, total = join(far_second, turned_far, proj_far, total)
    far_second_other = swap_core(far_second)
    out_mine = jnp.stack([turned, turned_far])
    out_other = swap_core(out_mine)
    out_quad = jnp.concatenate([out_mine, out_other])
    out_first = spread_y(out_quad)
    attended = accumulate(
        columns, [far_second, far_second_other], met[14:16], total, qk_gain.transpose(1, 0, 2)
    )

    whole_att, low, high = join(*attended)
    far = swap_zl(whole_att)
    left_low, right_high, far, out_first, low, high, proj_far = join(
        shift_x(low, 1), shift_x(high, -1), far, out_first, low, high, proj_far
    )
    proj_mine = jnp.stack([proj_weight, proj_far])
    proj_other = swap_core(proj_mine)
    out_second = spread_y(out_first[:2])
    out_first_other = swap_core(out_first)
    from_left, from_right, out_second, out_first_other, proj_other = join(
        shift_x(jnp.concatenate([left_low, high]), 1),
        shift_x(jnp.concatenate([right_high, low]), -1),
        out_second,
        out_first_other,
        proj_other,
    )
    proj_quad = jnp.concatenate([proj_mine, proj_other])
    near = [whole_att, far, left_low, right_high, from_left, from_right]
    pieces, last_pieces = piece_places(PATCHES)
    out_second_other = swap_core(out_second)
    proj_first = spread_y(proj_quad)
    beyond = jnp.concatenate([from_left[:PATCHES], from_right[:PATCHES]])
    last = [shift_x(far, -1), shift_x(far, 1), swap_zl(beyond)]
    parts = [out_quad, out_first, out_first_other, out_second, out_second_other]
    total, left = out_project(near, pieces, parts, out_shards, kept=6)
    block_out, low, high, stats = out_project(
        last, last_pieces, [left], mp_slot, total=total, patches=patches
    )

    proj_first, whole_block, low, high, stats = join(proj_first, block_out, low, high, stats)
    far = swap_zl(whole_block)
    proj_second = spread_y(proj_first[:2])
    proj_first_other = swap_core(proj_first)
    left_low, right_high, proj_first_other, proj_second, low, high = join(
        shift_x(low, 1), shift_x(high, -1), proj_first_other, proj_second, low, high
    )
    from_left, from_right, far = join(
        shift_x(jnp.concatenate([left_low, high]), 1),
        shift_x(jnp.concatenate([right_high, low]), -1),
        far,
    )
    stats = add_sums(stats, [(left_low, 0), (right_high, 0), (from_left, 0)])
    stats_z = swap_zl(stats)
    stats = stats + stats_z
    near = [whole_block, far, left_low, right_high, from_left, from_right]
    pieces, last_pieces = piece_places(PATCHES + EXTRA)
    beyond = jnp.concatenate([from_left[:PATCHES], from_right[:PATCHES]])
    beyond = join(beyond, stats_z)[0]
    last = [shift_x(far, -1), shift_x(far, 1), swap_zl(beyond)]
    parts = [proj_quad, proj_first, proj_first_other, proj_second, swap_core(proj_second)]

    total, left = project(
        near,
        pieces,
        stats,
        final_gain,
        parts,
        first_index,
        kept=6,
    )
    (outgoing,) = project(
        last,
        last_pieces,
        stats,
        final_gain,
        [left],
        last_index,
        total=total,
    )
    arrived = lax.all_to_all(outgoing, "mp", split_axis=0, concat_axis=0, tiled=True)
    sequence = pack(arrived, text_embed[0], pack_index)
    return (block_out, sequence[None])


def solution(mesh):
    in_specs = (
        P("dp", None),
        P(),
        P("dp", "mp", None),
        P(None, "mp", None),
        P("dp", "mp"),
        P(),
        P("dp", "mp"),
        P("dp", "mp", None),
        P("dp"),
        P("dp"),
    )
    out_specs = (P("dp", "mp"), P("dp", "mp", None))
    return jax.shard_map(local, mesh=mesh, in_specs=in_specs, out_specs=out_specs, check_vma=False)
```

```python
import functools
import math

import jax
import jax.numpy as jnp
import numpy as np
from jax import lax
from jax.experimental import pallas as pl
from jax.experimental.pallas import tpu as pltpu
from jax.sharding import PartitionSpec as P

PATCHES = 256
HALF = 128
AXES = ("dp", "mp")
MEGA = 1024 * 1024
epsilon = 1e-06
EXTRA = 16
SMALL = pl.CostEstimate(flops=1, bytes_accessed=1, transcendentals=0)


def coordinates():
    return [
        (zh, y, c, zl, x)
        for zh in range(2)
        for y in range(4)
        for c in range(2)
        for zl in range(2)
        for x in range(4)
    ]


def device_index(zh, y, c, zl, x):
    return ((zh * 4 + y) * 2 + c) * 8 + zl * 4 + x


def move(values, target):
    pairs = [(device_index(*at), device_index(*target(*at))) for at in coordinates()]
    return lax.ppermute(values, AXES, pairs)


def swap_core(values):
    return move(values, lambda zh, y, c, zl, x: (zh, y, 1 - c, zl, x))


def swap_zh(values):
    return move(values, lambda zh, y, c, zl, x: (1 - zh, y, c, zl, x))


def swap_zl(values):
    return move(values, lambda zh, y, c, zl, x: (zh, y, c, 1 - zl, x))


def spread_y(values):
    return move(values, lambda zh, y, c, zl, x: (zh, (y + 1 - 2 * c) % 4, c, zl, x))


def shift_x(values, step):
    return move(values, lambda zh, y, c, zl, x: (zh, y, c, zl, (x + step) % 4))


def turn_first(values):
    return move(values, lambda zh, y, c, zl, x: (zl, (x + y) % 4, c, zh, x))


def turn_second(values):
    return move(values, lambda zh, y, c, zl, x: (zh, y, c, zl, (y - x) % 4))


def per_device(order):
    table = np.zeros((16, 16), np.int32)
    for zh in range(2):
        for y in range(4):
            for c in range(2):
                met = order(zh, y, c, 2 * c - 1)
                table[zh * 8 + y * 2 + c] = [r % 2 * 8 + yy % 4 * 2 + cc % 2 for r, yy, cc in met]
    return table


def early_order(zh, y, c, step):
    return [
        (zh, y, c),
        (zh, y, c + 1),
        (zh + 1, y, c),
        (zh + 1, y, c + 1),
        (zh, y + step, c),
        (zh, y - step, c + 1),
        (zh, y + step, c + 1),
        (zh, y - step, c),
        (zh + 1, y + step, c),
        (zh + 1, y - step, c + 1),
        (zh, y + 2, c),
        (zh, y + 2, c + 1),
        (zh + 1, y + step, c + 1),
        (zh + 1, y - step, c),
        (zh + 1, y + 2, c),
        (zh + 1, y + 2, c + 1),
    ]


def late_order(zh, y, c, step):
    order = []
    for yy, cores in (
        (y, (c, c + 1)),
        (y + step, (c, c + 1)),
        (y - step, (c + 1, c)),
        (y + 2, (c, c + 1)),
    ):
        for core in cores:
            order += [(zh, yy, core), (zh + 1, yy, core)]
    return order


NEAR = [(0, 0), (1, 0), (0, 1), (0, 3), (0, 2), (1, 1), (1, 3), (1, 2)]


def place_tables():
    met = per_device(late_order)
    groups = np.zeros((8, 8), np.int32)
    shards = np.zeros((2, 16, 8, 16), np.int32)
    for mp in range(8):
        for r, (dz, dx) in enumerate(NEAR):
            group = (mp // 4 ^ dz) * 4 + (mp + dx) % 4
            groups[mp, r] = group
            turned = group // 4 * 4 + (group + mp) % 4
            for dp in range(16):
                for half in range(2):
                    shards[0, dp, mp, 2 * r + half] = np.argmax(met[dp] == 2 * group + half)
                    shards[1, dp, mp, 2 * r + half] = np.argmax(met[dp] == 2 * turned + half)
    return groups, shards


def norm_kernel(values_ref, gain_ref, out_ref):
    values = values_ref[...].astype(jnp.float32)
    width = values.shape[1]
    row_mean = jnp.sum(values, -1, keepdims=True) / width
    squares = jnp.sum(values * values, -1, keepdims=True) / width
    scale = lax.rsqrt(squares - row_mean * row_mean + epsilon)
    normed = ((values - row_mean) * scale * gain_ref[...]).astype(jnp.bfloat16)
    depth = out_ref.shape[2]
    for k in range(out_ref.shape[0]):
        out_ref[k] = normed[:, k * depth : (k + 1) * depth]


def norm_columns(values, gain, chunks):
    rows, width = values.shape
    block = 64
    return pl.pallas_call(
        norm_kernel,
        grid=(rows // block,),
        in_specs=[
            pl.BlockSpec((block, width), lambda i: (i, 0)),
            pl.BlockSpec((1, width), lambda i: (0, 0)),
        ],
        out_specs=pl.BlockSpec((chunks, block, width // chunks), lambda i: (0, i, 0)),
        out_shape=jax.ShapeDtypeStruct((chunks, rows, width // chunks), jnp.bfloat16),
        compiler_params=pltpu.CompilerParams(vmem_limit_bytes=16 * MEGA),
        cost_estimate=SMALL,
        name="norm_columns",
    )(*in_hbm([values]), gain.reshape(1, width))


def row_norm(values, gain):
    row_mean = jnp.mean(values, -1, keepdims=True)
    squares = jnp.mean(values * values, -1, keepdims=True)
    return (values - row_mean) * lax.rsqrt(squares - row_mean * row_mean + epsilon) * gain


def accumulate_kernel(shard_counts, has_total, attend, index_ref, *refs):
    del index_ref
    count = sum(shard_counts)
    columns, refs = refs[:count], refs[count:]
    shards, refs = refs[: len(shard_counts)], refs[len(shard_counts) :]
    total = None
    if has_total:
        total, refs = refs[0][0], refs[1:]
    held = [ref[k, 0] for ref, number in zip(shards, shard_counts) for k in range(number)]
    term = jnp.dot(
        jnp.concatenate([ref[0] for ref in columns], 1),
        jnp.concatenate(held, 0),
        preferred_element_type=jnp.float32,
    )
    total = term if total is None else total + term
    if not attend:
        refs[0][0] = total
        return
    gain_ref, out_ref, *image_refs = refs
    size = gain_ref.shape[2]
    gains = gain_ref[0]
    query = row_norm(total[:, :size], gains[0:1]).astype(jnp.bfloat16)
    key = row_norm(total[:, size : 2 * size], gains[1:2]).astype(jnp.bfloat16)
    value = total[:, 2 * size :].astype(jnp.bfloat16)
    for image in range(total.shape[0] // PATCHES):
        rows = slice(image * PATCHES, (image + 1) * PATCHES)
        scores = lax.dot_general(
            query[rows], key[rows], (((1,), (1,)), ((), ())), preferred_element_type=jnp.float32
        ) / math.sqrt(size)
        raised = jnp.exp(scores - jnp.max(scores, -1, keepdims=True))
        weights = (raised / jnp.sum(raised, -1, keepdims=True)).astype(jnp.bfloat16)
        attended = jnp.dot(weights, value[rows], preferred_element_type=jnp.float32)
        attended = attended.astype(jnp.bfloat16)
        out_ref[rows, :] = attended
        image_refs[image][...] = attended


def accumulate(columns, shards, index, total=None, gains=None):
    shards = [held if held.ndim == 4 else held[None] for held in shards]
    counts = tuple(held.shape[0] for held in shards)
    _, rows, depth = columns.shape
    heads, wide = shards[0].shape[1], shards[0].shape[3]
    in_specs = [
        pl.BlockSpec((1, rows, depth), functools.partial(lambda k, h, index: (index[k], 0, 0), k))
        for k in range(sum(counts))
    ]
    in_specs += [
        pl.BlockSpec((number, 1, depth, wide), lambda h, index: (0, h, 0, 0)) for number in counts
    ]
    operands = [columns] * sum(counts) + (in_hbm(shards) if gains is None else shards)
    total_spec = pl.BlockSpec((1, rows, wide), lambda h, index: (h, 0, 0))
    if total is not None:
        in_specs.append(total_spec)
        operands.append(total)
    aliases = {}
    if gains is None:
        out_spec = total_spec
        out_shape = jax.ShapeDtypeStruct((heads, rows, wide), jnp.float32)
        if total is not None:
            aliases = {len(operands): 0}
    else:
        in_specs.append(pl.BlockSpec((1, 2, wide // 3), lambda h, index: (h, 0, 0)))
        operands.append(gains)
        sizes = [rows] + [PATCHES] * (rows // PATCHES)
        out_spec = [pl.BlockSpec((size, wide // 3), lambda h, index: (0, h)) for size in sizes]
        out_shape = [
            jax.ShapeDtypeStruct((size, heads * wide // 3), jnp.bfloat16) for size in sizes
        ]
    return pl.pallas_call(
        functools.partial(accumulate_kernel, counts, total is not None, gains is not None),
        grid_spec=pltpu.PrefetchScalarGridSpec(
            num_scalar_prefetch=1, grid=(heads,), in_specs=in_specs, out_specs=out_spec
        ),
        out_shape=out_shape,
        input_output_aliases=aliases,
        compiler_params=pltpu.CompilerParams(vmem_limit_bytes=20 * MEGA),
        cost_estimate=SMALL,
        name="accumulate",
    )(index, *operands)


def start_shards(parts, held_ref, sems):
    at = 0
    copies = []
    for k, part in enumerate(parts):
        number = part.shape[0]
        copies.append(pltpu.make_async_copy(part, held_ref.at[pl.ds(at, number)], sems.at[k]))
        copies[-1].start()
        at += number
    return copies


def start_pieces(pieces, near, near_ref, sems):
    copies = []
    count = 0
    for at, piece in enumerate(pieces):
        copies.append([])
        rows = near_ref.shape[1] // len(piece)
        for part, (k, first) in enumerate(piece):
            source = near[k].at[pl.ds(first, rows)]
            place = near_ref.at[at, pl.ds(part * rows, rows)]
            copies[-1].append(pltpu.make_async_copy(source, place, sems.at[count]))
            copies[-1][-1].start()
            count += 1
    return copies


def wait_all(copies):
    for copy in copies:
        copy.wait()


def out_kernel(pieces, held, count, kept, finish, index_ref, *refs):
    near, refs = refs[:held], refs[held:]
    parts, refs = refs[:count], refs[count:]
    if finish:
        given_ref, own_ref, block_ref, *half_refs, stats_ref = refs[:-4]
    else:
        total_ref, kept_ref = refs[:-4]
    near_ref, held_ref, near_sems, sems = refs[-4:]
    shard_copies = start_shards(parts, held_ref, sems)
    piece_copies = start_pieces(pieces, near, near_ref, near_sems)
    wait_all(shard_copies)
    depth = held_ref.shape[1]
    total = [given_ref[0], given_ref[1]] if finish else [None, None]
    for k in range(len(pieces)):
        wait_all(piece_copies[k])
        for half in range(2):
            term = lax.dot_general(
                near_ref[k],
                held_ref[2 * k + half if finish else index_ref[2 * k + half]],
                (((1,), (1,)), ((), ())),
                preferred_element_type=jnp.float32,
            )
            term = term.astype(jnp.bfloat16).astype(jnp.float32)
            total[half] = term if total[half] is None else total[half] + term
    if not finish:
        total_ref[0] = total[0]
        total_ref[1] = total[1]
        for k in range(kept):
            kept_ref[k] = held_ref[index_ref[2 * len(pieces) + k]]
        return
    sums, squares = 0.0, 0.0
    for half in range(2):
        cols = slice(half * depth, (half + 1) * depth)
        block = (own_ref[:, cols].astype(jnp.float32) + total[half]).astype(jnp.bfloat16)
        block_ref[:, cols] = block
        rows = block.shape[0] // 2
        half_refs[0][:rows, cols] = block[:rows]
        half_refs[1][:rows, cols] = block[rows:]
        block = block.astype(jnp.float32)
        sums += jnp.sum(block, 1, keepdims=True)
        squares += jnp.sum(block * block, 1, keepdims=True)
    lane = lax.broadcasted_iota(jnp.int32, (sums.shape[0], 128), 1)
    both = jnp.where(lane == 0, sums, squares).T[:8]
    stats_ref[...] = both
    row = lax.broadcasted_iota(jnp.int32, (EXTRA, both.shape[1]), 0)
    carried = jnp.zeros(row.shape, jnp.float32)
    for k in range(2):
        rest = both[k : k + 1]
        for part in range(3):
            rounded = rest.astype(jnp.bfloat16).astype(jnp.float32)
            carried = jnp.where(row == 3 * k + part, rounded, carried)
            rest = rest - rounded
    carried = carried.astype(jnp.bfloat16)
    for half_ref in half_refs:
        half_ref[rows:, : carried.shape[1]] = carried
        half_ref[rows:, carried.shape[1] :] = jnp.zeros(
            (EXTRA, half_ref.shape[1] - carried.shape[1]), jnp.bfloat16
        )


def held_scratch(pieces, near, parts, wide):
    rows = near[0].shape[0]
    depth = parts[0].shape[1]
    return [
        pltpu.VMEM((len(pieces), rows, near[0].shape[1]), jnp.bfloat16),
        pltpu.VMEM((sum(part.shape[0] for part in parts), depth, wide), jnp.bfloat16),
        pltpu.SemaphoreType.DMA((sum(len(piece) for piece in pieces),)),
        pltpu.SemaphoreType.DMA((len(parts),)),
    ]


def in_hbm(arrays):
    return [pltpu.with_memory_space_constraint(array, pltpu.HBM) for array in arrays]


def whole(shape):
    return pl.BlockSpec(shape, lambda i, index: (0,) * len(shape))


def out_project(near, pieces, parts, index, kept=0, total=None, patches=None):
    depth = parts[0].shape[1]
    finish = total is not None
    place = pl.ANY if finish else pltpu.HBM
    in_specs = [pl.BlockSpec(memory_space=place) for _ in (*near, *parts)]
    operands = [*near, *parts] if finish else in_hbm((*near, *parts))
    rows = near[0].shape[0]
    if finish:
        rows = patches.shape[0]
        in_specs.append(whole(total.shape))
        in_specs.append(pl.BlockSpec((rows, 2 * depth), lambda i, index: (0, index[0])))
        operands += [total, *in_hbm([patches])]
        out_shape = [
            jax.ShapeDtypeStruct((rows, 2 * depth), jnp.bfloat16),
            jax.ShapeDtypeStruct((rows // 2 + EXTRA, 2 * depth), jnp.bfloat16),
            jax.ShapeDtypeStruct((rows // 2 + EXTRA, 2 * depth), jnp.bfloat16),
            jax.ShapeDtypeStruct((8, rows), jnp.float32),
        ]
    else:
        out_shape = [
            jax.ShapeDtypeStruct((2, rows, depth), jnp.float32),
            jax.ShapeDtypeStruct((kept, depth, depth), jnp.bfloat16),
        ]
    return pl.pallas_call(
        functools.partial(out_kernel, pieces, len(near), len(parts), kept, finish),
        grid_spec=pltpu.PrefetchScalarGridSpec(
            num_scalar_prefetch=1,
            grid=(1,),
            in_specs=in_specs,
            out_specs=[whole(out.shape) for out in out_shape],
            scratch_shapes=held_scratch(pieces, near, parts, depth),
        ),
        out_shape=out_shape,
        compiler_params=pltpu.CompilerParams(vmem_limit_bytes=20 * MEGA),
        cost_estimate=SMALL,
        name="out_project",
    )(index, *operands)


def sums_kernel(own_ref, *refs):
    *carried, out_ref = refs
    total = own_ref[...]
    row = lax.broadcasted_iota(jnp.int32, total.shape, 0)
    for ref in carried:
        parts = ref[...].astype(jnp.float32)
        sums, squares = (
            parts[k : k + 1] + parts[k + 1 : k + 2] + parts[k + 2 : k + 3] for k in (0, 3)
        )
        total = total + jnp.where(row == 0, sums, squares)
    out_ref[...] = total


def add_sums(own, carried):
    rows = own.shape[1]
    in_specs = [pl.BlockSpec(own.shape, lambda i: (0, 0))]
    for _, first in carried:
        place = (first + PATCHES) // EXTRA
        in_specs.append(
            pl.BlockSpec((EXTRA, rows), functools.partial(lambda place, i: (place, 0), place))
        )
    return pl.pallas_call(
        sums_kernel,
        grid=(1,),
        in_specs=in_specs,
        out_specs=pl.BlockSpec(own.shape, lambda i: (0, 0)),
        out_shape=jax.ShapeDtypeStruct(own.shape, own.dtype),
        compiler_params=pltpu.CompilerParams(vmem_limit_bytes=4 * MEGA),
        cost_estimate=SMALL,
        name="add_sums",
    )(own, *in_hbm([array for array, _ in carried]))


def project_kernel(pieces, held, count, kept, finish, width, index_ref, *refs):
    near, refs = refs[:held], refs[held:]
    stats_ref, refs = refs[0], refs[1:]
    gains, refs = refs[: len(pieces)], refs[len(pieces) :]
    parts, refs = refs[:count], refs[count:]
    if finish:
        total, (out_ref, *refs, blocks_ref) = refs[0][...], refs[1:]
    else:
        total, (out_ref, kept_ref, *refs) = None, refs
    near_ref, held_ref, near_sems, sems = refs
    shard_copies = start_shards(parts, held_ref, sems)
    piece_copies = start_pieces(pieces, near, near_ref, near_sems)
    rows = stats_ref.shape[1]
    row = lax.broadcasted_iota(jnp.int32, (128, rows), 0)
    stats = jnp.where(row == 0, stats_ref[0:1], stats_ref[1:2]).T
    row_mean = stats[:, 0:1] / width
    scale = lax.rsqrt(stats[:, 1:2] / width - row_mean * row_mean + epsilon)
    wait_all(shard_copies)
    for k in range(len(pieces)):
        wait_all(piece_copies[k])
        values = near_ref[k].astype(jnp.float32)
        normed = ((values - row_mean) * scale * gains[k][...]).astype(jnp.bfloat16)
        held = [
            held_ref[2 * k + half if finish else index_ref[2 * k + half]] for half in range(2)
        ]
        term = jnp.dot(normed, jnp.concatenate(held, 0), preferred_element_type=jnp.float32)
        total = term if total is None else total + term
    if not finish:
        out_ref[...] = total
        for k in range(kept):
            kept_ref[k] = held_ref[index_ref[2 * len(pieces) + k]]
        return
    blocks_ref[...] = total.astype(jnp.bfloat16).reshape(blocks_ref.shape)
    for block in range(out_ref.shape[0]):
        source = index_ref[len(pieces) + block]
        value = blocks_ref[jnp.maximum(source, 0)]
        out_ref[block] = jnp.where(source >= 0, value, jnp.zeros_like(value))


def project(near, pieces, stats, gain, parts, index, kept=0, total=None):
    rows = stats.shape[1]
    width = gain.shape[0]
    depth, wide = parts[0].shape[1:]
    count = len(pieces)
    finish = total is not None
    at = 0 if finish else 2 * count + kept
    place = pl.ANY if finish else pltpu.HBM
    in_specs = [pl.BlockSpec(memory_space=place) for _ in near]
    in_specs.append(whole(stats.shape))
    in_specs += [
        pl.BlockSpec((1, 2 * depth), functools.partial(lambda k, i, index: (0, index[k]), k))
        for k in range(at, at + count)
    ]
    in_specs += [pl.BlockSpec(memory_space=place) for _ in parts]
    operands = (list(near) if finish else in_hbm(near)) + [stats]
    operands += [gain.reshape(1, width)] * count
    operands += parts if finish else in_hbm(parts)
    scratch = held_scratch(pieces, near, parts, wide)
    if finish:
        in_specs.append(whole(total.shape))
        operands.append(total)
        out_shape = [jax.ShapeDtypeStruct((8, HALF, wide), jnp.bfloat16)]
        scratch.append(pltpu.VMEM((rows // HALF, HALF, wide), jnp.bfloat16))
    else:
        out_shape = [
            jax.ShapeDtypeStruct((rows, wide), jnp.float32),
            jax.ShapeDtypeStruct((kept, depth, wide), jnp.bfloat16),
        ]
    return pl.pallas_call(
        functools.partial(
            project_kernel, pieces, len(near), len(parts), kept, finish, width
        ),
        grid_spec=pltpu.PrefetchScalarGridSpec(
            num_scalar_prefetch=1,
            grid=(1,),
            in_specs=in_specs,
            out_specs=[whole(out.shape) for out in out_shape],
            scratch_shapes=scratch,
        ),
        out_shape=out_shape,
        compiler_params=pltpu.CompilerParams(vmem_limit_bytes=28 * MEGA),
        cost_estimate=SMALL,
        name="project",
    )(index, *operands)


def pack_kernel(place_ref, arrived_ref, text_ref, out_ref):
    start, first, second, length = (place_ref[k] for k in range(4))
    rows, wide = arrived_ref.shape[1:]
    covered = ((start >= first) & (start < first + PATCHES)) | (
        (start >= second) & (start < second + PATCHES)
    )

    @pl.when(covered)
    def _():
        for k in range(arrived_ref.shape[0]):
            out_ref[:, k * wide : (k + 1) * wide] = arrived_ref[k]

    @pl.when(jnp.logical_not(covered))
    def _():
        position = start + lax.broadcasted_iota(jnp.int32, (rows, wide), 0)
        before = jnp.clip(position - first, 0, PATCHES) + jnp.clip(position - second, 0, PATCHES)
        is_text = position - before < length
        for k in range(arrived_ref.shape[0]):
            text = text_ref[:, k * wide : (k + 1) * wide].astype(jnp.float32)
            out_ref[:, k * wide : (k + 1) * wide] = jnp.where(is_text, text, 0.0).astype(
                jnp.bfloat16
            )


def pack(arrived, text, place):
    return pl.pallas_call(
        pack_kernel,
        grid_spec=pltpu.PrefetchScalarGridSpec(
            num_scalar_prefetch=1,
            grid=(1,),
            in_specs=[whole(arrived.shape), whole(text.shape)],
            out_specs=whole(text.shape),
        ),
        out_shape=jax.ShapeDtypeStruct(text.shape, text.dtype),
        compiler_params=pltpu.CompilerParams(vmem_limit_bytes=8 * MEGA),
        cost_estimate=SMALL,
        name="pack",
    )(place, arrived, text)


def join(*values):
    return lax.optimization_barrier(values)


def piece_places(step):
    first = (
        ((0, 0),),
        ((1, 0),),
        ((5, step), (3, 0)),
        ((2, 0), (4, step)),
        ((4, 0), (5, 0)),
    )
    return first, (((0, 0),), ((1, 0),), ((2, 0), (2, PATCHES)))


def local(
    patches,
    norm_gain,
    qkv_weight,
    qk_gain,
    out_weight,
    final_gain,
    proj_weight,
    text_embed,
    slot_offset,
    text_len,
):
    own = qkv_weight.transpose(1, 0, 2)
    first = spread_y(own)
    other = swap_core(own)
    far = swap_zh(own)
    half_turned = turn_first(out_weight)
    (other,) = join(other)
    beside = spread_y(other)
    columns = norm_columns(join(patches, other)[0], norm_gain, 16)
    dp = lax.axis_index("dp")
    mp = lax.axis_index("mp")
    met = jnp.asarray(per_device(early_order))[dp]
    total = accumulate(columns, [own, other], met[0:2])

    far, first, beside, half_turned, total = join(far, first, beside, half_turned, total)
    far_first = spread_y(far)
    second = spread_y(first)
    far_beside = swap_zh(beside)
    turned = turn_second(half_turned)
    far_other, first_other, beside_other = join(
        swap_core(far), swap_core(first), swap_core(beside)
    )
    total = accumulate(
        columns,
        [far, far_other, first, first_other, beside, beside_other],
        met[2:8],
        total,
    )
    total, slot_offset, text_len, dp, mp = join(total, slot_offset, text_len, dp, mp)
    groups, shards = place_tables()
    groups, shards = jnp.asarray(groups)[mp], jnp.asarray(shards)[:, dp, mp]
    shards, out_shards = shards[0], shards[1]
    mp_slot = mp[None].astype(jnp.int32)
    slot = slot_offset // HALF
    block = jnp.arange(8, dtype=jnp.int32)
    in_first = (block >= slot[0]) & (block < slot[0] + 2)
    in_second = (block >= slot[1]) & (block < slot[1] + 2)
    source = jnp.where(in_first, block - slot[0], jnp.where(in_second, block - slot[1] + 2, -1))

    first_index = jnp.concatenate([shards, groups[:5]])
    last_index = jnp.concatenate([groups[5:], source])
    pack_index = jnp.concatenate([mp_slot * HALF, slot_offset, text_len])

    far_first, second, far_beside, turned, total, first_index, last_index, pack_index = join(
        far_first, second, far_beside, turned, total, first_index, last_index, pack_index
    )
    far_second = spread_y(far_first)
    turned_far = swap_zh(turned)
    proj_far = swap_zh(join(proj_weight, turned)[0])
    far_first_other, second_other, far_beside_other = join(
        swap_core(far_first), swap_core(second), swap_core(far_beside)
    )
    total = accumulate(
        columns,
        [far_first, far_first_other, second, second_other, far_beside, far_beside_other],
        met[8:14],
        total,
    )

    far_second, turned_far, proj_far, total = join(far_second, turned_far, proj_far, total)
    far_second_other = swap_core(far_second)
    out_mine = jnp.stack([turned, turned_far])
    out_other = swap_core(out_mine)
    out_quad = jnp.concatenate([out_mine, out_other])
    out_first = spread_y(out_quad)
    attended = accumulate(
        columns, [far_second, far_second_other], met[14:16], total, qk_gain.transpose(1, 0, 2)
    )

    whole_att, low, high = join(*attended)
    far = swap_zl(whole_att)
    left_low, right_high, far, out_first, low, high, proj_far = join(
        shift_x(low, 1), shift_x(high, -1), far, out_first, low, high, proj_far
    )
    proj_mine = jnp.stack([proj_weight, proj_far])
    proj_other = swap_core(proj_mine)
    out_second = spread_y(out_first[:2])
    out_first_other = swap_core(out_first)
    from_left, from_right, out_second, out_first_other, proj_other = join(
        shift_x(jnp.concatenate([left_low, high]), 1),
        shift_x(jnp.concatenate([right_high, low]), -1),
        out_second,
        out_first_other,
        proj_other,
    )
    proj_quad = jnp.concatenate([proj_mine, proj_other])
    near = [whole_att, far, left_low, right_high, from_left, from_right]
    pieces, last_pieces = piece_places(PATCHES)
    out_second_other = swap_core(out_second)
    proj_first = spread_y(proj_quad)
    beyond = jnp.concatenate([from_left[:PATCHES], from_right[:PATCHES]])
    last = [shift_x(far, -1), shift_x(far, 1), swap_zl(beyond)]
    parts = [out_quad, out_first, out_first_other, out_second, out_second_other]
    total, left = out_project(near, pieces, parts, out_shards, kept=6)
    block_out, low, high, stats = out_project(
        last, last_pieces, [left], mp_slot, total=total, patches=patches
    )

    proj_first, whole_block, low, high, stats = join(proj_first, block_out, low, high, stats)
    far = swap_zl(whole_block)
    proj_second = spread_y(proj_first[:2])
    proj_first_other = swap_core(proj_first)
    left_low, right_high, proj_first_other, proj_second, low, high = join(
        shift_x(low, 1), shift_x(high, -1), proj_first_other, proj_second, low, high
    )
    from_left, from_right, far = join(
        shift_x(jnp.concatenate([left_low, high]), 1),
        shift_x(jnp.concatenate([right_high, low]), -1),
        far,
    )
    near = [whole_block, far, left_low, right_high, from_left, from_right]
    pieces, last_pieces = piece_places(PATCHES + EXTRA)
    last = [shift_x(far, -1), shift_x(far, 1), swap_zl(from_left[:PATCHES])]
    stats = add_sums(stats, [(left_low, 0), (right_high, 0), (from_left, 0)])
    stats_z = swap_zl(stats)
    from_right_held, stats = join(from_right, stats)
    last.append(swap_zl(from_right_held[:PATCHES]))
    last_pieces = (*last_pieces[:2], ((2, 0), (3, 0)))
    stats = stats + stats_z
    parts = [proj_quad, proj_first, proj_first_other, proj_second, swap_core(proj_second)]

    total, left = project(
        near,
        pieces,
        stats,
        final_gain,
        parts,
        first_index,
        kept=6,
    )
    (outgoing,) = project(
        last,
        last_pieces,
        stats,
        final_gain,
        [left],
        last_index,
        total=total,
    )
    arrived = lax.all_to_all(outgoing, "mp", split_axis=0, concat_axis=0, tiled=True)
    sequence = pack(arrived, text_embed[0], pack_index)
    return (block_out, sequence[None])


def solution(mesh):
    in_specs = (
        P("dp", None),
        P(),
        P("dp", "mp", None),
        P(None, "mp", None),
        P("dp", "mp"),
        P(),
        P("dp", "mp"),
        P("dp", "mp", None),
        P("dp"),
        P("dp"),
    )
    out_specs = (P("dp", "mp"), P("dp", "mp", None))
    return jax.shard_map(local, mesh=mesh, in_specs=in_specs, out_specs=out_specs, check_vma=False)
```

```python
import functools
import math

import jax
import jax.numpy as jnp
import numpy as np
from jax import lax
from jax.experimental import pallas as pl
from jax.experimental.pallas import tpu as pltpu
from jax.sharding import PartitionSpec as P

PATCHES = 256
HALF = 128
AXES = ("dp", "mp")
MEGA = 1024 * 1024
epsilon = 1e-06
EXTRA = 16
SMALL = pl.CostEstimate(flops=1, bytes_accessed=1, transcendentals=0)


def coordinates():
    return [
        (zh, y, c, zl, x)
        for zh in range(2)
        for y in range(4)
        for c in range(2)
        for zl in range(2)
        for x in range(4)
    ]


def device_index(zh, y, c, zl, x):
    return ((zh * 4 + y) * 2 + c) * 8 + zl * 4 + x


def move(values, target):
    pairs = [(device_index(*at), device_index(*target(*at))) for at in coordinates()]
    return lax.ppermute(values, AXES, pairs)


def swap_core(values):
    return move(values, lambda zh, y, c, zl, x: (zh, y, 1 - c, zl, x))


def swap_zh(values):
    return move(values, lambda zh, y, c, zl, x: (1 - zh, y, c, zl, x))


def swap_zl(values):
    return move(values, lambda zh, y, c, zl, x: (zh, y, c, 1 - zl, x))


def spread_y(values):
    return move(values, lambda zh, y, c, zl, x: (zh, (y + 1 - 2 * c) % 4, c, zl, x))


def shift_x(values, step):
    return move(values, lambda zh, y, c, zl, x: (zh, y, c, zl, (x + step) % 4))


def turn_first(values):
    return move(values, lambda zh, y, c, zl, x: (zl, (x + y) % 4, c, zh, x))


def turn_second(values):
    return move(values, lambda zh, y, c, zl, x: (zh, y, c, zl, (y - x) % 4))


def per_device(order):
    table = np.zeros((16, 16), np.int32)
    for zh in range(2):
        for y in range(4):
            for c in range(2):
                met = order(zh, y, c, 2 * c - 1)
                table[zh * 8 + y * 2 + c] = [r % 2 * 8 + yy % 4 * 2 + cc % 2 for r, yy, cc in met]
    return table


def early_order(zh, y, c, step):
    return [
        (zh, y, c),
        (zh, y, c + 1),
        (zh + 1, y, c),
        (zh + 1, y, c + 1),
        (zh, y + step, c),
        (zh, y - step, c + 1),
        (zh, y + step, c + 1),
        (zh, y - step, c),
        (zh + 1, y + step, c),
        (zh + 1, y - step, c + 1),
        (zh, y + 2, c),
        (zh, y + 2, c + 1),
        (zh + 1, y + step, c + 1),
        (zh + 1, y - step, c),
        (zh + 1, y + 2, c),
        (zh + 1, y + 2, c + 1),
    ]


def late_order(zh, y, c, step):
    order = []
    for yy, cores in (
        (y, (c, c + 1)),
        (y + step, (c, c + 1)),
        (y - step, (c + 1, c)),
        (y + 2, (c, c + 1)),
    ):
        for core in cores:
            order += [(zh, yy, core), (zh + 1, yy, core)]
    return order


NEAR = [(0, 0), (1, 0), (0, 1), (0, 3), (0, 2), (1, 1), (1, 3), (1, 2)]


def place_tables():
    met = per_device(late_order)
    groups = np.zeros((8, 8), np.int32)
    shards = np.zeros((2, 16, 8, 16), np.int32)
    for mp in range(8):
        for r, (dz, dx) in enumerate(NEAR):
            group = (mp // 4 ^ dz) * 4 + (mp + dx) % 4
            groups[mp, r] = group
            turned = group // 4 * 4 + (group + mp) % 4
            for dp in range(16):
                for half in range(2):
                    shards[0, dp, mp, 2 * r + half] = np.argmax(met[dp] == 2 * group + half)
                    shards[1, dp, mp, 2 * r + half] = np.argmax(met[dp] == 2 * turned + half)
    return groups, shards


def norm_kernel(values_ref, gain_ref, out_ref):
    values = values_ref[...].astype(jnp.float32)
    width = values.shape[1]
    row_mean = jnp.sum(values, -1, keepdims=True) / width
    squares = jnp.sum(values * values, -1, keepdims=True) / width
    scale = lax.rsqrt(squares - row_mean * row_mean + epsilon)
    normed = ((values - row_mean) * scale * gain_ref[...]).astype(jnp.bfloat16)
    depth = out_ref.shape[2]
    for k in range(out_ref.shape[0]):
        out_ref[k] = normed[:, k * depth : (k + 1) * depth]


def norm_columns(values, gain, chunks):
    rows, width = values.shape
    block = 64
    return pl.pallas_call(
        norm_kernel,
        grid=(rows // block,),
        in_specs=[
            pl.BlockSpec((block, width), lambda i: (i, 0)),
            pl.BlockSpec((1, width), lambda i: (0, 0)),
        ],
        out_specs=pl.BlockSpec((chunks, block, width // chunks), lambda i: (0, i, 0)),
        out_shape=jax.ShapeDtypeStruct((chunks, rows, width // chunks), jnp.bfloat16),
        compiler_params=pltpu.CompilerParams(vmem_limit_bytes=16 * MEGA),
        cost_estimate=SMALL,
        name="norm_columns",
    )(*in_hbm([values]), gain.reshape(1, width))


def row_norm(values, gain):
    row_mean = jnp.mean(values, -1, keepdims=True)
    squares = jnp.mean(values * values, -1, keepdims=True)
    return (values - row_mean) * lax.rsqrt(squares - row_mean * row_mean + epsilon) * gain


def accumulate_kernel(shard_counts, has_total, attend, index_ref, *refs):
    del index_ref
    count = sum(shard_counts)
    columns, refs = refs[:count], refs[count:]
    shards, refs = refs[: len(shard_counts)], refs[len(shard_counts) :]
    total = None
    if has_total:
        total, refs = refs[0][0], refs[1:]
    held = [ref[k, 0] for ref, number in zip(shards, shard_counts) for k in range(number)]
    term = jnp.dot(
        jnp.concatenate([ref[0] for ref in columns], 1),
        jnp.concatenate(held, 0),
        preferred_element_type=jnp.float32,
    )
    total = term if total is None else total + term
    if not attend:
        refs[0][0] = total
        return
    gain_ref, out_ref, *image_refs = refs
    size = gain_ref.shape[2]
    gains = gain_ref[0]
    query = row_norm(total[:, :size], gains[0:1]).astype(jnp.bfloat16)
    key = row_norm(total[:, size : 2 * size], gains[1:2]).astype(jnp.bfloat16)
    value = total[:, 2 * size :].astype(jnp.bfloat16)
    for image in range(total.shape[0] // PATCHES):
        rows = slice(image * PATCHES, (image + 1) * PATCHES)
        scores = lax.dot_general(
            query[rows], key[rows], (((1,), (1,)), ((), ())), preferred_element_type=jnp.float32
        ) / math.sqrt(size)
        raised = jnp.exp(scores - jnp.max(scores, -1, keepdims=True))
        weights = (raised / jnp.sum(raised, -1, keepdims=True)).astype(jnp.bfloat16)
        attended = jnp.dot(weights, value[rows], preferred_element_type=jnp.float32)
        attended = attended.astype(jnp.bfloat16)
        out_ref[rows, :] = attended
        image_refs[image][...] = attended


def accumulate(columns, shards, index, total=None, gains=None):
    shards = [held if held.ndim == 4 else held[None] for held in shards]
    counts = tuple(held.shape[0] for held in shards)
    _, rows, depth = columns.shape
    heads, wide = shards[0].shape[1], shards[0].shape[3]
    in_specs = [
        pl.BlockSpec((1, rows, depth), functools.partial(lambda k, h, index: (index[k], 0, 0), k))
        for k in range(sum(counts))
    ]
    in_specs += [
        pl.BlockSpec((number, 1, depth, wide), lambda h, index: (0, h, 0, 0)) for number in counts
    ]
    operands = [columns] * sum(counts) + (in_hbm(shards) if gains is None else shards)
    total_spec = pl.BlockSpec((1, rows, wide), lambda h, index: (h, 0, 0))
    if total is not None:
        in_specs.append(total_spec)
        operands.append(total)
    aliases = {}
    if gains is None:
        out_spec = total_spec
        out_shape = jax.ShapeDtypeStruct((heads, rows, wide), jnp.float32)
        if total is not None:
            aliases = {len(operands): 0}
    else:
        in_specs.append(pl.BlockSpec((1, 2, wide // 3), lambda h, index: (h, 0, 0)))
        operands.append(gains)
        sizes = [rows] + [PATCHES] * (rows // PATCHES)
        out_spec = [pl.BlockSpec((size, wide // 3), lambda h, index: (0, h)) for size in sizes]
        out_shape = [
            jax.ShapeDtypeStruct((size, heads * wide // 3), jnp.bfloat16) for size in sizes
        ]
    return pl.pallas_call(
        functools.partial(accumulate_kernel, counts, total is not None, gains is not None),
        grid_spec=pltpu.PrefetchScalarGridSpec(
            num_scalar_prefetch=1, grid=(heads,), in_specs=in_specs, out_specs=out_spec
        ),
        out_shape=out_shape,
        input_output_aliases=aliases,
        compiler_params=pltpu.CompilerParams(vmem_limit_bytes=20 * MEGA),
        cost_estimate=SMALL,
        name="accumulate",
    )(index, *operands)


def start_shards(parts, held_ref, sems):
    at = 0
    copies = []
    for k, part in enumerate(parts):
        number = part.shape[0]
        copies.append(pltpu.make_async_copy(part, held_ref.at[pl.ds(at, number)], sems.at[k]))
        copies[-1].start()
        at += number
    return copies


def start_pieces(pieces, near, near_ref, sems):
    copies = []
    count = 0
    for at, piece in enumerate(pieces):
        copies.append([])
        rows = near_ref.shape[1] // len(piece)
        for part, (k, first) in enumerate(piece):
            source = near[k].at[pl.ds(first, rows)]
            place = near_ref.at[at, pl.ds(part * rows, rows)]
            copies[-1].append(pltpu.make_async_copy(source, place, sems.at[count]))
            copies[-1][-1].start()
            count += 1
    return copies


def wait_all(copies):
    for copy in copies:
        copy.wait()


def out_kernel(pieces, held, count, kept, finish, index_ref, *refs):
    near, refs = refs[:held], refs[held:]
    parts, refs = refs[:count], refs[count:]
    if finish:
        given_ref, own_ref, block_ref, *half_refs, stats_ref = refs[:-4]
    else:
        total_ref, kept_ref = refs[:-4]
    near_ref, held_ref, near_sems, sems = refs[-4:]
    shard_copies = start_shards(parts, held_ref, sems)
    piece_copies = start_pieces(pieces, near, near_ref, near_sems)
    wait_all(shard_copies)
    depth = held_ref.shape[1]
    total = [given_ref[0], given_ref[1]] if finish else [None, None]
    for k in range(len(pieces)):
        wait_all(piece_copies[k])
        for half in range(2):
            term = lax.dot_general(
                near_ref[k],
                held_ref[2 * k + half if finish else index_ref[2 * k + half]],
                (((1,), (1,)), ((), ())),
                preferred_element_type=jnp.float32,
            )
            term = term.astype(jnp.bfloat16).astype(jnp.float32)
            total[half] = term if total[half] is None else total[half] + term
    if not finish:
        total_ref[0] = total[0]
        total_ref[1] = total[1]
        for k in range(kept):
            kept_ref[k] = held_ref[index_ref[2 * len(pieces) + k]]
        return
    sums, squares = 0.0, 0.0
    for half in range(2):
        cols = slice(half * depth, (half + 1) * depth)
        block = (own_ref[:, cols].astype(jnp.float32) + total[half]).astype(jnp.bfloat16)
        block_ref[:, cols] = block
        rows = block.shape[0] // 2
        half_refs[0][:rows, cols] = block[:rows]
        half_refs[1][:rows, cols] = block[rows:]
        block = block.astype(jnp.float32)
        sums += jnp.sum(block, 1, keepdims=True)
        squares += jnp.sum(block * block, 1, keepdims=True)
    lane = lax.broadcasted_iota(jnp.int32, (sums.shape[0], 128), 1)
    both = jnp.where(lane == 0, sums, squares).T[:8]
    stats_ref[...] = both
    row = lax.broadcasted_iota(jnp.int32, (EXTRA, both.shape[1]), 0)
    carried = jnp.zeros(row.shape, jnp.float32)
    for k in range(2):
        rest = both[k : k + 1]
        for part in range(3):
            rounded = rest.astype(jnp.bfloat16).astype(jnp.float32)
            carried = jnp.where(row == 3 * k + part, rounded, carried)
            rest = rest - rounded
    carried = carried.astype(jnp.bfloat16)
    for half_ref in half_refs:
        half_ref[rows:, : carried.shape[1]] = carried
        half_ref[rows:, carried.shape[1] :] = jnp.zeros(
            (EXTRA, half_ref.shape[1] - carried.shape[1]), jnp.bfloat16
        )


def held_scratch(pieces, near, parts, wide):
    rows = near[0].shape[0]
    depth = parts[0].shape[1]
    return [
        pltpu.VMEM((len(pieces), rows, near[0].shape[1]), jnp.bfloat16),
        pltpu.VMEM((sum(part.shape[0] for part in parts), depth, wide), jnp.bfloat16),
        pltpu.SemaphoreType.DMA((sum(len(piece) for piece in pieces),)),
        pltpu.SemaphoreType.DMA((len(parts),)),
    ]


def in_hbm(arrays):
    return [pltpu.with_memory_space_constraint(array, pltpu.HBM) for array in arrays]


def whole(shape):
    return pl.BlockSpec(shape, lambda i, index: (0,) * len(shape))


def out_project(near, pieces, parts, index, kept=0, total=None, patches=None):
    depth = parts[0].shape[1]
    finish = total is not None
    place = pl.ANY if finish else pltpu.HBM
    in_specs = [pl.BlockSpec(memory_space=place) for _ in (*near, *parts)]
    operands = [*near, *parts] if finish else in_hbm((*near, *parts))
    rows = near[0].shape[0]
    if finish:
        rows = patches.shape[0]
        in_specs.append(whole(total.shape))
        in_specs.append(pl.BlockSpec((rows, 2 * depth), lambda i, index: (0, index[0])))
        operands += [total, *in_hbm([patches])]
        out_shape = [
            jax.ShapeDtypeStruct((rows, 2 * depth), jnp.bfloat16),
            jax.ShapeDtypeStruct((rows // 2 + EXTRA, 2 * depth), jnp.bfloat16),
            jax.ShapeDtypeStruct((rows // 2 + EXTRA, 2 * depth), jnp.bfloat16),
            jax.ShapeDtypeStruct((8, rows), jnp.float32),
        ]
    else:
        out_shape = [
            jax.ShapeDtypeStruct((2, rows, depth), jnp.float32),
            jax.ShapeDtypeStruct((kept, depth, depth), jnp.bfloat16),
        ]
    return pl.pallas_call(
        functools.partial(out_kernel, pieces, len(near), len(parts), kept, finish),
        grid_spec=pltpu.PrefetchScalarGridSpec(
            num_scalar_prefetch=1,
            grid=(1,),
            in_specs=in_specs,
            out_specs=[whole(out.shape) for out in out_shape],
            scratch_shapes=held_scratch(pieces, near, parts, depth),
        ),
        out_shape=out_shape,
        compiler_params=pltpu.CompilerParams(vmem_limit_bytes=20 * MEGA),
        cost_estimate=SMALL,
        name="out_project",
    )(index, *operands)


def sums_kernel(own_ref, *refs):
    *carried, out_ref = refs
    total = own_ref[...]
    row = lax.broadcasted_iota(jnp.int32, total.shape, 0)
    for ref in carried:
        parts = ref[...].astype(jnp.float32)
        sums, squares = (
            parts[k : k + 1] + parts[k + 1 : k + 2] + parts[k + 2 : k + 3] for k in (0, 3)
        )
        total = total + jnp.where(row == 0, sums, squares)
    out_ref[...] = total


def add_sums(own, carried):
    rows = own.shape[1]
    in_specs = [pl.BlockSpec(own.shape, lambda i: (0, 0))]
    for _, first in carried:
        place = (first + PATCHES) // EXTRA
        in_specs.append(
            pl.BlockSpec((EXTRA, rows), functools.partial(lambda place, i: (place, 0), place))
        )
    return pl.pallas_call(
        sums_kernel,
        grid=(1,),
        in_specs=in_specs,
        out_specs=pl.BlockSpec(own.shape, lambda i: (0, 0)),
        out_shape=jax.ShapeDtypeStruct(own.shape, own.dtype),
        compiler_params=pltpu.CompilerParams(vmem_limit_bytes=4 * MEGA),
        cost_estimate=SMALL,
        name="add_sums",
    )(own, *in_hbm([array for array, _ in carried]))


def project_kernel(pieces, held, count, kept, finish, width, index_ref, *refs):
    near, refs = refs[:held], refs[held:]
    stats_ref, refs = refs[0], refs[1:]
    gains, refs = refs[: len(pieces)], refs[len(pieces) :]
    parts, refs = refs[:count], refs[count:]
    if finish:
        total, (out_ref, *refs, blocks_ref) = refs[0][...], refs[1:]
    else:
        total, (out_ref, kept_ref, *refs) = None, refs
    near_ref, held_ref, near_sems, sems = refs
    shard_copies = start_shards(parts, held_ref, sems)
    piece_copies = start_pieces(pieces, near, near_ref, near_sems)
    rows = stats_ref.shape[1]
    row = lax.broadcasted_iota(jnp.int32, (128, rows), 0)
    stats = jnp.where(row == 0, stats_ref[0:1], stats_ref[1:2]).T
    row_mean = stats[:, 0:1] / width
    scale = lax.rsqrt(stats[:, 1:2] / width - row_mean * row_mean + epsilon)
    wait_all(shard_copies)
    for k in range(len(pieces)):
        wait_all(piece_copies[k])
        values = near_ref[k].astype(jnp.float32)
        normed = ((values - row_mean) * scale * gains[k][...]).astype(jnp.bfloat16)
        held = [
            held_ref[2 * k + half if finish else index_ref[2 * k + half]] for half in range(2)
        ]
        term = jnp.dot(normed, jnp.concatenate(held, 0), preferred_element_type=jnp.float32)
        total = term if total is None else total + term
    if not finish:
        out_ref[...] = total
        for k in range(kept):
            kept_ref[k] = held_ref[index_ref[2 * len(pieces) + k]]
        return
    blocks_ref[...] = total.astype(jnp.bfloat16).reshape(blocks_ref.shape)
    for block in range(out_ref.shape[0]):
        source = index_ref[len(pieces) + block]
        value = blocks_ref[jnp.maximum(source, 0)]
        out_ref[block] = jnp.where(source >= 0, value, jnp.zeros_like(value))


def project(near, pieces, stats, gain, parts, index, kept=0, total=None):
    rows = stats.shape[1]
    width = gain.shape[0]
    depth, wide = parts[0].shape[1:]
    count = len(pieces)
    finish = total is not None
    at = 0 if finish else 2 * count + kept
    place = pl.ANY if finish else pltpu.HBM
    in_specs = [pl.BlockSpec(memory_space=place) for _ in near]
    in_specs.append(whole(stats.shape))
    in_specs += [
        pl.BlockSpec((1, 2 * depth), functools.partial(lambda k, i, index: (0, index[k]), k))
        for k in range(at, at + count)
    ]
    in_specs += [pl.BlockSpec(memory_space=place) for _ in parts]
    operands = (list(near) if finish else in_hbm(near)) + [stats]
    operands += [gain.reshape(1, width)] * count
    operands += parts if finish else in_hbm(parts)
    scratch = held_scratch(pieces, near, parts, wide)
    if finish:
        in_specs.append(whole(total.shape))
        operands.append(total)
        out_shape = [jax.ShapeDtypeStruct((8, HALF, wide), jnp.bfloat16)]
        scratch.append(pltpu.VMEM((rows // HALF, HALF, wide), jnp.bfloat16))
    else:
        out_shape = [
            jax.ShapeDtypeStruct((rows, wide), jnp.float32),
            jax.ShapeDtypeStruct((kept, depth, wide), jnp.bfloat16),
        ]
    return pl.pallas_call(
        functools.partial(
            project_kernel, pieces, len(near), len(parts), kept, finish, width
        ),
        grid_spec=pltpu.PrefetchScalarGridSpec(
            num_scalar_prefetch=1,
            grid=(1,),
            in_specs=in_specs,
            out_specs=[whole(out.shape) for out in out_shape],
            scratch_shapes=scratch,
        ),
        out_shape=out_shape,
        compiler_params=pltpu.CompilerParams(vmem_limit_bytes=28 * MEGA),
        cost_estimate=SMALL,
        name="project",
    )(index, *operands)


def pack_kernel(place_ref, arrived_ref, text_ref, out_ref):
    start, first, second, length = (place_ref[k] for k in range(4))
    rows, wide = arrived_ref.shape[1:]
    covered = ((start >= first) & (start < first + PATCHES)) | (
        (start >= second) & (start < second + PATCHES)
    )

    @pl.when(covered)
    def _():
        for k in range(arrived_ref.shape[0]):
            out_ref[:, k * wide : (k + 1) * wide] = arrived_ref[k]

    @pl.when(jnp.logical_not(covered))
    def _():
        position = start + lax.broadcasted_iota(jnp.int32, (rows, wide), 0)
        before = jnp.clip(position - first, 0, PATCHES) + jnp.clip(position - second, 0, PATCHES)
        is_text = position - before < length
        for k in range(arrived_ref.shape[0]):
            text = text_ref[:, k * wide : (k + 1) * wide].astype(jnp.float32)
            out_ref[:, k * wide : (k + 1) * wide] = jnp.where(is_text, text, 0.0).astype(
                jnp.bfloat16
            )


def pack(arrived, text, place):
    return pl.pallas_call(
        pack_kernel,
        grid_spec=pltpu.PrefetchScalarGridSpec(
            num_scalar_prefetch=1,
            grid=(1,),
            in_specs=[whole(arrived.shape), whole(text.shape)],
            out_specs=whole(text.shape),
        ),
        out_shape=jax.ShapeDtypeStruct(text.shape, text.dtype),
        compiler_params=pltpu.CompilerParams(vmem_limit_bytes=8 * MEGA),
        cost_estimate=SMALL,
        name="pack",
    )(place, arrived, text)


def join(*values):
    return lax.optimization_barrier(values)


def piece_places(step):
    first = (
        ((0, 0),),
        ((1, 0),),
        ((5, step), (3, 0)),
        ((2, 0), (4, step)),
        ((4, 0), (5, 0)),
    )
    return first, (((0, 0),), ((1, 0),), ((2, 0), (2, PATCHES)))


def local(
    patches,
    norm_gain,
    qkv_weight,
    qk_gain,
    out_weight,
    final_gain,
    proj_weight,
    text_embed,
    slot_offset,
    text_len,
):
    own = qkv_weight.transpose(1, 0, 2)
    first = spread_y(own)
    other = swap_core(own)
    far = swap_zh(own)
    half_turned = turn_first(out_weight)
    (other,) = join(other)
    beside = spread_y(other)
    columns = norm_columns(join(patches, other)[0], norm_gain, 16)
    dp = lax.axis_index("dp")
    mp = lax.axis_index("mp")
    met = jnp.asarray(per_device(early_order))[dp]
    total = accumulate(columns, [own, other], met[0:2])

    far, first, beside, half_turned, total = join(far, first, beside, half_turned, total)
    far_first = spread_y(far)
    second = spread_y(first)
    far_beside = swap_zh(beside)
    turned = turn_second(half_turned)
    far_other, first_other, beside_other = join(
        swap_core(far), swap_core(first), swap_core(beside)
    )
    total = accumulate(
        columns,
        [far, far_other, first, first_other, beside, beside_other],
        met[2:8],
        total,
    )
    total, slot_offset, text_len, dp, mp = join(total, slot_offset, text_len, dp, mp)
    groups, shards = place_tables()
    groups, shards = jnp.asarray(groups)[mp], jnp.asarray(shards)[:, dp, mp]
    shards, out_shards = shards[0], shards[1]
    mp_slot = mp[None].astype(jnp.int32)
    slot = slot_offset // HALF
    block = jnp.arange(8, dtype=jnp.int32)
    in_first = (block >= slot[0]) & (block < slot[0] + 2)
    in_second = (block >= slot[1]) & (block < slot[1] + 2)
    source = jnp.where(in_first, block - slot[0], jnp.where(in_second, block - slot[1] + 2, -1))

    first_index = jnp.concatenate([shards, groups[:5]])
    last_index = jnp.concatenate([groups[5:], source])
    pack_index = jnp.concatenate([mp_slot * HALF, slot_offset, text_len])

    far_first, second, far_beside, turned, total, first_index, last_index, pack_index = join(
        far_first, second, far_beside, turned, total, first_index, last_index, pack_index
    )
    far_second = spread_y(far_first)
    turned_far = swap_zh(turned)
    far_first_other, second_other, far_beside_other = join(
        swap_core(far_first), swap_core(second), swap_core(far_beside)
    )
    total = accumulate(
        columns,
        [far_first, far_first_other, second, second_other, far_beside, far_beside_other],
        met[8:14],
        total,
    )

    far_second, turned_far, proj_held, total = join(far_second, turned_far, proj_weight, total)
    proj_far = swap_zh(proj_held)
    far_second_other = swap_core(far_second)
    out_mine = jnp.stack([turned, turned_far])
    out_other = swap_core(out_mine)
    out_quad = jnp.concatenate([out_mine, out_other])
    out_first = spread_y(out_quad)
    attended = accumulate(
        columns, [far_second, far_second_other], met[14:16], total, qk_gain.transpose(1, 0, 2)
    )

    whole_att, low, high = join(*attended)
    far = swap_zl(whole_att)
    left_low, right_high, far, out_first, low, high, proj_far = join(
        shift_x(low, 1), shift_x(high, -1), far, out_first, low, high, proj_far
    )
    proj_mine = jnp.stack([proj_weight, proj_far])
    proj_other = swap_core(proj_mine)
    out_second = spread_y(out_first[:2])
    out_first_other = swap_core(out_first)
    from_left, from_right, out_second, out_first_other, proj_other = join(
        shift_x(jnp.concatenate([left_low, high]), 1),
        shift_x(jnp.concatenate([right_high, low]), -1),
        out_second,
        out_first_other,
        proj_other,
    )
    proj_quad = jnp.concatenate([proj_mine, proj_other])
    near = [whole_att, far, left_low, right_high, from_left, from_right]
    pieces, last_pieces = piece_places(PATCHES)
    out_second_other = swap_core(out_second)
    proj_first = spread_y(proj_quad)
    beyond = jnp.concatenate([from_left[:PATCHES], from_right[:PATCHES]])
    last = [shift_x(far, -1), shift_x(far, 1), swap_zl(beyond)]
    parts = [out_quad, out_first, out_first_other, out_second, out_second_other]
    total, left = out_project(near, pieces, parts, out_shards, kept=6)
    block_out, low, high, stats = out_project(
        last, last_pieces, [left], mp_slot, total=total, patches=patches
    )

    proj_first, whole_block, low, high, stats = join(proj_first, block_out, low, high, stats)
    far = swap_zl(whole_block)
    proj_second = spread_y(proj_first[:2])
    proj_first_other = swap_core(proj_first)
    left_low, right_high, proj_first_other, proj_second, low, high = join(
        shift_x(low, 1), shift_x(high, -1), proj_first_other, proj_second, low, high
    )
    from_left, from_right, far = join(
        shift_x(jnp.concatenate([left_low, high]), 1),
        shift_x(jnp.concatenate([right_high, low]), -1),
        far,
    )
    near = [whole_block, far, left_low, right_high, from_left, from_right]
    pieces, last_pieces = piece_places(PATCHES + EXTRA)
    last = [shift_x(far, -1), shift_x(far, 1), swap_zl(from_left[:PATCHES])]
    stats = add_sums(stats, [(left_low, 0), (right_high, 0), (from_left, 0)])
    stats_z = swap_zl(stats)
    from_right_held, stats = join(from_right, stats)
    last.append(swap_zl(from_right_held[:PATCHES]))
    last_pieces = (*last_pieces[:2], ((2, 0), (3, 0)))
    stats = stats + stats_z
    parts = [proj_quad, proj_first, proj_first_other, proj_second, swap_core(proj_second)]

    total, left = project(
        near,
        pieces,
        stats,
        final_gain,
        parts,
        first_index,
        kept=6,
    )
    (outgoing,) = project(
        last,
        last_pieces,
        stats,
        final_gain,
        [left],
        last_index,
        total=total,
    )
    arrived = lax.all_to_all(outgoing, "mp", split_axis=0, concat_axis=0, tiled=True)
    sequence = pack(arrived, text_embed[0], pack_index)
    return (block_out, sequence[None])


def solution(mesh):
    in_specs = (
        P("dp", None),
        P(),
        P("dp", "mp", None),
        P(None, "mp", None),
        P("dp", "mp"),
        P(),
        P("dp", "mp"),
        P("dp", "mp", None),
        P("dp"),
        P("dp"),
    )
    out_specs = (P("dp", "mp"), P("dp", "mp", None))
    return jax.shard_map(local, mesh=mesh, in_specs=in_specs, out_specs=out_specs, check_vma=False)
```
